32 devices in a mesh: band: 16 (over z, x, core), comp: 2 (over y).
Axes of the slice: x: 2, y: 2, z: 4, core: 2. Of those that a mesh axis runs over, the one named last changes fastest.
Arguments:
- energy: bfloat16 [720, 32, 1024], P('comp', 'band'), may hold values from 0.19921875 to 2
- depth_speed: float32 [32, 1024], P('band'), may hold values from 0.3 to 1
- ocean_mask: int32 [32, 1024], P('band'), may hold values from 0 to 1, as said below
- interp_first: bfloat16 [720, 720], replicated, may hold values from -0.21875 to 0.21875
- interp_second: bfloat16 [720, 720], replicated, may hold values from -0.21875 to 0.21875
- transfer_matrix: bfloat16 [720, 720], replicated, may hold values from -0.21875 to 0.21875
- growth: float32 [720], replicated, may hold values from -0.5 to 1
Outputs:
- energy_next: bfloat16 [720, 32, 1024], P('comp', 'band')
The draws below stay inside these ranges and needn't reach their ends.
Inputs may be any that keep to these rules, and one draw needn't show every extreme that they name: `ocean_mask`: split the 1024 columns into equal longitude blocks of 512 columns, one for each index of comp; within each band of 2 rows every block of 1024 cells holds at most 768 ocean cells, and in every band one block holds exactly 768.
All inputs are finite; a program needn't handle non-finite values.
Results may differ from the reference program's by a relative error of at most 0.0048.
Values may be sent and summed in bfloat16 or wider, within the bound.
No kernel may reach another device: no remote copies, remote signals or barrier semaphores. Data moves between devices by JAX's collectives and lax.ppermute only.
A program may use at most 64 MiB of HBM per device.

```python
import math
import jax
import jax.numpy as jnp
from jax import lax

ND = 24
NF = 30
ROWS = 2
NLON = 1024
K = 720
NLAT = 32
BLK = 1024
CAP = 768


def draw_ocean_mask(key, part):
    key = jax.random.fold_in(key, 7)
    block_width = BLK // ROWS
    block_count = NLON // block_width
    band_count = NLAT // ROWS
    key_full, key_fill, key_rank = jax.random.split(key, 3)
    full_block = jax.random.randint(key_full, (band_count, 1), 0, block_count)
    filled = jax.random.randint(key_fill, (band_count, block_count), CAP // 4, CAP + 1)
    filled = jnp.where(jnp.arange(block_count)[None] == full_block, CAP, filled)
    rank_keys = jax.random.split(key_rank, band_count * block_count)

    def rank_cells(cell_key):
        return jax.random.permutation(cell_key, BLK)
    ranks = jax.vmap(rank_cells)(rank_keys)
    ocean = (ranks < filled.reshape(-1, 1)).astype(jnp.int32)
    ocean = ocean.reshape(band_count, block_count, ROWS, block_width).transpose(0, 2, 1, 3)
    return ocean.reshape(NLAT, NLON)


def level_of(own_key, shape, shards, least, high):
    factor_of, own = 1.0, jax.random.fold_in(own_key, 6)
    for axis_at, blocks in shards:
        heights = jnp.exp(jax.random.uniform(jax.random.fold_in(own, axis_at), (blocks,), jnp.float32, least / len(shards), high / len(shards)))
        factor_of = factor_of * jnp.repeat(heights, shape[axis_at] // blocks).reshape([-1 if axis == axis_at else 1 for axis in range(len(shape))])
    return factor_of


def gaussian(rng, shape, width, bound, kind=jnp.bfloat16):
    result = width * jax.random.normal(rng, shape, jnp.float32)
    return jnp.clip(result, min=-bound, max=bound).astype(kind)


def setup_inputs(seed: int = 0) -> dict:
    key_list = jax.random.split(jax.random.key(seed), 8)
    energy = jnp.clip(jnp.exp(math.log(2.0) - 2.306499 * jax.random.uniform(key_list[0], (K, NLAT, NLON), jnp.float32) ** level_of(key_list[0], (K, NLAT, NLON), ((0, 2), (1, 16)), -0.2, 0.2)), 0.19921875, 2.0).astype(jnp.bfloat16)
    depth_speed = jnp.clip(0.3 + 0.7 * jax.random.uniform(key_list[1], (NLAT, NLON), jnp.float32) ** level_of(key_list[1], (NLAT, NLON), ((0, 16),), -0.2, 0.2), 0.3, 1.0)
    ocean_mask = draw_ocean_mask(jax.random.fold_in(key_list[7], 71), 0)
    interp_first = gaussian(key_list[3], (K, K), K ** -0.5, 0.21875)
    interp_second = gaussian(key_list[4], (K, K), K ** -0.5, 0.21875)
    transfer_matrix = gaussian(key_list[5], (K, K), K ** -0.5, 0.21875)
    growth = jnp.clip(jax.random.uniform(key_list[6], (K,), jnp.float32, -0.5, 1.0), -0.5, 1.0)
    return dict(energy=energy, depth_speed=depth_speed, ocean_mask=ocean_mask, interp_first=interp_first, interp_second=interp_second, transfer_matrix=transfer_matrix, growth=growth)


SOURCE_STEP = 0.5
COURANT_TOP = 0.9
FREQ_RATIO = 1.1


def courant_numbers():
    components = jnp.arange(K, dtype=jnp.int32)
    frequency = (components // ND).astype(jnp.float32)
    direction = (components % ND).astype(jnp.float32)
    heading = 2.0 * jnp.pi * (direction + 0.5) / ND
    factor = COURANT_TOP * jnp.power(jnp.float32(FREQ_RATIO), -frequency)
    return factor * jnp.cos(heading), factor * jnp.sin(heading)


def upwind(middle, lower_one, lower_two, upper_one, upper_two, courant):
    magnitude = jnp.abs(courant)
    first_up = jnp.where(courant > 0, lower_one, upper_one)
    second_up = jnp.where(courant > 0, lower_two, upper_two)
    return (middle - 0.5 * magnitude * (3.0 * middle - 4.0 * first_up + second_up)
            + 0.5 * magnitude * magnitude * (middle - 2.0 * first_up + second_up))


def lat_sweep(extended, courant):
    return upwind(extended[:, 2:-2], extended[:, 1:-3], extended[:, :-4],
                  extended[:, 3:-1], extended[:, 4:], courant)


def lon_sweep(field_values, courant):
    return upwind(field_values, jnp.roll(field_values, 1, axis=2), jnp.roll(field_values, 2, axis=2),
                  jnp.roll(field_values, -1, axis=2), jnp.roll(field_values, -2, axis=2), courant)


def half_step(field_values, lat_courant, lon_courant, depth_speed, ocean):
    blocks = field_values.reshape(NF, ND, NLAT, NLON)

    def sweep_block(operands):
        comp_block, lat_block, lon_block = operands
        extended = jnp.pad(comp_block, ((0, 0), (2, 2), (0, 0)))
        swept = lat_sweep(extended, lat_block[:, None, None] * depth_speed[None])
        return ocean[None] * lon_sweep(swept, lon_block[:, None, None] * depth_speed[None])

    swept_blocks = lax.map(sweep_block, (blocks, lat_courant.reshape(NF, ND), lon_courant.reshape(NF, ND)))
    return swept_blocks.reshape(K, NLAT, NLON)


def source_terms(cell_spectra, interp_first, interp_second, transfer_matrix, growth):
    spectra32 = cell_spectra.astype(jnp.float32)
    forward_interp = jnp.dot(interp_first.astype(jnp.float32), spectra32)
    backward_interp = jnp.dot(interp_second.astype(jnp.float32), spectra32)
    product = (forward_interp * backward_interp).astype(jnp.bfloat16)
    nonlinear = jnp.dot(transfer_matrix.astype(jnp.float32), product.astype(jnp.float32))
    mean_level = jnp.mean(spectra32, axis=0)
    damping = mean_level * mean_level / (1.0 + mean_level * mean_level)
    total = SOURCE_STEP * (nonlinear + (growth[:, None] - damping[None]) * spectra32)
    return total.astype(jnp.bfloat16)


def reference(energy, depth_speed, ocean_mask, interp_first, interp_second, transfer_matrix, growth):
    ocean = ocean_mask.astype(jnp.float32)
    lat_courant, lon_courant = courant_numbers()
    start = ocean[None] * energy.astype(jnp.float32)
    half_one = half_step(start, lat_courant, lon_courant, depth_speed, ocean)
    spectra = half_one.astype(jnp.bfloat16)
    band_count = NLAT // ROWS
    grouped = jnp.moveaxis(spectra.reshape(K, band_count, ROWS * NLON), 1, 0)

    def band_source(cell_spectra):
        return source_terms(cell_spectra, interp_first, interp_second, transfer_matrix, growth)

    source = lax.map(band_source, grouped)
    source = jnp.moveaxis(source, 0, 1).reshape(K, NLAT, NLON)
    updated = ocean[None] * (half_one + source.astype(jnp.float32))
    final_field = half_step(updated, lat_courant, lon_courant, depth_speed, ocean)
    return final_field.astype(jnp.bfloat16)
```

```python
import functools

import jax
import jax.numpy as jnp
import ml_dtypes
import numpy as np
from jax import lax
from jax.experimental import pallas as pl
from jax.experimental.pallas import tpu as pltpu
from jax.sharding import PartitionSpec as P

ND = 24


SOURCE_STEP = 0.5
COURANT_TOP = 0.9
FREQ_RATIO = 1.1

F32 = jnp.float32
BF16 = jnp.bfloat16


def with_halo(value, sides, width):
    for axis, dim in sides:
        peers, length = (lax.axis_size(axis), value.shape[dim])
        up = [(i, (i + 1) % peers) for i in range(peers - 1)]
        down = [(j, i) for i, j in up]
        last = lax.slice_in_dim(value, length - width, length, axis=dim)
        first = lax.slice_in_dim(value, 0, width, axis=dim)
        before = lax.ppermute(last, axis, up)
        after = lax.ppermute(first, axis, down)
        value = jnp.concatenate([before, value, after], axis=dim)
    return value


def courant_numbers(first_comp, local_comps):
    components = first_comp + jnp.arange(local_comps, dtype=jnp.int32)
    frequency = (components // ND).astype(jnp.float32)
    direction = (components % ND).astype(jnp.float32)
    heading = 2.0 * jnp.pi * (direction + 0.5) / ND
    factor = COURANT_TOP * jnp.power(jnp.float32(FREQ_RATIO), -frequency)
    return (factor * jnp.cos(heading), factor * jnp.sin(heading))


def upwind(middle, lower_one, lower_two, upper_one, upper_two, courant):
    magnitude = jnp.abs(courant)
    first_up = jnp.where(courant > 0, lower_one, upper_one)
    second_up = jnp.where(courant > 0, lower_two, upper_two)
    return (
        middle
        - 0.5 * magnitude * (3.0 * middle - 4.0 * first_up + second_up)
        + 0.5 * magnitude * magnitude * (middle - 2.0 * first_up + second_up)
    )


def half_step(extended, lat_courant, lon_courant, depth_speed, ocean):
    widened = extended.astype(jnp.float32)
    swept = upwind(
        widened[:, 2:-2],
        widened[:, 1:-3],
        widened[:, :-4],
        widened[:, 3:-1],
        widened[:, 4:],
        lat_courant[:, None, None] * depth_speed[None],
    )
    lon_values = lon_courant[:, None, None] * depth_speed[None]
    swept = upwind(
        swept,
        jnp.roll(swept, 1, axis=2),
        jnp.roll(swept, 2, axis=2),
        jnp.roll(swept, -1, axis=2),
        jnp.roll(swept, -2, axis=2),
        lon_values,
    )
    return ocean[None] * swept


def source_terms(cell_spectra, interp_first, interp_second, transfer_matrix, growth):
    forward_interp = jnp.dot(interp_first, cell_spectra, preferred_element_type=jnp.float32)
    backward_interp = jnp.dot(interp_second, cell_spectra, preferred_element_type=jnp.float32)
    product = (forward_interp * backward_interp).astype(jnp.bfloat16)
    nonlinear = jnp.dot(transfer_matrix, product, preferred_element_type=jnp.float32)
    spectra32 = cell_spectra.astype(jnp.float32)
    mean_level = jnp.mean(spectra32, axis=0)
    damping = mean_level * mean_level / (1.0 + mean_level * mean_level)
    total = SOURCE_STEP * (nonlinear + (growth[:, None] - damping[None]) * spectra32)
    return total.astype(jnp.bfloat16)


def general_shards(energy, depth_speed, ocean_mask, interp_first, interp_second, transfer_matrix, growth):
    local_comps = energy.shape[0]
    lat_courant, lon_courant = courant_numbers(lax.axis_index("comp") * local_comps, local_comps)
    ocean = ocean_mask.astype(jnp.float32)
    start = (ocean[None] * energy.astype(jnp.float32)).astype(jnp.bfloat16)
    rimmed = with_halo(start, (("band", 1),), 2)
    half_one = half_step(rimmed, lat_courant, lon_courant, depth_speed, ocean)
    spectra = half_one.astype(jnp.bfloat16)
    block_in = lax.all_to_all(spectra, "comp", split_axis=2, concat_axis=0, tiled=True)
    total_comps = block_in.shape[0]
    flat_cells = block_in.reshape(total_comps, -1)
    result = source_terms(flat_cells, interp_first, interp_second, transfer_matrix, growth)
    source = lax.all_to_all(
        result.reshape(block_in.shape), "comp", split_axis=0, concat_axis=2, tiled=True
    ).astype(jnp.float32)
    updated = ocean[None] * (half_one + source)
    rimmed_mid = with_halo(updated, (("band", 1),), 2)
    final_field = half_step(rimmed_mid, lat_courant, lon_courant, depth_speed, ocean)
    return final_field.astype(jnp.bfloat16)


class Plan:
    def __init__(self, local_comps, columns):
        self.local = local_comps
        self.total = 2 * local_comps
        self.columns = columns
        self.half = local_comps // 4
        self.slots = 2 * self.half
        self.rows = -(-self.slots // 8) * 8
        self.pitch = -(-self.slots // 16) * 16
        self.out_rows = -(-(self.total + 1) // 16) * 16

    def members(self, parity, group):
        south = (parity == 0) == (group == 0)
        east, west = (range(6, 12), range(12, 18)) if south else (range(0, 6), range(18, 24))
        frequencies = range(self.local // ND)
        slots = [f * ND + d for side in (east, west) for f in frequencies for d in side]
        return np.array(slots), (1, 0) if south else (0, 1)

    def tables(self):
        pitch, local = self.pitch, self.local
        regroup = np.zeros((2, 4 * pitch, 2 * local), np.float32)
        columns = np.zeros((4, self.total, 4 * pitch), np.float32)
        courant = np.zeros((4, 2, 2, self.rows, 128), np.float32)
        comps = np.arange(self.total, dtype=np.int32)
        heading = np.float32(2.0 * np.pi) * ((comps % ND).astype(np.float32) + np.float32(0.5)) / np.float32(ND)
        factor = np.float32(COURANT_TOP) * np.power(np.float32(FREQ_RATIO), -(comps // ND).astype(np.float32))
        lat, lon = np.abs(factor * np.cos(heading)), np.abs(factor * np.sin(heading))
        at = np.arange(self.slots)
        for parity in range(2):
            for group in range(2):
                slots, rows = self.members(parity, group)
                for r in range(2):
                    regroup[parity, (2 * group + r) * pitch + at, 2 * slots + rows[r]] = 1
                for comp in range(2):
                    which = 2 * comp + parity
                    for side, owner in enumerate((comp, 1 - comp)):
                        columns[which, owner * local + slots, (2 * group + side) * pitch + at] = 1
                    own = comp * local + slots
                    courant[which, group, 0, at] = lat[own][:, None]
                    courant[which, group, 1, at] = lon[own][:, None]
        owners = [columns[:, :, 2 * g * pitch : (2 * g + 1) * pitch] for g in range(2)]
        rows_of = np.concatenate(owners, axis=2).transpose(0, 2, 1)
        half = ml_dtypes.bfloat16
        return (
            regroup.astype(half),
            regroup.transpose(0, 2, 1).astype(half),
            columns.astype(half),
            np.ascontiguousarray(rows_of).astype(half),
            courant,
        )


VMEM_LIMIT = 40 << 20


def whole(shape):
    return pl.BlockSpec(shape, lambda i, ids: (0,) * len(shape))


def picked(shape, at, rest=()):
    tail = (0,) * (len(shape) - 1 - len(rest))
    return pl.BlockSpec((1,) + tuple(shape[1:]), lambda i, ids: (ids[at],) + tuple(rest) + tail)


def call(body, ids, operands, specs, outs, scratch=(), flops=0):
    moved = sum(x.size * x.dtype.itemsize for x in operands if x.size < 1 << 21)
    return pl.pallas_call(
        body,
        grid_spec=pltpu.PrefetchScalarGridSpec(
            num_scalar_prefetch=1,
            grid=(1,),
            in_specs=specs,
            out_specs=[whole(o.shape) for o in outs],
            scratch_shapes=list(scratch),
        ),
        out_shape=outs,
        compiler_params=pltpu.CompilerParams(vmem_limit_bytes=VMEM_LIMIT),
        cost_estimate=pl.CostEstimate(flops=flops, bytes_accessed=moved, transcendentals=0),
    )(ids, *operands)


def in_order(ids, value, group):
    even = ids[0] == 0
    one, two = value[0:1], value[1:2]
    first, second = jnp.where(even, one, two), jnp.where(even, two, one)
    return (second, first) if group == 0 else (first, second)


def prep_body(plan, ids, regroup, energy, mask, *outs):
    ocean = mask[...].astype(F32)
    flat = energy[...].reshape(2 * plan.local, plan.columns)
    moved = jnp.dot(regroup[0], flat, preferred_element_type=F32)
    for group in range(2):
        rows = in_order(ids, ocean, group)
        for r in range(2):
            at = (2 * group + r) * plan.pitch
            outs[group][r] = (moved[at : at + plan.rows] * rows[r]).astype(BF16)


def sweep(u, p, q, a):
    d = p - u
    e = (q - p) - d
    return u + a * (d + (0.5 * a - 0.5) * e)


def lon_sweep(u, a, shift, size):
    def back(x):
        return pltpu.roll(x, shift % size, 1)

    d = back(u) - u
    e = back(d) - d
    return u + a * (d + (0.5 * a - 0.5) * e)


def half_steps(plan, group, ids, courant, depth, mask, depth8, ocean8, load, store):
    size = plan.columns
    for r, row in enumerate(in_order(ids, depth[...], group)):
        depth8[r] = jnp.broadcast_to(row, (8, size))
    for r, row in enumerate(in_order(ids, mask[...].astype(F32), group)):
        ocean8[r] = jnp.broadcast_to(row, (8, size))

    def block(start, rows, side):
        u0, u1, h0, h1 = load(start, rows)
        c_lat = courant[0, group, 0, pl.ds(start, rows)]
        c_lon = courant[0, group, 1, pl.ds(start, rows)]
        news = ([], [])
        for s in range(0, rows, 8):
            part = slice(s, s + 8)
            lat = jnp.concatenate([c_lat[part]] * (size // 128), axis=1)
            lon = jnp.concatenate([c_lon[part]] * (size // 128), axis=1)
            stencil = ((u0[part], h0[part], h1[part]), (u1[part], u0[part], h0[part]))
            for r in range(2):
                dep = depth8[r]
                u = sweep(*stencil[r], lat * dep)
                a = lon * dep
                if side == 0:
                    at = lax.broadcasted_iota(jnp.int32, (8, size), 0) + (start + s)
                    u = jnp.where(at < plan.half, lon_sweep(u, a, 1, size), lon_sweep(u, a, -1, size))
                else:
                    u = lon_sweep(u, a, side, size)
                news[r].append(u * ocean8[r])
        store(start, rows, jnp.concatenate(news[0], axis=0), jnp.concatenate(news[1], axis=0))

    east = plan.half // 16
    west = -(-plan.half // 16)
    full = plan.rows // 16

    @pl.loop(0, east)
    def _(i):
        block(pl.multiple_of(i * 16, 16), 16, 1)

    for i in range(east, west):
        block(i * 16, 16, 0)

    @pl.loop(west, full)
    def _(i):
        block(pl.multiple_of(i * 16, 16), 16, -1)

    if plan.rows % 16:
        block(full * 16, plan.rows % 16, -1)


def first_body(plan, group, ids, courant, depth, mask, field, halo, *rest):
    half, spectra, (depth8, ocean8) = rest[:2], rest[2:-2], rest[-2:]

    def load(start, rows):
        at = pl.ds(start, rows)
        return tuple(ref[r, at].astype(F32) for ref, r in ((field, 0), (field, 1), (halo, 1), (halo, 0)))

    def store(start, rows, new0, new1):
        at = pl.ds(start, rows)
        for r, new in enumerate((new0, new1)):
            half[r][at] = new
            if len(spectra) == 1:
                spectra[0][r, at] = new.astype(BF16)
            else:
                spectra[r][at] = new.astype(BF16)

    half_steps(plan, group, ids, courant, depth, mask, depth8, ocean8, load, store)


def last_body(plan, group, ids, courant, depth, mask, u0, u1, h0, h1, *rest):
    depth8, ocean8 = rest[-2:]

    def load(start, rows):
        at = pl.ds(start, rows)
        return tuple(ref[at].astype(F32) for ref in (u0, u1, h0, h1))

    def fill(ref):
        def store(start, rows, new0, new1):
            for r, new in enumerate((new0, new1)):
                at = r * plan.pitch + start
                if rows < 16:
                    new = jnp.concatenate([new, jnp.zeros((16 - rows, plan.columns), F32)], axis=0)
                ref[pl.ds(pl.multiple_of(at, 16), 16)] = new.astype(BF16)

        return store

    if group == 0:
        (done,) = rest[:1]
        half_steps(plan, group, ids, courant, depth, mask, depth8, ocean8, load, fill(done))
    else:
        earlier, restore, out, done = rest[:4]
        half_steps(plan, group, ids, courant, depth, mask, depth8, ocean8, load, fill(done))
        split = 2 * plan.pitch
        flat = jnp.dot(restore[0][:, :split], earlier[...], preferred_element_type=F32)
        flat += jnp.dot(restore[0][:, split:], done[...], preferred_element_type=F32)
        out[...] = flat.astype(BF16).reshape(plan.local, 2, plan.columns)


def weights_body(plan, ids, columns, rows_of, first, second, transfer, growth, first_out, second_out, transfer_out, growth_out):
    total = plan.total
    first_out[:total] = jnp.dot(first[...], columns[0], preferred_element_type=F32).astype(BF16)
    extra = plan.out_rows - total
    ones = lax.broadcasted_iota(jnp.int32, (extra, 4 * plan.pitch), 0) == 0
    first_out[total:] = jnp.where(ones, 1.0, 0.0).astype(BF16)
    second_out[...] = jnp.dot(second[...], columns[0], preferred_element_type=F32).astype(BF16)
    chosen = rows_of[0]
    transfer_out[...] = jnp.dot(chosen, transfer[...], preferred_element_type=F32).astype(BF16)
    rate = jnp.sum(chosen.astype(F32) * growth[...], axis=1, keepdims=True)
    growth_out[...] = jnp.broadcast_to(rate, growth_out.shape)


TILE = 256


def source_body(plan, turn, ids, first, second, transfer, growth, mask, own0, peer0, own1, peer1, half0, half1, *rest):
    full0, sent0, full1, sent1, cells = rest
    total, rows, pitch = plan.total, plan.rows, plan.pitch
    mine = (own0[turn], own1[...])
    for i, block in enumerate((mine[0], peer0[turn], mine[1], peer1[...])):
        whole_rows = rows // 16 * 16
        cells[i * pitch : i * pitch + whole_rows] = block[:whole_rows]
        if whole_rows < pitch:
            tail = block[whole_rows:].astype(F32)
            tail = jnp.concatenate([tail, jnp.zeros((pitch - rows, plan.columns), F32)], axis=0)
            cells[i * pitch + whole_rows : (i + 1) * pitch] = tail.astype(BF16)
    ocean = in_order(ids, mask[...].astype(F32), 0)[turn]
    for c in range(0, plan.columns, TILE):
        at = slice(c, c + TILE)
        piece = cells[:, at]
        forward = jnp.dot(first[...], piece, preferred_element_type=F32)
        backward = jnp.dot(second[...], piece, preferred_element_type=F32)
        product = (forward[:total] * backward).astype(BF16)
        nonlinear = jnp.dot(transfer[...], product, preferred_element_type=F32)
        level = forward[total : total + 1] / total
        damping = level * level / (1.0 + level * level)
        for group, (half, full, sent) in enumerate(((half0, full0, sent0), (half1, full1, sent1))):
            begin = group * pitch
            rate = jnp.concatenate([growth[begin : begin + rows]] * (TILE // 128), axis=1)
            spectra = cells[2 * group * pitch : (2 * group + 1) * pitch, at].astype(F32)[:rows]
            source = SOURCE_STEP * (nonlinear[begin : begin + rows] + (rate - damping) * spectra)
            updated = ocean[:, at] * (half[:, at] + source.astype(BF16).astype(F32))
            full[:, at] = updated
            sent[:, at] = updated.astype(BF16)


def paired_shards(energy, depth_speed, ocean_mask, interp_first, interp_second, transfer_matrix, growth):
    plan = Plan(energy.shape[0], energy.shape[2])
    size, rows, pitch, total = plan.columns, plan.rows, plan.pitch, plan.total
    regroup, restore, columns, rows_of, courant = plan.tables()
    bands = lax.axis_size("band")
    parity = lax.axis_index("band") % 2
    ids = jnp.stack([parity, 2 * lax.axis_index("comp") + parity]).astype(jnp.int32)
    growth = growth.reshape(1, total)

    inner = [(i, i ^ 1) for i in range(bands)]
    outer = [(i, j) for i in range(1, bands - 1) for j in [i + 1 if i % 2 else i - 1]]
    peers = [(0, 1), (1, 0)]

    def shape(*dims, kind=BF16):
        return jax.ShapeDtypeStruct(dims, kind)

    sweeps = 2 * 40 * rows * size
    rims = [pltpu.VMEM((2, 8, size), F32)] * 2

    fields = call(
        functools.partial(prep_body, plan),
        ids,
        (regroup, energy, ocean_mask),
        [picked(regroup.shape, 0), whole(energy.shape), whole(ocean_mask.shape)],
        [shape(2, rows, size)] * 2,
        flops=2 * 4 * pitch * 2 * plan.local * size,
    )
    halo0 = lax.ppermute(fields[1], "band", inner)
    halo1 = lax.ppermute(fields[0], "band", outer)

    def first_step(group, halo, spectra):
        return call(
            functools.partial(first_body, plan, group),
            ids,
            (courant, depth_speed, ocean_mask, fields[group], halo),
            [picked(courant.shape, 1)] + [whole(x.shape) for x in (depth_speed, ocean_mask, halo, halo)],
            [shape(rows, size, kind=F32)] * 2 + spectra,
            rims,
            flops=sweeps,
        )

    *half0, own0 = first_step(0, halo0, [shape(2, rows, size)])
    peer0 = lax.ppermute(own0, "comp", peers)
    first, second, transfer, rate = call(
        functools.partial(weights_body, plan),
        ids,
        (columns, rows_of, interp_first, interp_second, transfer_matrix, growth),
        [picked(columns.shape, 1), picked(rows_of.shape, 1)] + [whole((total, total))] * 3 + [whole((1, total))],
        [shape(plan.out_rows, 4 * pitch), shape(total, 4 * pitch), shape(2 * pitch, total), shape(2 * pitch, 128, kind=F32)],
        flops=2 * total * total * 10 * pitch,
    )
    *half1, own1_0, own1_1 = first_step(1, halo1, [shape(rows, size)] * 2)
    own1 = (own1_0, own1_1)
    peer1 = [None, None]
    peer1[1] = lax.ppermute(own1[1], "comp", peers)
    peer1[0] = lax.ppermute(own1[0], "comp", peers)

    full0, sent0, full1, sent1 = [None] * 2, [None] * 2, [None] * 2, [None] * 2
    for turn in range(2):
        operands = (
            first, second, transfer, rate, ocean_mask, own0, peer0, own1[1 - turn], peer1[1 - turn], half0[turn], half1[1 - turn],
        )
        full0[turn], sent0[turn], full1[1 - turn], sent1[1 - turn] = call(
            functools.partial(source_body, plan, turn),
            ids,
            operands,
            [whole(x.shape) for x in operands],
            [shape(rows, size, kind=F32), shape(rows, size)] * 2,
            [pltpu.VMEM((4 * pitch, size), BF16)],
            flops=2 * total * 10 * pitch * size,
        )
    rim1 = [lax.ppermute(x, "band", outer) for x in sent0]
    rim0 = [lax.ppermute(x, "band", inner) for x in sent1]

    def last_step(group, full, rim, more, outs, scratch):
        operands = (courant, depth_speed, ocean_mask, full[0], full[1], rim[1], rim[0]) + more
        specs = [picked(courant.shape, 1)] + [whole(x.shape) for x in operands[1:7]]
        if more:
            specs += [whole(more[0].shape), picked(more[1].shape, 0)]
        return call(
            functools.partial(last_body, plan, group), ids, operands, specs, outs, list(scratch) + rims, flops=sweeps
        )

    (early,) = last_step(0, full0, rim0, (), [shape(2 * pitch, size)], ())
    (out,) = last_step(1, full1, rim1, (early, restore), [shape(*energy.shape)], [pltpu.VMEM((2 * pitch, size), BF16)])
    return out


def solution(mesh):
    def shards(energy, *others):
        paired = lax.axis_size("comp") == 2 and lax.axis_size("band") % 2 == 0
        if paired and energy.shape[0] % ND == 0 and energy.shape[1] == 2 and energy.shape[2] % TILE == 0:
            return paired_shards(energy, *others)
        return general_shards(energy, *others)

    in_specs = (P("comp", "band", None), P("band", None), P("band", None), P(), P(), P(), P())
    out_specs = P("comp", "band", None)
    return jax.shard_map(shards, mesh=mesh, in_specs=in_specs, out_specs=out_specs, check_vma=False)
```

```python
import functools
import math

import jax
import jax.numpy as jnp
from jax import lax
from jax.experimental import pallas as pl
from jax.experimental.pallas import tpu as pltpu
from jax.sharding import PartitionSpec as P

ND = 24


SOURCE_STEP = 0.5
COURANT_TOP = 0.9
FREQ_RATIO = 1.1

F32 = jnp.float32
BF16 = jnp.bfloat16


def with_halo(value, sides, width):
    for axis, dim in sides:
        peers, length = (lax.axis_size(axis), value.shape[dim])
        up = [(i, (i + 1) % peers) for i in range(peers - 1)]
        down = [(j, i) for i, j in up]
        last = lax.slice_in_dim(value, length - width, length, axis=dim)
        first = lax.slice_in_dim(value, 0, width, axis=dim)
        before = lax.ppermute(last, axis, up)
        after = lax.ppermute(first, axis, down)
        value = jnp.concatenate([before, value, after], axis=dim)
    return value


def courant_numbers(first_comp, local_comps):
    components = first_comp + jnp.arange(local_comps, dtype=jnp.int32)
    frequency = (components // ND).astype(jnp.float32)
    direction = (components % ND).astype(jnp.float32)
    heading = 2.0 * jnp.pi * (direction + 0.5) / ND
    factor = COURANT_TOP * jnp.power(jnp.float32(FREQ_RATIO), -frequency)
    return (factor * jnp.cos(heading), factor * jnp.sin(heading))


def upwind(middle, lower_one, lower_two, upper_one, upper_two, courant):
    magnitude = jnp.abs(courant)
    first_up = jnp.where(courant > 0, lower_one, upper_one)
    second_up = jnp.where(courant > 0, lower_two, upper_two)
    return (
        middle
        - 0.5 * magnitude * (3.0 * middle - 4.0 * first_up + second_up)
        + 0.5 * magnitude * magnitude * (middle - 2.0 * first_up + second_up)
    )


def half_step(extended, lat_courant, lon_courant, depth_speed, ocean):
    widened = extended.astype(jnp.float32)
    swept = upwind(
        widened[:, 2:-2],
        widened[:, 1:-3],
        widened[:, :-4],
        widened[:, 3:-1],
        widened[:, 4:],
        lat_courant[:, None, None] * depth_speed[None],
    )
    lon_values = lon_courant[:, None, None] * depth_speed[None]
    swept = upwind(
        swept,
        jnp.roll(swept, 1, axis=2),
        jnp.roll(swept, 2, axis=2),
        jnp.roll(swept, -1, axis=2),
        jnp.roll(swept, -2, axis=2),
        lon_values,
    )
    return ocean[None] * swept


def source_terms(cell_spectra, interp_first, interp_second, transfer_matrix, growth):
    forward_interp = jnp.dot(interp_first, cell_spectra, preferred_element_type=jnp.float32)
    backward_interp = jnp.dot(interp_second, cell_spectra, preferred_element_type=jnp.float32)
    product = (forward_interp * backward_interp).astype(jnp.bfloat16)
    nonlinear = jnp.dot(transfer_matrix, product, preferred_element_type=jnp.float32)
    spectra32 = cell_spectra.astype(jnp.float32)
    mean_level = jnp.mean(spectra32, axis=0)
    damping = mean_level * mean_level / (1.0 + mean_level * mean_level)
    total = SOURCE_STEP * (nonlinear + (growth[:, None] - damping[None]) * spectra32)
    return total.astype(jnp.bfloat16)


def general_shards(energy, depth_speed, ocean_mask, interp_first, interp_second, transfer_matrix, growth):
    local_comps = energy.shape[0]
    lat_courant, lon_courant = courant_numbers(lax.axis_index("comp") * local_comps, local_comps)
    ocean = ocean_mask.astype(jnp.float32)
    start = (ocean[None] * energy.astype(jnp.float32)).astype(jnp.bfloat16)
    rimmed = with_halo(start, (("band", 1),), 2)
    half_one = half_step(rimmed, lat_courant, lon_courant, depth_speed, ocean)
    spectra = half_one.astype(jnp.bfloat16)
    block_in = lax.all_to_all(spectra, "comp", split_axis=2, concat_axis=0, tiled=True)
    total_comps = block_in.shape[0]
    flat_cells = block_in.reshape(total_comps, -1)
    result = source_terms(flat_cells, interp_first, interp_second, transfer_matrix, growth)
    source = lax.all_to_all(
        result.reshape(block_in.shape), "comp", split_axis=0, concat_axis=2, tiled=True
    ).astype(jnp.float32)
    updated = ocean[None] * (half_one + source)
    rimmed_mid = with_halo(updated, (("band", 1),), 2)
    final_field = half_step(rimmed_mid, lat_courant, lon_courant, depth_speed, ocean)
    return final_field.astype(jnp.bfloat16)


class Plan:
    def __init__(self, local_comps, columns):
        self.local = local_comps
        self.total = 2 * local_comps
        self.columns = columns
        self.half = local_comps // 4
        self.slots = 2 * self.half
        self.rows = -(-self.slots // 8) * 8
        self.pitch = -(-self.slots // 16) * 16
        self.out_rows = -(-(self.total + 1) // 16) * 16

    def slot_parts(self, slot):
        east = slot < self.half
        j = jnp.where(east, slot, slot - self.half)
        f = (j * 10923) >> 16
        return east, f, j - 6 * f

    def courant(self, ids, group):
        east, f, turn = self.slot_parts(lax.broadcasted_iota(jnp.int32, (self.rows, 128), 0))
        factor = jnp.where(ids[1] >= 2, COURANT_TOP * FREQ_RATIO ** -(self.local // ND), COURANT_TOP).astype(F32)
        for bit in range(self.local.bit_length()):
            if 1 << bit < self.local // ND:
                factor = factor * jnp.where((f >> bit) & 1 == 1, FREQ_RATIO ** -(1 << bit), 1.0)
        falling = east == jnp.logical_not(southward(ids, group))
        place = jnp.where(falling, turn, 5 - turn)
        cosine, sine = factor, factor
        for i in range(6):
            cosine = jnp.where(place == i, factor * math.cos(2 * math.pi * (i + 0.5) / ND), cosine)
            sine = jnp.where(place == i, factor * math.sin(2 * math.pi * (i + 0.5) / ND), sine)
        return cosine, sine

    def slot_comp(self, slot, south):
        east, f, turn = self.slot_parts(slot)
        comp = ND * f + turn + jnp.where(east, jnp.where(south, 6, 0), jnp.where(south, 12, 18))
        return jnp.where(slot < self.slots, comp, -4 * self.total)


def southward(ids, group):
    return ids[0] == group


def actual_row(r, south):
    return jnp.where(south, 1 - r, r)


def one_hot(match):
    return jnp.where(match, 1.0, 0.0).astype(BF16)


def spread(value, width):
    parts = [value] * (width // 128)
    if width % 128:
        parts.append(value[:, : width % 128])
    return jnp.concatenate(parts, axis=1)


VMEM = pl.BlockSpec(memory_space=pltpu.VMEM)
SMEM = pl.BlockSpec(memory_space=pltpu.SMEM)


def call(body, ids, operands, outs, scratch=(), limit=40, cost=1.0):
    return pl.pallas_call(
        body,
        in_specs=[SMEM] + [VMEM] * len(operands),
        out_specs=[VMEM] * len(outs),
        scratch_shapes=list(scratch),
        out_shape=outs,
        compiler_params=pltpu.CompilerParams(vmem_limit_bytes=int(limit * 2**20)),
        cost_estimate=pl.CostEstimate(flops=int(cost * 1.1e9), bytes_accessed=0, transcendentals=0),
    )(ids, *operands)


def in_order(ids, value, group):
    south = southward(ids, group)
    one, two = value[0:1], value[1:2]
    return jnp.where(south, two, one), jnp.where(south, one, two)


def prep_body(plan, ids, energy, mask, field0, field1, courant, regroup):
    for group in range(2):
        courant[group, 0], courant[group, 1] = plan.courant(ids, group)
    width, pitch = 2 * plan.local, plan.pitch
    column = lax.broadcasted_iota(jnp.int32, (pitch, width), 1)
    for group in range(2):
        south = southward(ids, group)
        comp = plan.slot_comp(lax.broadcasted_iota(jnp.int32, (pitch, 128), 0), south)
        for r in range(2):
            begin = (2 * group + r) * pitch
            regroup[begin : begin + pitch] = one_hot(spread(2 * comp + actual_row(r, south), width) == column)
    ocean = mask[...].astype(F32)
    flat = energy[...].reshape(width, plan.columns)
    moved = jnp.dot(regroup[...], flat, preferred_element_type=F32)
    for group, field in enumerate((field0, field1)):
        rows = in_order(ids, ocean, group)
        for r in range(2):
            at = (2 * group + r) * pitch
            field[r] = (moved[at : at + plan.rows] * rows[r]).astype(BF16)


def sweep(u, p, q, a):
    d = p - u
    e = (q - p) - d
    return u + a * (d + (0.5 * a - 0.5) * e)


def lon_sweep(u, a, shift, size):
    def back(x):
        return pltpu.roll(x, shift % size, 1)

    d = back(u) - u
    e = back(d) - d
    return u + a * (d + (0.5 * a - 0.5) * e)


def half_steps(plan, group, ids, courant, depth, mask, depth8, ocean8, load, store):
    size = plan.columns
    for r, row in enumerate(in_order(ids, depth[...], group)):
        depth8[r] = jnp.broadcast_to(row, (8, size))
    for r, row in enumerate(in_order(ids, mask[...].astype(F32), group)):
        ocean8[r] = jnp.broadcast_to(row, (8, size))

    def block(start, rows, side):
        u0, u1, h0, h1 = load(start, rows)
        c_lat = courant[group, 0, pl.ds(start, rows)]
        c_lon = courant[group, 1, pl.ds(start, rows)]
        news = ([], [])
        for s in range(0, rows, 8):
            part = slice(s, s + 8)
            lat, lon = spread(c_lat[part], size), spread(c_lon[part], size)
            stencil = ((u0[part], h0[part], h1[part]), (u1[part], u0[part], h0[part]))
            for r in range(2):
                dep = depth8[r]
                u = sweep(*stencil[r], lat * dep)
                a = lon * dep
                if side == 0:
                    at = lax.broadcasted_iota(jnp.int32, (8, size), 0) + (start + s)
                    u = jnp.where(at < plan.half, lon_sweep(u, a, 1, size), lon_sweep(u, a, -1, size))
                else:
                    u = lon_sweep(u, a, side, size)
                news[r].append(u * ocean8[r])
        store(start, rows, jnp.concatenate(news[0], axis=0), jnp.concatenate(news[1], axis=0))

    east = plan.half // 16
    west = -(-plan.half // 16)
    full = plan.rows // 16

    @pl.loop(0, east, unroll=2)
    def _(i):
        block(pl.multiple_of(i * 16, 16), 16, 1)

    for i in range(east, west):
        block(i * 16, 16, 0)

    @pl.loop(west, full, unroll=2)
    def _(i):
        block(pl.multiple_of(i * 16, 16), 16, -1)

    if plan.rows % 16:
        block(full * 16, plan.rows % 16, -1)


def first_body(plan, group, ids, courant, depth, mask, field, halo, *rest):
    half, spectra, (depth8, ocean8) = rest[:2], rest[2:-2], rest[-2:]

    def load(start, rows):
        at = pl.ds(start, rows)
        return tuple(ref[r, at].astype(F32) for ref, r in ((field, 0), (field, 1), (halo, 1), (halo, 0)))

    def store(start, rows, new0, new1):
        at = pl.ds(start, rows)
        for r, new in enumerate((new0, new1)):
            half[r][at] = new
            if len(spectra) == 1:
                spectra[0][r, at] = new.astype(BF16)
            else:
                spectra[r][at] = new.astype(BF16)

    half_steps(plan, group, ids, courant, depth, mask, depth8, ocean8, load, store)


def last_body(plan, group, ids, courant, depth, mask, u0, u1, h0, h1, *rest):
    *rest, done, depth8, ocean8 = rest
    width, pitch = 2 * plan.local, plan.pitch

    def load(start, rows):
        at = pl.ds(start, rows)
        return tuple(ref[at].astype(F32) for ref in (u0, u1, h0, h1))

    def store(start, rows, new0, new1):
        for r, new in enumerate((new0, new1)):
            at = r * pitch + start
            if rows < 16:
                new = jnp.concatenate([new, jnp.zeros((16 - rows, plan.columns), F32)], axis=0)
            done[pl.ds(pl.multiple_of(at, 16), 16)] = new.astype(BF16)

    half_steps(plan, group, ids, courant, depth, mask, depth8, ocean8, load, store)
    if group == 0:
        partial, restore = rest
        tables = []
        for g in range(2):
            lane = lax.broadcasted_iota(jnp.int32, (8, 2 * pitch), 1)
            r = jnp.where(lane >= pitch, 1, 0)
            south = southward(ids, g)
            target = 2 * plan.slot_comp(lane - pitch * r, south) + actual_row(r, south)
            target = jnp.concatenate([target] * (width // 8), axis=0)
            tables.append(one_hot(target == lax.broadcasted_iota(jnp.int32, (width, 2 * pitch), 0)))
        restore[...] = tables[1]
        partial[...] = jnp.dot(tables[0], done[...], preferred_element_type=F32)
    else:
        partial, restore, out = rest
        flat = partial[...] + jnp.dot(restore[...], done[...], preferred_element_type=F32)
        out[...] = flat.astype(BF16).reshape(plan.local, 2, plan.columns)


def weights_body(plan, ids, first, second, transfer, growth, first_out, second_out, transfer_out, growth_out, columns):
    total, local, pitch = plan.total, plan.local, plan.pitch
    comp_index = ids[1] // 2
    chosen = []
    for group in range(2):
        south = southward(ids, group)
        lane = lax.broadcasted_iota(jnp.int32, (8, 2 * pitch), 1)
        other = jnp.where(lane >= pitch, 1, 0)
        owner = jnp.where(other == 0, comp_index, 1 - comp_index)
        source = plan.slot_comp(lane - pitch * other, south) + local * owner
        source = jnp.concatenate([source] * (total // 8), axis=0)
        hot = one_hot(source == lax.broadcasted_iota(jnp.int32, (total, 2 * pitch), 0))
        columns[:, 2 * group * pitch : 2 * (group + 1) * pitch] = hot
        comp = plan.slot_comp(lax.broadcasted_iota(jnp.int32, (pitch, 128), 0), south) + local * comp_index
        chosen.append(spread(comp, total) == lax.broadcasted_iota(jnp.int32, (pitch, total), 1))
    first_out[:total] = jnp.dot(first[...], columns[...], preferred_element_type=F32).astype(BF16)
    extra = plan.out_rows - total
    first_out[total:] = one_hot(lax.broadcasted_iota(jnp.int32, (extra, 4 * pitch), 0) == 0)
    second_out[...] = jnp.dot(second[...], columns[...], preferred_element_type=F32).astype(BF16)
    for group in range(2):
        at = slice(group * pitch, (group + 1) * pitch)
        pick = jnp.where(chosen[group], 1.0, 0.0)
        transfer_out[at] = jnp.dot(pick.astype(BF16), transfer[...], preferred_element_type=F32).astype(BF16)
        rate = jnp.sum(pick * growth[...], axis=1, keepdims=True)
        growth_out[at] = jnp.broadcast_to(rate, (pitch, 128))


TILE = 256


def fill_cells(plan, cells, blocks):
    rows, pitch = plan.rows, plan.pitch
    for i, block in enumerate(blocks):
        whole_rows = rows // 16 * 16
        cells[i * pitch : i * pitch + whole_rows] = block[:whole_rows]
        if whole_rows < pitch:
            tail = block[whole_rows:].astype(F32)
            tail = jnp.concatenate([tail, jnp.zeros((pitch - rows, plan.columns), F32)], axis=0)
            cells[i * pitch + whole_rows : (i + 1) * pitch] = tail.astype(BF16)


def early_body(plan, ids, first, second, own0, peer0, own1_0, own1_1, *rest):
    outs, cells = rest[:4], rest[4]
    own1 = (own1_0, own1_1)
    known = 3 * plan.pitch
    for turn in range(2):
        fill_cells(plan, cells, (own0[turn], peer0[turn], own1[1 - turn][...]))
        for c in range(0, plan.columns, TILE):
            at = slice(c, c + TILE)
            outs[2 * turn][:, at] = jnp.dot(first[:, :known], cells[:, at], preferred_element_type=F32)
            outs[2 * turn + 1][:, at] = jnp.dot(second[:, :known], cells[:, at], preferred_element_type=F32)


def source_body(plan, turn, ids, first, second, transfer, growth, mask, *rest):
    (early_first, early_second, own0, own1, peer1, half0, half1, full0, sent0, full1, sent1, cells) = rest
    total, rows, pitch = plan.total, plan.rows, plan.pitch
    known = 3 * pitch
    fill_cells(plan, cells, (peer1[...],))
    ocean = in_order(ids, mask[...].astype(F32), 0)[turn]
    for c in range(0, plan.columns, TILE):
        at = slice(c, c + TILE)
        piece = cells[:, at]
        forward = early_first[:, at] + jnp.dot(first[:, known:], piece, preferred_element_type=F32)
        backward = early_second[:, at] + jnp.dot(second[:, known:], piece, preferred_element_type=F32)
        product = (forward[:total] * backward).astype(BF16)
        nonlinear = jnp.dot(transfer[...], product, preferred_element_type=F32)
        level = forward[total : total + 1] / total
        damping = level * level / (1.0 + level * level)
        for group, (own, half, full, sent) in enumerate(((own0, half0, full0, sent0), (own1, half1, full1, sent1))):
            begin = group * pitch
            rate = spread(growth[begin : begin + rows], TILE)
            spectra = (own[turn, :, at] if group == 0 else own[:, at]).astype(F32)
            source = SOURCE_STEP * (nonlinear[begin : begin + rows] + (rate - damping) * spectra)
            updated = ocean[:, at] * (half[:, at] + source.astype(BF16).astype(F32))
            full[:, at] = updated
            sent[:, at] = updated.astype(BF16)


def paired_shards(energy, depth_speed, ocean_mask, interp_first, interp_second, transfer_matrix, growth):
    plan = Plan(energy.shape[0], energy.shape[2])
    size, rows, pitch, total = plan.columns, plan.rows, plan.pitch, plan.total
    bands = lax.axis_size("band")
    parity = lax.axis_index("band") % 2
    ids = jnp.stack([parity, 2 * lax.axis_index("comp") + parity]).astype(jnp.int32)

    inner = [(i, i ^ 1) for i in range(bands)]
    outer = [(i, j) for i in range(1, bands - 1) for j in [i + 1 if i % 2 else i - 1]]
    peers = [(0, 1), (1, 0)]

    def shape(*dims, kind=BF16):
        return jax.ShapeDtypeStruct(dims, kind)

    rims = [pltpu.VMEM((2, 8, size), F32)] * 2

    field0, field1, courant = call(
        functools.partial(prep_body, plan),
        ids,
        (energy, ocean_mask),
        [shape(2, rows, size)] * 2 + [shape(2, 2, rows, 128, kind=F32)],
        [pltpu.VMEM((4 * pitch, 2 * plan.local), BF16)],
        cost=2,
    )
    halo0 = lax.ppermute(field1, "band", inner)
    halo1 = lax.ppermute(field0, "band", outer)

    def first_step(group, field, halo, spectra):
        operands = (courant, depth_speed, ocean_mask, field, halo)
        outs = [shape(rows, size, kind=F32)] * 2 + spectra
        return call(functools.partial(first_body, plan, group), ids, operands, outs, rims, limit=20, cost=2)

    *half0, own0 = first_step(0, field0, halo0, [shape(2, rows, size)])
    peer0 = lax.ppermute(own0, "comp", peers)
    first, second, transfer, rate = call(
        functools.partial(weights_body, plan),
        ids,
        (interp_first, interp_second, transfer_matrix, growth.reshape(1, total)),
        [shape(plan.out_rows, 4 * pitch), shape(total, 4 * pitch), shape(2 * pitch, total), shape(2 * pitch, 128, kind=F32)],
        [pltpu.VMEM((total, 4 * pitch), BF16)],
        cost=3,
    )
    *half1, own1_0, own1_1 = first_step(1, field1, halo1, [shape(rows, size)] * 2)
    own1 = (own1_0, own1_1)
    peer1 = [None, None]
    peer1[1] = lax.ppermute(own1[1], "comp", peers)
    peer1[0] = lax.ppermute(own1[0], "comp", peers)
    early = call(
        functools.partial(early_body, plan),
        ids,
        (first, second, own0, peer0, own1_0, own1_1),
        [shape(plan.out_rows, size, kind=F32), shape(total, size, kind=F32)] * 2,
        [pltpu.VMEM((3 * pitch, size), BF16)],
        limit=30,
        cost=4,
    )

    full0, sent0, full1, sent1 = [None] * 2, [None] * 2, [None] * 2, [None] * 2
    for turn in range(2):
        full0[turn], sent0[turn], full1[1 - turn], sent1[1 - turn] = call(
            functools.partial(source_body, plan, turn),
            ids,
            (first, second, transfer, rate, ocean_mask, early[2 * turn], early[2 * turn + 1])
            + (own0, own1[1 - turn], peer1[1 - turn], half0[turn], half1[1 - turn]),
            [shape(rows, size, kind=F32), shape(rows, size)] * 2,
            [pltpu.VMEM((pitch, size), BF16)],
            limit=30,
            cost=4,
        )
    rim1 = [lax.ppermute(x, "band", outer) for x in sent0]
    rim0 = [lax.ppermute(x, "band", inner) for x in sent1]

    def last_step(group, full, rim, more, outs, cost):
        operands = (courant, depth_speed, ocean_mask, full[0], full[1], rim[1], rim[0]) + more
        scratch = [pltpu.VMEM((2 * pitch, size), BF16)] + rims
        return call(functools.partial(last_body, plan, group), ids, operands, outs, scratch, limit=30, cost=cost)

    width = 2 * plan.local
    full0[0], rim1[0] = lax.optimization_barrier((full0[0], rim1[0]))
    more = last_step(0, full0, rim0, (), [shape(width, size, kind=F32), shape(width, 2 * pitch)], 3)
    (out,) = last_step(1, full1, rim1, tuple(more), [shape(*energy.shape)], 4)
    return out


def solution(mesh):
    def shards(energy, *others):
        paired = lax.axis_size("comp") == 2 and lax.axis_size("band") % 2 == 0
        if paired and energy.shape[0] % ND == 0 and energy.shape[1] == 2 and energy.shape[2] % TILE == 0:
            return paired_shards(energy, *others)
        return general_shards(energy, *others)

    in_specs = (P("comp", "band", None), P("band", None), P("band", None), P(), P(), P(), P())
    out_specs = P("comp", "band", None)
    return jax.shard_map(shards, mesh=mesh, in_specs=in_specs, out_specs=out_specs, check_vma=False)
```

```python
import functools
import math

import jax
import jax.numpy as jnp
from jax import lax
from jax.experimental import pallas as pl
from jax.experimental.pallas import tpu as pltpu
from jax.sharding import PartitionSpec as P

ND = 24


SOURCE_STEP = 0.5
COURANT_TOP = 0.9
FREQ_RATIO = 1.1

F32 = jnp.float32
BF16 = jnp.bfloat16


def with_halo(value, sides, width):
    for axis, dim in sides:
        peers, length = (lax.axis_size(axis), value.shape[dim])
        up = [(i, (i + 1) % peers) for i in range(peers - 1)]
        down = [(j, i) for i, j in up]
        last = lax.slice_in_dim(value, length - width, length, axis=dim)
        first = lax.slice_in_dim(value, 0, width, axis=dim)
        before = lax.ppermute(last, axis, up)
        after = lax.ppermute(first, axis, down)
        value = jnp.concatenate([before, value, after], axis=dim)
    return value


def courant_numbers(first_comp, local_comps):
    components = first_comp + jnp.arange(local_comps, dtype=jnp.int32)
    frequency = (components // ND).astype(jnp.float32)
    direction = (components % ND).astype(jnp.float32)
    heading = 2.0 * jnp.pi * (direction + 0.5) / ND
    factor = COURANT_TOP * jnp.power(jnp.float32(FREQ_RATIO), -frequency)
    return (factor * jnp.cos(heading), factor * jnp.sin(heading))


def upwind(middle, lower_one, lower_two, upper_one, upper_two, courant):
    magnitude = jnp.abs(courant)
    first_up = jnp.where(courant > 0, lower_one, upper_one)
    second_up = jnp.where(courant > 0, lower_two, upper_two)
    return (
        middle
        - 0.5 * magnitude * (3.0 * middle - 4.0 * first_up + second_up)
        + 0.5 * magnitude * magnitude * (middle - 2.0 * first_up + second_up)
    )


def half_step(extended, lat_courant, lon_courant, depth_speed, ocean):
    widened = extended.astype(jnp.float32)
    swept = upwind(
        widened[:, 2:-2],
        widened[:, 1:-3],
        widened[:, :-4],
        widened[:, 3:-1],
        widened[:, 4:],
        lat_courant[:, None, None] * depth_speed[None],
    )
    lon_values = lon_courant[:, None, None] * depth_speed[None]
    swept = upwind(
        swept,
        jnp.roll(swept, 1, axis=2),
        jnp.roll(swept, 2, axis=2),
        jnp.roll(swept, -1, axis=2),
        jnp.roll(swept, -2, axis=2),
        lon_values,
    )
    return ocean[None] * swept


def source_terms(cell_spectra, interp_first, interp_second, transfer_matrix, growth):
    forward_interp = jnp.dot(interp_first, cell_spectra, preferred_element_type=jnp.float32)
    backward_interp = jnp.dot(interp_second, cell_spectra, preferred_element_type=jnp.float32)
    product = (forward_interp * backward_interp).astype(jnp.bfloat16)
    nonlinear = jnp.dot(transfer_matrix, product, preferred_element_type=jnp.float32)
    spectra32 = cell_spectra.astype(jnp.float32)
    mean_level = jnp.mean(spectra32, axis=0)
    damping = mean_level * mean_level / (1.0 + mean_level * mean_level)
    total = SOURCE_STEP * (nonlinear + (growth[:, None] - damping[None]) * spectra32)
    return total.astype(jnp.bfloat16)


def general_shards(energy, depth_speed, ocean_mask, interp_first, interp_second, transfer_matrix, growth):
    local_comps = energy.shape[0]
    lat_courant, lon_courant = courant_numbers(lax.axis_index("comp") * local_comps, local_comps)
    ocean = ocean_mask.astype(jnp.float32)
    start = (ocean[None] * energy.astype(jnp.float32)).astype(jnp.bfloat16)
    rimmed = with_halo(start, (("band", 1),), 2)
    half_one = half_step(rimmed, lat_courant, lon_courant, depth_speed, ocean)
    spectra = half_one.astype(jnp.bfloat16)
    block_in = lax.all_to_all(spectra, "comp", split_axis=2, concat_axis=0, tiled=True)
    total_comps = block_in.shape[0]
    flat_cells = block_in.reshape(total_comps, -1)
    result = source_terms(flat_cells, interp_first, interp_second, transfer_matrix, growth)
    source = lax.all_to_all(
        result.reshape(block_in.shape), "comp", split_axis=0, concat_axis=2, tiled=True
    ).astype(jnp.float32)
    updated = ocean[None] * (half_one + source)
    rimmed_mid = with_halo(updated, (("band", 1),), 2)
    final_field = half_step(rimmed_mid, lat_courant, lon_courant, depth_speed, ocean)
    return final_field.astype(jnp.bfloat16)


class Plan:
    def __init__(self, local_comps, columns):
        self.local = local_comps
        self.total = 2 * local_comps
        self.columns = columns
        self.half = local_comps // 4
        self.slots = 2 * self.half
        self.rows = -(-self.slots // 8) * 8
        self.pitch = -(-self.slots // 16) * 16
        self.out_rows = -(-(self.total + 1) // 16) * 16

    def slot_parts(self, slot):
        east = slot < self.half
        j = jnp.where(east, slot, slot - self.half)
        f = (j * 10923) >> 16
        return east, f, j - 6 * f

    def courant(self, ids, group):
        east, f, turn = self.slot_parts(lax.broadcasted_iota(jnp.int32, (self.rows, 128), 0))
        factor = jnp.where(ids[1] >= 2, COURANT_TOP * FREQ_RATIO ** -(self.local // ND), COURANT_TOP).astype(F32)
        for bit in range(self.local.bit_length()):
            if 1 << bit < self.local // ND:
                factor = factor * jnp.where((f >> bit) & 1 == 1, FREQ_RATIO ** -(1 << bit), 1.0)
        falling = east == jnp.logical_not(southward(ids, group))
        place = jnp.where(falling, turn, 5 - turn)
        cosine, sine = factor, factor
        for i in range(6):
            cosine = jnp.where(place == i, factor * math.cos(2 * math.pi * (i + 0.5) / ND), cosine)
            sine = jnp.where(place == i, factor * math.sin(2 * math.pi * (i + 0.5) / ND), sine)
        return cosine, sine

    def slot_comp(self, slot, south):
        east, f, turn = self.slot_parts(slot)
        comp = ND * f + turn + jnp.where(east, jnp.where(south, 6, 0), jnp.where(south, 12, 18))
        return jnp.where(slot < self.slots, comp, -4 * self.total)


def southward(ids, group):
    return ids[0] == group


def actual_row(r, south):
    return jnp.where(south, 1 - r, r)


def one_hot(match):
    return jnp.where(match, 1.0, 0.0).astype(BF16)


def spread(value, width):
    parts = [value] * (width // 128)
    if width % 128:
        parts.append(value[:, : width % 128])
    return jnp.concatenate(parts, axis=1)


VMEM = pl.BlockSpec(memory_space=pltpu.VMEM)
SMEM = pl.BlockSpec(memory_space=pltpu.SMEM)


def call(body, ids, operands, outs, scratch=(), limit=40, cost=1.0):
    return pl.pallas_call(
        body,
        in_specs=[SMEM] + [VMEM] * len(operands),
        out_specs=[VMEM] * len(outs),
        scratch_shapes=list(scratch),
        out_shape=outs,
        compiler_params=pltpu.CompilerParams(vmem_limit_bytes=int(limit * 2**20)),
        cost_estimate=pl.CostEstimate(flops=int(cost * 1.1e9), bytes_accessed=0, transcendentals=0),
    )(ids, *operands)


def in_order(ids, value, group):
    south = southward(ids, group)
    one, two = value[0:1], value[1:2]
    return jnp.where(south, two, one), jnp.where(south, one, two)


def prep_body(plan, ids, energy, mask, field0, field1, courant, regroup):
    for group in range(2):
        courant[group, 0], courant[group, 1] = plan.courant(ids, group)
    width, pitch = 2 * plan.local, plan.pitch
    column = lax.broadcasted_iota(jnp.int32, (pitch, width), 1)
    for group in range(2):
        south = southward(ids, group)
        comp = plan.slot_comp(lax.broadcasted_iota(jnp.int32, (pitch, 128), 0), south)
        for r in range(2):
            begin = (2 * group + r) * pitch
            regroup[begin : begin + pitch] = one_hot(spread(2 * comp + actual_row(r, south), width) == column)
    ocean = mask[...].astype(F32)
    flat = energy[...].reshape(width, plan.columns)
    moved = jnp.dot(regroup[...], flat, preferred_element_type=F32)
    for group, field in enumerate((field0, field1)):
        rows = in_order(ids, ocean, group)
        for r in range(2):
            at = (2 * group + r) * pitch
            field[r] = (moved[at : at + plan.rows] * rows[r]).astype(BF16)


def sweep(u, p, q, a):
    d = p - u
    e = (q - p) - d
    return u + a * (d + (0.5 * a - 0.5) * e)


def lon_sweep(u, a, shift, size):
    def back(x):
        return pltpu.roll(x, shift % size, 1)

    d = back(u) - u
    e = back(d) - d
    return u + a * (d + (0.5 * a - 0.5) * e)


def half_steps(plan, group, ids, courant, depth, mask, depth8, ocean8, load, store):
    size = plan.columns
    for r, row in enumerate(in_order(ids, depth[...], group)):
        depth8[r] = jnp.broadcast_to(row, (8, size))
    for r, row in enumerate(in_order(ids, mask[...].astype(F32), group)):
        ocean8[r] = jnp.broadcast_to(row, (8, size))

    def block(start, rows, side):
        u0, u1, h0, h1 = load(start, rows)
        c_lat = courant[group, 0, pl.ds(start, rows)]
        c_lon = courant[group, 1, pl.ds(start, rows)]
        news = ([], [])
        for s in range(0, rows, 8):
            part = slice(s, s + 8)
            lat, lon = spread(c_lat[part], size), spread(c_lon[part], size)
            stencil = ((u0[part], h0[part], h1[part]), (u1[part], u0[part], h0[part]))
            for r in range(2):
                dep = depth8[r]
                u = sweep(*stencil[r], lat * dep)
                a = lon * dep
                if side == 0:
                    at = lax.broadcasted_iota(jnp.int32, (8, size), 0) + (start + s)
                    u = jnp.where(at < plan.half, lon_sweep(u, a, 1, size), lon_sweep(u, a, -1, size))
                else:
                    u = lon_sweep(u, a, side, size)
                news[r].append(u * ocean8[r])
        store(start, rows, jnp.concatenate(news[0], axis=0), jnp.concatenate(news[1], axis=0))

    east = plan.half // 16
    west = -(-plan.half // 16)
    full = plan.rows // 16

    @pl.loop(0, east, unroll=2)
    def _(i):
        block(pl.multiple_of(i * 16, 16), 16, 1)

    for i in range(east, west):
        block(i * 16, 16, 0)

    @pl.loop(west, full, unroll=2)
    def _(i):
        block(pl.multiple_of(i * 16, 16), 16, -1)

    if plan.rows % 16:
        block(full * 16, plan.rows % 16, -1)


def within(ids, group, rows):
    return rows if group == 0 else [jnp.where(ids[2] == 1, row, 0.0) for row in rows]


def first_body(plan, group, ids, courant, depth, mask, field, halo, *rest):
    half, spectra, (depth8, ocean8) = rest[:2], rest[2:-2], rest[-2:]

    def load(start, rows):
        at = pl.ds(start, rows)
        values = [ref[r, at].astype(F32) for ref, r in ((field, 0), (field, 1), (halo, 1), (halo, 0))]
        return values[:2] + within(ids, group, values[2:])

    def store(start, rows, new0, new1):
        at = pl.ds(start, rows)
        for r, new in enumerate((new0, new1)):
            half[r][at] = new
            if len(spectra) == 1:
                spectra[0][r, at] = new.astype(BF16)
            else:
                spectra[r][at] = new.astype(BF16)

    half_steps(plan, group, ids, courant, depth, mask, depth8, ocean8, load, store)


def last_body(plan, group, ids, courant, depth, mask, u0, u1, h0, h1, *rest):
    *rest, done, depth8, ocean8 = rest
    width, pitch = 2 * plan.local, plan.pitch

    def load(start, rows):
        at = pl.ds(start, rows)
        values = [ref[at].astype(F32) for ref in (u0, u1, h0, h1)]
        return values[:2] + within(ids, group, values[2:])

    def store(start, rows, new0, new1):
        for r, new in enumerate((new0, new1)):
            at = r * pitch + start
            if rows < 16:
                new = jnp.concatenate([new, jnp.zeros((16 - rows, plan.columns), F32)], axis=0)
            done[pl.ds(pl.multiple_of(at, 16), 16)] = new.astype(BF16)

    half_steps(plan, group, ids, courant, depth, mask, depth8, ocean8, load, store)
    if group == 0:
        partial, restore = rest
        tables = []
        for g in range(2):
            lane = lax.broadcasted_iota(jnp.int32, (8, 2 * pitch), 1)
            r = jnp.where(lane >= pitch, 1, 0)
            south = southward(ids, g)
            target = 2 * plan.slot_comp(lane - pitch * r, south) + actual_row(r, south)
            target = jnp.concatenate([target] * (width // 8), axis=0)
            tables.append(one_hot(target == lax.broadcasted_iota(jnp.int32, (width, 2 * pitch), 0)))
        restore[...] = tables[1]
        partial[...] = jnp.dot(tables[0], done[...], preferred_element_type=F32)
    else:
        partial, restore, out = rest
        flat = partial[...] + jnp.dot(restore[...], done[...], preferred_element_type=F32)
        out[...] = flat.astype(BF16).reshape(plan.local, 2, plan.columns)


def weights_body(plan, ids, first, second, transfer, growth, first_out, second_out, transfer_out, growth_out, columns):
    total, local, pitch = plan.total, plan.local, plan.pitch
    comp_index = ids[1] // 2
    chosen = []
    for group in range(2):
        south = southward(ids, group)
        lane = lax.broadcasted_iota(jnp.int32, (8, 2 * pitch), 1)
        other = jnp.where(lane >= pitch, 1, 0)
        owner = jnp.where(other == 0, comp_index, 1 - comp_index)
        source = plan.slot_comp(lane - pitch * other, south) + local * owner
        source = jnp.concatenate([source] * (total // 8), axis=0)
        hot = one_hot(source == lax.broadcasted_iota(jnp.int32, (total, 2 * pitch), 0))
        columns[:, 2 * group * pitch : 2 * (group + 1) * pitch] = hot
        comp = plan.slot_comp(lax.broadcasted_iota(jnp.int32, (pitch, 128), 0), south) + local * comp_index
        chosen.append(spread(comp, total) == lax.broadcasted_iota(jnp.int32, (pitch, total), 1))
    first_out[:total] = jnp.dot(first[...], columns[...], preferred_element_type=F32).astype(BF16)
    extra = plan.out_rows - total
    first_out[total:] = one_hot(lax.broadcasted_iota(jnp.int32, (extra, 4 * pitch), 0) == 0)
    second_out[...] = jnp.dot(second[...], columns[...], preferred_element_type=F32).astype(BF16)
    for group in range(2):
        at = slice(group * pitch, (group + 1) * pitch)
        pick = jnp.where(chosen[group], 1.0, 0.0)
        transfer_out[at] = jnp.dot(pick.astype(BF16), transfer[...], preferred_element_type=F32).astype(BF16)
        rate = jnp.sum(pick * growth[...], axis=1, keepdims=True)
        growth_out[at] = jnp.broadcast_to(rate, (pitch, 128))


TILE = 256


def fill_cells(plan, cells, blocks):
    rows, pitch = plan.rows, plan.pitch
    for i, block in enumerate(blocks):
        whole_rows = rows // 16 * 16
        cells[i * pitch : i * pitch + whole_rows] = block[:whole_rows]
        if whole_rows < pitch:
            tail = block[whole_rows:].astype(F32)
            tail = jnp.concatenate([tail, jnp.zeros((pitch - rows, plan.columns), F32)], axis=0)
            cells[i * pitch + whole_rows : (i + 1) * pitch] = tail.astype(BF16)


def early_body(plan, ids, first, second, own0, peer0, own1_0, own1_1, *rest):
    outs, cells = rest[:4], rest[4]
    own1 = (own1_0, own1_1)
    known = 3 * plan.pitch
    for turn in range(2):
        fill_cells(plan, cells, (own0[turn], peer0[turn], own1[1 - turn][...]))
        for c in range(0, plan.columns, TILE):
            at = slice(c, c + TILE)
            outs[2 * turn][:, at] = jnp.dot(first[:, :known], cells[:, at], preferred_element_type=F32)
            outs[2 * turn + 1][:, at] = jnp.dot(second[:, :known], cells[:, at], preferred_element_type=F32)


def source_body(plan, turn, ids, first, second, transfer, growth, mask, *rest):
    (early_first, early_second, own0, own1, peer1, half0, half1, full0, sent0, full1, sent1, cells) = rest
    total, rows, pitch = plan.total, plan.rows, plan.pitch
    known = 3 * pitch
    fill_cells(plan, cells, (peer1[...],))
    ocean = in_order(ids, mask[...].astype(F32), 0)[turn]
    for c in range(0, plan.columns, TILE):
        at = slice(c, c + TILE)
        piece = cells[:, at]
        forward = early_first[:, at] + jnp.dot(first[:, known:], piece, preferred_element_type=F32)
        backward = early_second[:, at] + jnp.dot(second[:, known:], piece, preferred_element_type=F32)
        product = (forward[:total] * backward).astype(BF16)
        nonlinear = jnp.dot(transfer[...], product, preferred_element_type=F32)
        level = forward[total : total + 1] / total
        damping = level * level / (1.0 + level * level)
        for group, (own, half, full, sent) in enumerate(((own0, half0, full0, sent0), (own1, half1, full1, sent1))):
            begin = group * pitch
            rate = spread(growth[begin : begin + rows], TILE)
            spectra = (own[turn, :, at] if group == 0 else own[:, at]).astype(F32)
            source = SOURCE_STEP * (nonlinear[begin : begin + rows] + (rate - damping) * spectra)
            updated = ocean[:, at] * (half[:, at] + source.astype(BF16).astype(F32))
            full[:, at] = updated
            sent[:, at] = updated.astype(BF16)


def paired_shards(energy, depth_speed, ocean_mask, interp_first, interp_second, transfer_matrix, growth):
    plan = Plan(energy.shape[0], energy.shape[2])
    size, rows, pitch, total = plan.columns, plan.rows, plan.pitch, plan.total
    bands = lax.axis_size("band")
    parity = lax.axis_index("band") % 2
    band = lax.axis_index("band")
    inside = jnp.logical_and(band > 0, band < bands - 1)
    ids = jnp.stack([parity, 2 * lax.axis_index("comp") + parity, inside.astype(jnp.int32)]).astype(jnp.int32)

    inner = [(i, i ^ 1) for i in range(bands)]
    outer = [(i, (i + 1 if i % 2 else i - 1) % bands) for i in range(bands)]
    peers = [(0, 1), (1, 0)]

    def shape(*dims, kind=BF16):
        return jax.ShapeDtypeStruct(dims, kind)

    rims = [pltpu.VMEM((2, 8, size), F32)] * 2

    field0, field1, courant = call(
        functools.partial(prep_body, plan),
        ids,
        (energy, ocean_mask),
        [shape(2, rows, size)] * 2 + [shape(2, 2, rows, 128, kind=F32)],
        [pltpu.VMEM((4 * pitch, 2 * plan.local), BF16)],
        cost=2,
    )
    halo0 = lax.ppermute(field1, "band", inner)
    halo1 = lax.ppermute(field0, "band", outer)

    def first_step(group, field, halo, spectra):
        operands = (courant, depth_speed, ocean_mask, field, halo)
        outs = [shape(rows, size, kind=F32)] * 2 + spectra
        return call(functools.partial(first_body, plan, group), ids, operands, outs, rims, limit=20, cost=2)

    *half0, own0 = first_step(0, field0, halo0, [shape(2, rows, size)])
    peer0 = lax.ppermute(own0, "comp", peers)
    first, second, transfer, rate = call(
        functools.partial(weights_body, plan),
        ids,
        (interp_first, interp_second, transfer_matrix, growth.reshape(1, total)),
        [shape(plan.out_rows, 4 * pitch), shape(total, 4 * pitch), shape(2 * pitch, total), shape(2 * pitch, 128, kind=F32)],
        [pltpu.VMEM((total, 4 * pitch), BF16)],
        cost=3,
    )
    *half1, own1_0, own1_1 = first_step(1, field1, halo1, [shape(rows, size)] * 2)
    own1 = (own1_0, own1_1)
    peer1 = [None, None]
    peer1[1] = lax.ppermute(own1[1], "comp", peers)
    peer1[0] = lax.ppermute(own1[0], "comp", peers)
    early = call(
        functools.partial(early_body, plan),
        ids,
        (first, second, own0, peer0, own1_0, own1_1),
        [shape(plan.out_rows, size, kind=F32), shape(total, size, kind=F32)] * 2,
        [pltpu.VMEM((3 * pitch, size), BF16)],
        limit=30,
        cost=4,
    )

    full0, sent0, full1, sent1 = [None] * 2, [None] * 2, [None] * 2, [None] * 2
    for turn in range(2):
        full0[turn], sent0[turn], full1[1 - turn], sent1[1 - turn] = call(
            functools.partial(source_body, plan, turn),
            ids,
            (first, second, transfer, rate, ocean_mask, early[2 * turn], early[2 * turn + 1])
            + (own0, own1[1 - turn], peer1[1 - turn], half0[turn], half1[1 - turn]),
            [shape(rows, size, kind=F32), shape(rows, size)] * 2,
            [pltpu.VMEM((pitch, size), BF16)],
            limit=30,
            cost=4,
        )
    rim1 = [lax.ppermute(x, "band", outer) for x in sent0]
    rim0 = [lax.ppermute(x, "band", inner) for x in sent1]

    def last_step(group, full, rim, more, outs, cost):
        operands = (courant, depth_speed, ocean_mask, full[0], full[1], rim[1], rim[0]) + more
        scratch = [pltpu.VMEM((2 * pitch, size), BF16)] + rims
        return call(functools.partial(last_body, plan, group), ids, operands, outs, scratch, limit=30, cost=cost)

    width = 2 * plan.local
    full0[0], rim1[0] = lax.optimization_barrier((full0[0], rim1[0]))
    more = last_step(0, full0, rim0, (), [shape(width, size, kind=F32), shape(width, 2 * pitch)], 3)
    (out,) = last_step(1, full1, rim1, tuple(more), [shape(*energy.shape)], 4)
    return out


def solution(mesh):
    def shards(energy, *others):
        paired = lax.axis_size("comp") == 2 and lax.axis_size("band") % 2 == 0
        if paired and energy.shape[0] % ND == 0 and energy.shape[1] == 2 and energy.shape[2] % TILE == 0:
            return paired_shards(energy, *others)
        return general_shards(energy, *others)

    in_specs = (P("comp", "band", None), P("band", None), P("band", None), P(), P(), P(), P())
    out_specs = P("comp", "band", None)
    return jax.shard_map(shards, mesh=mesh, in_specs=in_specs, out_specs=out_specs, check_vma=False)
```

```python
import functools
import math

import jax
import jax.numpy as jnp
from jax import lax
from jax.experimental import pallas as pl
from jax.experimental.pallas import tpu as pltpu
from jax.sharding import PartitionSpec as P

ND = 24


SOURCE_STEP = 0.5
COURANT_TOP = 0.9
FREQ_RATIO = 1.1

F32 = jnp.float32
BF16 = jnp.bfloat16


def with_halo(value, sides, width):
    for axis, dim in sides:
        peers, length = (lax.axis_size(axis), value.shape[dim])
        up = [(i, (i + 1) % peers) for i in range(peers - 1)]
        down = [(j, i) for i, j in up]
        last = lax.slice_in_dim(value, length - width, length, axis=dim)
        first = lax.slice_in_dim(value, 0, width, axis=dim)
        before = lax.ppermute(last, axis, up)
        after = lax.ppermute(first, axis, down)
        value = jnp.concatenate([before, value, after], axis=dim)
    return value


def courant_numbers(first_comp, local_comps):
    components = first_comp + jnp.arange(local_comps, dtype=jnp.int32)
    frequency = (components // ND).astype(jnp.float32)
    direction = (components % ND).astype(jnp.float32)
    heading = 2.0 * jnp.pi * (direction + 0.5) / ND
    factor = COURANT_TOP * jnp.power(jnp.float32(FREQ_RATIO), -frequency)
    return (factor * jnp.cos(heading), factor * jnp.sin(heading))


def upwind(middle, lower_one, lower_two, upper_one, upper_two, courant):
    magnitude = jnp.abs(courant)
    first_up = jnp.where(courant > 0, lower_one, upper_one)
    second_up = jnp.where(courant > 0, lower_two, upper_two)
    return (
        middle
        - 0.5 * magnitude * (3.0 * middle - 4.0 * first_up + second_up)
        + 0.5 * magnitude * magnitude * (middle - 2.0 * first_up + second_up)
    )


def half_step(extended, lat_courant, lon_courant, depth_speed, ocean):
    widened = extended.astype(jnp.float32)
    swept = upwind(
        widened[:, 2:-2],
        widened[:, 1:-3],
        widened[:, :-4],
        widened[:, 3:-1],
        widened[:, 4:],
        lat_courant[:, None, None] * depth_speed[None],
    )
    lon_values = lon_courant[:, None, None] * depth_speed[None]
    swept = upwind(
        swept,
        jnp.roll(swept, 1, axis=2),
        jnp.roll(swept, 2, axis=2),
        jnp.roll(swept, -1, axis=2),
        jnp.roll(swept, -2, axis=2),
        lon_values,
    )
    return ocean[None] * swept


def source_terms(cell_spectra, interp_first, interp_second, transfer_matrix, growth):
    forward_interp = jnp.dot(interp_first, cell_spectra, preferred_element_type=jnp.float32)
    backward_interp = jnp.dot(interp_second, cell_spectra, preferred_element_type=jnp.float32)
    product = (forward_interp * backward_interp).astype(jnp.bfloat16)
    nonlinear = jnp.dot(transfer_matrix, product, preferred_element_type=jnp.float32)
    spectra32 = cell_spectra.astype(jnp.float32)
    mean_level = jnp.mean(spectra32, axis=0)
    damping = mean_level * mean_level / (1.0 + mean_level * mean_level)
    total = SOURCE_STEP * (nonlinear + (growth[:, None] - damping[None]) * spectra32)
    return total.astype(jnp.bfloat16)


def general_shards(energy, depth_speed, ocean_mask, interp_first, interp_second, transfer_matrix, growth):
    local_comps = energy.shape[0]
    lat_courant, lon_courant = courant_numbers(lax.axis_index("comp") * local_comps, local_comps)
    ocean = ocean_mask.astype(jnp.float32)
    start = (ocean[None] * energy.astype(jnp.float32)).astype(jnp.bfloat16)
    rimmed = with_halo(start, (("band", 1),), 2)
    half_one = half_step(rimmed, lat_courant, lon_courant, depth_speed, ocean)
    spectra = half_one.astype(jnp.bfloat16)
    block_in = lax.all_to_all(spectra, "comp", split_axis=2, concat_axis=0, tiled=True)
    total_comps = block_in.shape[0]
    flat_cells = block_in.reshape(total_comps, -1)
    result = source_terms(flat_cells, interp_first, interp_second, transfer_matrix, growth)
    source = lax.all_to_all(
        result.reshape(block_in.shape), "comp", split_axis=0, concat_axis=2, tiled=True
    ).astype(jnp.float32)
    updated = ocean[None] * (half_one + source)
    rimmed_mid = with_halo(updated, (("band", 1),), 2)
    final_field = half_step(rimmed_mid, lat_courant, lon_courant, depth_speed, ocean)
    return final_field.astype(jnp.bfloat16)


class Plan:
    def __init__(self, local_comps, columns):
        self.local = local_comps
        self.total = 2 * local_comps
        self.columns = columns
        self.half = local_comps // 4
        self.slots = 2 * self.half
        self.rows = -(-self.slots // 8) * 8
        self.pitch = -(-self.slots // 16) * 16
        self.out_rows = -(-(self.total + 1) // 16) * 16
        self.side = columns // 2
        self.cap = 3 * columns // 4

    def pieces(self):
        ends = [0, self.cap, (self.cap + 2 * self.columns) // 2, 2 * self.columns]
        return list(zip(ends[:-1], ends[1:]))

    def slot_parts(self, slot):
        east = slot < self.half
        j = jnp.where(east, slot, slot - self.half)
        f = (j * 10923) >> 16
        return east, f, j - 6 * f

    def courant(self, ids, group):
        east, f, turn = self.slot_parts(lax.broadcasted_iota(jnp.int32, (self.rows, 128), 0))
        factor = jnp.where(ids[1] >= 2, COURANT_TOP * FREQ_RATIO ** -(self.local // ND), COURANT_TOP).astype(F32)
        for bit in range(self.local.bit_length()):
            if 1 << bit < self.local // ND:
                factor = factor * jnp.where((f >> bit) & 1 == 1, FREQ_RATIO ** -(1 << bit), 1.0)
        falling = east == jnp.logical_not(southward(ids, group))
        place = jnp.where(falling, turn, 5 - turn)
        cosine, sine = factor, factor
        for i in range(6):
            cosine = jnp.where(place == i, factor * math.cos(2 * math.pi * (i + 0.5) / ND), cosine)
            sine = jnp.where(place == i, factor * math.sin(2 * math.pi * (i + 0.5) / ND), sine)
        return cosine, sine

    def slot_comp(self, slot, south):
        east, f, turn = self.slot_parts(slot)
        comp = ND * f + turn + jnp.where(east, jnp.where(south, 6, 0), jnp.where(south, 12, 18))
        return jnp.where(slot < self.slots, comp, -4 * self.total)


def southward(ids, group):
    return ids[0] == group


def actual_row(r, south):
    return jnp.where(south, 1 - r, r)


def one_hot(match):
    return jnp.where(match, 1.0, 0.0).astype(BF16)


def spread(value, width):
    parts = [value] * (width // 128)
    if width % 128:
        parts.append(value[:, : width % 128])
    return jnp.concatenate(parts, axis=1)


VMEM = pl.BlockSpec(memory_space=pltpu.VMEM)
SMEM = pl.BlockSpec(memory_space=pltpu.SMEM)


def call(body, ids, operands, outs, scratch=(), limit=40, cost=1.0):
    return pl.pallas_call(
        body,
        in_specs=[SMEM] + [VMEM] * len(operands),
        out_specs=[VMEM] * len(outs),
        scratch_shapes=list(scratch),
        out_shape=outs,
        compiler_params=pltpu.CompilerParams(vmem_limit_bytes=int(limit * 2**20)),
        cost_estimate=pl.CostEstimate(flops=int(cost * 1.1e9), bytes_accessed=0, transcendentals=0),
    )(ids, *operands)


def in_order(ids, value, group):
    south = southward(ids, group)
    one, two = value[0:1], value[1:2]
    return jnp.where(south, two, one), jnp.where(south, one, two)


def prep_body(plan, ids, energy, mask, field0, field1, courant, regroup):
    for group in range(2):
        courant[group, 0], courant[group, 1] = plan.courant(ids, group)
    width, pitch = 2 * plan.local, plan.pitch
    column = lax.broadcasted_iota(jnp.int32, (pitch, width), 1)
    for group in range(2):
        south = southward(ids, group)
        comp = plan.slot_comp(lax.broadcasted_iota(jnp.int32, (pitch, 128), 0), south)
        for r in range(2):
            begin = (2 * group + r) * pitch
            regroup[begin : begin + pitch] = one_hot(spread(2 * comp + actual_row(r, south), width) == column)
    ocean = mask[...].astype(F32)
    flat = energy[...].reshape(width, plan.columns)
    moved = jnp.dot(regroup[...], flat, preferred_element_type=F32)
    for group, field in enumerate((field0, field1)):
        rows = in_order(ids, ocean, group)
        for r in range(2):
            at = (2 * group + r) * pitch
            start = moved[at : at + plan.rows] * rows[r]
            if group == 0:
                place = lax.broadcasted_iota(jnp.int32, (8, plan.columns), 0) + (plan.rows - 8)
                tail = jnp.where(place == plan.slots, rows[r], start[-8:])
                start = jnp.concatenate([start[:-8], tail], axis=0)
            field[r] = start.astype(BF16)


def sweep(u, p, q, a):
    d = p - u
    e = (q - p) - d
    return u + a * (d + (0.5 * a - 0.5) * e)


def lon_sweep(u, a, shift, size):
    def back(x):
        return pltpu.roll(x, shift % size, 1)

    d = back(u) - u
    e = back(d) - d
    return u + a * (d + (0.5 * a - 0.5) * e)


def half_steps(plan, group, ids, courant, depth, mask, depth8, ocean8, load, store):
    size = plan.columns
    for r, row in enumerate(in_order(ids, depth[...], group)):
        depth8[r] = jnp.broadcast_to(row, (8, size))
    for r, row in enumerate(in_order(ids, mask[...].astype(F32), group)):
        ocean8[r] = jnp.broadcast_to(row, (8, size))

    def block(start, rows, side):
        u0, u1, h0, h1 = load(start, rows)
        c_lat = courant[group, 0, pl.ds(start, rows)]
        c_lon = courant[group, 1, pl.ds(start, rows)]
        news = ([], [])
        for s in range(0, rows, 8):
            part = slice(s, s + 8)
            lat, lon = spread(c_lat[part], size), spread(c_lon[part], size)
            stencil = ((u0[part], h0[part], h1[part]), (u1[part], u0[part], h0[part]))
            for r in range(2):
                dep = depth8[r]
                u = sweep(*stencil[r], lat * dep)
                a = lon * dep
                if side == 0:
                    at = lax.broadcasted_iota(jnp.int32, (8, size), 0) + (start + s)
                    u = jnp.where(at < plan.half, lon_sweep(u, a, 1, size), lon_sweep(u, a, -1, size))
                else:
                    u = lon_sweep(u, a, side, size)
                news[r].append(u * ocean8[r])
        store(start, rows, jnp.concatenate(news[0], axis=0), jnp.concatenate(news[1], axis=0))

    east = plan.half // 16
    west = -(-plan.half // 16)
    full = plan.rows // 16

    @pl.loop(0, east, unroll=2)
    def _(i):
        block(pl.multiple_of(i * 16, 16), 16, 1)

    for i in range(east, west):
        block(i * 16, 16, 0)

    @pl.loop(west, full, unroll=2)
    def _(i):
        block(pl.multiple_of(i * 16, 16), 16, -1)

    if plan.rows % 16:
        block(full * 16, plan.rows % 16, -1)


def within(ids, group, rows):
    return rows if group == 0 else [jnp.where(ids[2] == 1, row, 0.0) for row in rows]


def place_body(plan, neighbour, ids, mask, *placed):
    side = plan.side
    if neighbour:
        tail = slice(plan.slots // 8 * 8, plan.rows)
        at = plan.slots % 8
        rows = [mask[r, tail].astype(F32)[at : at + 1] for r in range(2)]
    else:
        rows = in_order(ids, mask[...].astype(F32), 0)
    parts = [row[:, b * side : (b + 1) * side] for b in range(2) for row in rows]
    stacked = jnp.concatenate(parts + [jnp.zeros((12, side), F32)], axis=0).astype(BF16)
    at = [lax.broadcasted_iota(jnp.int32, (side, side), axis) for axis in range(2)]
    ahead = jnp.dot(stacked, one_hot(at[0] < at[1]), preferred_element_type=F32)
    target = lax.broadcasted_iota(jnp.int32, (plan.cap, side), 0)
    for b in range(2):
        begin = jnp.zeros((1, 1), F32)
        for r in range(2):
            part = parts[2 * b + r]
            place = jnp.where(part > 0, ahead[2 * b + r : 2 * b + r + 1] + begin, -1.0).astype(jnp.int32)
            placed[b][:, r * side : (r + 1) * side] = one_hot(target == place)
            begin = begin + jnp.sum(part, axis=1, keepdims=True)


def gather_cells(cells, placed):
    dims = (((1,), (1,)), ((), ()))
    return lax.dot_general(cells, placed, dims, preferred_element_type=F32).astype(BF16)


def first_body(plan, group, ids, courant, depth, mask, field, halo, placed0, placed1, *rest):
    half, spectra, (depth8, ocean8, cells) = rest[:2], rest[2:-3], rest[-3:]
    side = plan.side

    def load(start, rows):
        at = pl.ds(start, rows)
        values = [ref[r, at].astype(F32) for ref, r in ((field, 0), (field, 1), (halo, 1), (halo, 0))]
        return values[:2] + within(ids, group, values[2:])

    def store(start, rows, new0, new1):
        at = pl.ds(start, rows)
        for r, new in enumerate((new0, new1)):
            half[r][at] = new
            begin = (r if group == 0 else 1 - r) * side
            for b in range(2):
                cells[b, at, begin : begin + side] = new[:, b * side : (b + 1) * side].astype(BF16)

    half_steps(plan, group, ids, courant, depth, mask, depth8, ocean8, load, store)
    for b, placed in enumerate((placed0, placed1)):
        gathered = gather_cells(cells[b], placed[...])
        if group == 0:
            spectra[0][:, b * plan.cap : (b + 1) * plan.cap] = gathered
        else:
            spectra[b][...] = gathered


def last_body(plan, group, ids, courant, depth, mask, full0, full1, *rest):
    *rest, done, depth8, ocean8 = rest
    width, pitch, rows, side = 2 * plan.local, plan.pitch, plan.rows, plan.side

    def scatter(cells, placed):
        return jnp.dot(cells[...], placed[...], preferred_element_type=F32)[:rows].astype(BF16)

    def both(a, b, at):
        return jnp.concatenate([a[at], b[at]], axis=1).astype(F32)

    def load(start, count):
        at = pl.ds(start, count)
        values = [both(full0.at[r], full1.at[r], at) for r in range(2)]
        if group == 0:
            rows_in = jnp.concatenate([piece[at] for piece in pieces], axis=1).astype(F32)
            return values + [rows_in[:, plan.columns :], rows_in[:, : plan.columns]]
        slots = [slice(slot * side, (slot + 1) * side) for slot in (1, 0)]
        return values + within(ids, group, [both(rim0.at[:, slot], rim1.at[:, slot], at) for slot in slots])

    def store(start, count, new0, new1):
        for r, new in enumerate((new0, new1)):
            at = r * pitch + start
            if count < 16:
                new = jnp.concatenate([new, jnp.zeros((16 - count, plan.columns), F32)], axis=0)
            done[pl.ds(pl.multiple_of(at, 16), 16)] = new.astype(BF16)

    if group == 0:
        *pieces, partial, restore = rest
    else:
        cells0, cells1, placed0, placed1, partial, restore, out, rim0, rim1 = rest
        rim0[...] = scatter(cells0, placed0)
        rim1[...] = scatter(cells1, placed1)
    half_steps(plan, group, ids, courant, depth, mask, depth8, ocean8, load, store)
    if group == 0:
        tables = []
        for g in range(2):
            lane = lax.broadcasted_iota(jnp.int32, (8, 2 * pitch), 1)
            r = jnp.where(lane >= pitch, 1, 0)
            south = southward(ids, g)
            target = 2 * plan.slot_comp(lane - pitch * r, south) + actual_row(r, south)
            target = jnp.concatenate([target] * (width // 8), axis=0)
            tables.append(one_hot(target == lax.broadcasted_iota(jnp.int32, (width, 2 * pitch), 0)))
        restore[...] = tables[1]
        partial[...] = jnp.dot(tables[0], done[...], preferred_element_type=F32)
    else:
        flat = partial[...] + jnp.dot(restore[...], done[...], preferred_element_type=F32)
        out[...] = flat.astype(BF16).reshape(plan.local, 2, plan.columns)


def weights_body(plan, ids, first, second, transfer, growth, first_out, second_out, transfer_out, growth_out, columns):
    total, local, pitch = plan.total, plan.local, plan.pitch
    comp_index = ids[1] // 2
    chosen = []
    for group in range(2):
        south = southward(ids, group)
        lane = lax.broadcasted_iota(jnp.int32, (8, 2 * pitch), 1)
        other = jnp.where(lane >= pitch, 1, 0)
        owner = jnp.where(other == 0, comp_index, 1 - comp_index)
        source = plan.slot_comp(lane - pitch * other, south) + local * owner
        source = jnp.concatenate([source] * (total // 8), axis=0)
        hot = one_hot(source == lax.broadcasted_iota(jnp.int32, (total, 2 * pitch), 0))
        columns[:, 2 * group * pitch : 2 * (group + 1) * pitch] = hot
        comp = plan.slot_comp(lax.broadcasted_iota(jnp.int32, (pitch, 128), 0), south) + local * comp_index
        chosen.append(spread(comp, total) == lax.broadcasted_iota(jnp.int32, (pitch, total), 1))
    first_out[:total] = jnp.dot(first[...], columns[...], preferred_element_type=F32).astype(BF16)
    extra = plan.out_rows - total
    first_out[total:] = one_hot(lax.broadcasted_iota(jnp.int32, (extra, 4 * pitch), 0) == 0)
    second_out[...] = jnp.dot(second[...], columns[...], preferred_element_type=F32).astype(BF16)
    for group in range(2):
        at = slice(group * pitch, (group + 1) * pitch)
        pick = jnp.where(chosen[group], 1.0, 0.0)
        transfer_out[at] = jnp.dot(pick.astype(BF16), transfer[...], preferred_element_type=F32).astype(BF16)
        rate = jnp.sum(pick * growth[...], axis=1, keepdims=True)
        growth_out[at] = jnp.broadcast_to(rate, (pitch, 128))


TILE = 256


def fill_cells(plan, cells, blocks):
    rows, pitch = plan.rows, plan.pitch
    for i, block in enumerate(blocks):
        whole_rows = rows // 16 * 16
        cells[i * pitch : i * pitch + whole_rows] = block[:whole_rows]
        if whole_rows < pitch:
            tail = block[whole_rows:].astype(F32)
            tail = jnp.concatenate([tail, jnp.zeros((pitch - rows, tail.shape[1]), F32)], axis=0)
            cells[i * pitch + whole_rows : (i + 1) * pitch] = tail.astype(BF16)


def early_body(plan, ids, first, second, own0, peer0, own1_0, own1_1, *rest):
    outs, cells = rest[:4], rest[4]
    known = 3 * plan.pitch
    for b, own1 in enumerate((own1_0, own1_1)):
        block = slice(b * plan.cap, (b + 1) * plan.cap)
        fill_cells(plan, cells, (own0[:, block], peer0[:, block], own1[...]))
        for c in range(0, plan.cap, TILE):
            at = slice(c, c + TILE)
            outs[2 * b][:, at] = jnp.dot(first[:, :known], cells[:, at], preferred_element_type=F32)
            outs[2 * b + 1][:, at] = jnp.dot(second[:, :known], cells[:, at], preferred_element_type=F32)


def source_body(plan, b, ids, first, second, transfer, growth, placed, *rest):
    (early_first, early_second, own0, own1, peer1, half00, half01, half10, half11) = rest[:9]
    *outs, cells, sources, leaving = rest[9:]
    full0, sent0, full1 = outs[-6:-3] if b else outs
    total, rows, pitch, cap, side = plan.total, plan.rows, plan.pitch, plan.cap, plan.side
    known = 3 * pitch
    fill_cells(plan, cells, (peer1[...],))
    for c in range(0, cap, TILE):
        at = slice(c, c + TILE)
        piece = cells[:, at]
        forward = early_first[:, at] + jnp.dot(first[:, known:], piece, preferred_element_type=F32)
        backward = early_second[:, at] + jnp.dot(second[:, known:], piece, preferred_element_type=F32)
        product = (forward[:total] * backward).astype(BF16)
        nonlinear = jnp.dot(transfer[...], product, preferred_element_type=F32)
        level = forward[total : total + 1] / total
        damping = level * level / (1.0 + level * level)
        for group in range(2):
            begin = group * pitch
            spectra = (own1[:, at] if group else own0[:, b * cap + c : b * cap + c + TILE]).astype(F32)
            spectra = jnp.concatenate([spectra, jnp.zeros((pitch - rows, TILE), F32)], axis=0)
            rate = spread(growth[begin : begin + pitch], TILE)
            source = SOURCE_STEP * (nonlinear[begin : begin + pitch] + (rate - damping) * spectra)
            sources[begin : begin + pitch, at] = source.astype(BF16)
    block = slice(b * side, (b + 1) * side)
    for slot in range(2):
        here = placed[:, slot * side : (slot + 1) * side]
        spread_out = jnp.dot(sources[...], here, preferred_element_type=F32)
        full0[slot] = (half00, half01)[slot][:, block] + spread_out[:rows]
        leaving[:, slot * side : (slot + 1) * side] = full0[slot].astype(BF16)
        full1[1 - slot] = (half10, half11)[1 - slot][:, block] + spread_out[pitch : pitch + rows]
    gathered = gather_cells(leaving[...], placed[...]).astype(F32)
    sent0[...] = jnp.concatenate([gathered, jnp.zeros((sent0.shape[0] - rows, cap), F32)], axis=0).astype(BF16)
    if b:
        parts = [full[r].astype(BF16) for r in range(2) for full in (outs[0], full1)]
        for piece, (begin, end) in zip(outs[-3:], plan.pieces()):
            ends = [(max(begin - i * side, 0), min(end - i * side, side)) for i in range(4)]
            piece[...] = jnp.concatenate([parts[i][:, x:y] for i, (x, y) in enumerate(ends) if x < y], axis=1)


def paired_shards(energy, depth_speed, ocean_mask, interp_first, interp_second, transfer_matrix, growth):
    plan = Plan(energy.shape[0], energy.shape[2])
    size, rows, pitch, total = plan.columns, plan.rows, plan.pitch, plan.total
    bands = lax.axis_size("band")
    parity = lax.axis_index("band") % 2
    band = lax.axis_index("band")
    inside = jnp.logical_and(band > 0, band < bands - 1)
    ids = jnp.stack([parity, 2 * lax.axis_index("comp") + parity, inside.astype(jnp.int32)]).astype(jnp.int32)

    inner = [(i, i ^ 1) for i in range(bands)]
    outer = [(i, (i + 1 if i % 2 else i - 1) % bands) for i in range(bands)]
    outer_beside = [(2 * i + c, 2 * j + c) for i, j in outer if 0 < i < bands - 1 for c in range(2)]
    outer_beside += [(2 * i + c, 2 * i + 1 - c) for i in (0, bands - 1) for c in range(2)]
    peers = [(0, 1), (1, 0)]

    def shape(*dims, kind=BF16):
        return jax.ShapeDtypeStruct(dims, kind)

    rims = [pltpu.VMEM((2, 8, size), F32)] * 2

    field0, field1, courant = call(
        functools.partial(prep_body, plan),
        ids,
        (energy, ocean_mask),
        [shape(2, rows, size)] * 2 + [shape(2, 2, rows, 128, kind=F32)],
        [pltpu.VMEM((4 * pitch, 2 * plan.local), BF16)],
        cost=2,
    )
    halo0 = lax.ppermute(field1, "band", inner)
    halo1 = lax.ppermute(field0, "band", outer)

    cap, side = plan.cap, plan.side
    def place(mask, neighbour, cost):
        return call(functools.partial(place_body, plan, neighbour), ids, (mask,), [shape(cap, size)] * 2, cost=cost)

    placed = place(ocean_mask, False, 2)
    outer_placed = place(halo1, True, 0.01)

    def first_step(group, field, halo, spectra):
        operands = (courant, depth_speed, ocean_mask, field, halo, *placed)
        outs = [shape(rows, size, kind=F32)] * 2 + spectra
        scratch = rims + [pltpu.VMEM((2, rows, size), BF16)]
        return call(functools.partial(first_body, plan, group), ids, operands, outs, scratch, limit=20, cost=2)

    *half0, own0 = first_step(0, field0, halo0, [shape(rows, 2 * cap)])
    peer0 = lax.ppermute(own0, "comp", peers)
    first, second, transfer, rate = call(
        functools.partial(weights_body, plan),
        ids,
        (interp_first, interp_second, transfer_matrix, growth.reshape(1, total)),
        [shape(plan.out_rows, 4 * pitch), shape(total, 4 * pitch), shape(2 * pitch, total), shape(2 * pitch, 128, kind=F32)],
        [pltpu.VMEM((total, 4 * pitch), BF16)],
        cost=3,
    )
    *half1, own1_0, own1_1 = first_step(1, field1, halo1, [shape(rows, cap)] * 2)
    own1 = (own1_0, own1_1)
    peer1 = [lax.ppermute(own, "comp", peers) for own in own1]
    early = call(
        functools.partial(early_body, plan),
        ids,
        (first, second, own0, peer0, own1_0, own1_1),
        [shape(plan.out_rows, cap, kind=F32), shape(total, cap, kind=F32)] * 2,
        [pltpu.VMEM((3 * pitch, cap), BF16)],
        limit=30,
        cost=4,
    )

    full0, sent0, full1 = [], [], []
    for b in range(2):
        own = call(
            functools.partial(source_body, plan, b),
            ids,
            (first, second, transfer, rate, placed[b], early[2 * b], early[2 * b + 1], own0, own1[b], peer1[b])
            + (*half0, *half1, *full1),
            [shape(2, rows, side, kind=F32), shape(rows + (24, 8)[b], cap), shape(2, rows, side, kind=F32)]
            + [shape(rows, end - begin) for begin, end in plan.pieces()] * b,
            [pltpu.VMEM((pitch, cap), BF16), pltpu.VMEM((2 * pitch, cap), BF16), pltpu.VMEM((rows, size), BF16)],
            limit=30,
            cost=4,
        )
        full0.append(own[0])
        sent0.append(own[1])
        full1.append(own[2])
    rim1 = [lax.ppermute(sent0[0], "band", outer), lax.ppermute(sent0[1], ("band", "comp"), outer_beside)]
    rim0 = [lax.ppermute(x, "band", inner) for x in own[3:]]

    width = 2 * plan.local
    done = pltpu.VMEM((2 * pitch, size), BF16)
    partial, restore = call(
        functools.partial(last_body, plan, 0),
        ids,
        (courant, depth_speed, ocean_mask, *full0, *rim0),
        [shape(width, size, kind=F32), shape(width, 2 * pitch)],
        [done] + rims,
        limit=30,
        cost=0.01,
    )
    (out,) = call(
        functools.partial(last_body, plan, 1),
        ids,
        (courant, depth_speed, ocean_mask, *full1, *rim1, *outer_placed, partial, restore),
        [shape(*energy.shape)],
        [pltpu.VMEM((rows, size), BF16)] * 2 + [done] + rims,
        limit=30,
        cost=4,
    )
    return out


def solution(mesh):
    def shards(energy, *others):
        paired = lax.axis_size("comp") == 2 and lax.axis_size("band") % 2 == 0
        if paired and energy.shape[0] % ND == 0 and energy.shape[1] == 2 and energy.shape[2] % (4 * TILE) == 0 and energy.shape[0] // 2 % 8:
            return paired_shards(energy, *others)
        return general_shards(energy, *others)

    in_specs = (P("comp", "band", None), P("band", None), P("band", None), P(), P(), P(), P())
    out_specs = P("comp", "band", None)
    return jax.shard_map(shards, mesh=mesh, in_specs=in_specs, out_specs=out_specs, check_vma=False)
```

```python
import functools
import math

import jax
import jax.numpy as jnp
from jax import lax
from jax.experimental import pallas as pl
from jax.experimental.pallas import tpu as pltpu
from jax.sharding import PartitionSpec as P

ND = 24


SOURCE_STEP = 0.5
COURANT_TOP = 0.9
FREQ_RATIO = 1.1

F32 = jnp.float32
BF16 = jnp.bfloat16


def with_halo(value, sides, width):
    for axis, dim in sides:
        peers, length = (lax.axis_size(axis), value.shape[dim])
        up = [(i, (i + 1) % peers) for i in range(peers - 1)]
        down = [(j, i) for i, j in up]
        last = lax.slice_in_dim(value, length - width, length, axis=dim)
        first = lax.slice_in_dim(value, 0, width, axis=dim)
        before = lax.ppermute(last, axis, up)
        after = lax.ppermute(first, axis, down)
        value = jnp.concatenate([before, value, after], axis=dim)
    return value


def courant_numbers(first_comp, local_comps):
    components = first_comp + jnp.arange(local_comps, dtype=jnp.int32)
    frequency = (components // ND).astype(jnp.float32)
    direction = (components % ND).astype(jnp.float32)
    heading = 2.0 * jnp.pi * (direction + 0.5) / ND
    factor = COURANT_TOP * jnp.power(jnp.float32(FREQ_RATIO), -frequency)
    return (factor * jnp.cos(heading), factor * jnp.sin(heading))


def upwind(middle, lower_one, lower_two, upper_one, upper_two, courant):
    magnitude = jnp.abs(courant)
    first_up = jnp.where(courant > 0, lower_one, upper_one)
    second_up = jnp.where(courant > 0, lower_two, upper_two)
    return (
        middle
        - 0.5 * magnitude * (3.0 * middle - 4.0 * first_up + second_up)
        + 0.5 * magnitude * magnitude * (middle - 2.0 * first_up + second_up)
    )


def half_step(extended, lat_courant, lon_courant, depth_speed, ocean):
    widened = extended.astype(jnp.float32)
    swept = upwind(
        widened[:, 2:-2],
        widened[:, 1:-3],
        widened[:, :-4],
        widened[:, 3:-1],
        widened[:, 4:],
        lat_courant[:, None, None] * depth_speed[None],
    )
    lon_values = lon_courant[:, None, None] * depth_speed[None]
    swept = upwind(
        swept,
        jnp.roll(swept, 1, axis=2),
        jnp.roll(swept, 2, axis=2),
        jnp.roll(swept, -1, axis=2),
        jnp.roll(swept, -2, axis=2),
        lon_values,
    )
    return ocean[None] * swept


def source_terms(cell_spectra, interp_first, interp_second, transfer_matrix, growth):
    forward_interp = jnp.dot(interp_first, cell_spectra, preferred_element_type=jnp.float32)
    backward_interp = jnp.dot(interp_second, cell_spectra, preferred_element_type=jnp.float32)
    product = (forward_interp * backward_interp).astype(jnp.bfloat16)
    nonlinear = jnp.dot(transfer_matrix, product, preferred_element_type=jnp.float32)
    spectra32 = cell_spectra.astype(jnp.float32)
    mean_level = jnp.mean(spectra32, axis=0)
    damping = mean_level * mean_level / (1.0 + mean_level * mean_level)
    total = SOURCE_STEP * (nonlinear + (growth[:, None] - damping[None]) * spectra32)
    return total.astype(jnp.bfloat16)


def general_shards(energy, depth_speed, ocean_mask, interp_first, interp_second, transfer_matrix, growth):
    local_comps = energy.shape[0]
    lat_courant, lon_courant = courant_numbers(lax.axis_index("comp") * local_comps, local_comps)
    ocean = ocean_mask.astype(jnp.float32)
    start = (ocean[None] * energy.astype(jnp.float32)).astype(jnp.bfloat16)
    rimmed = with_halo(start, (("band", 1),), 2)
    half_one = half_step(rimmed, lat_courant, lon_courant, depth_speed, ocean)
    spectra = half_one.astype(jnp.bfloat16)
    block_in = lax.all_to_all(spectra, "comp", split_axis=2, concat_axis=0, tiled=True)
    total_comps = block_in.shape[0]
    flat_cells = block_in.reshape(total_comps, -1)
    result = source_terms(flat_cells, interp_first, interp_second, transfer_matrix, growth)
    source = lax.all_to_all(
        result.reshape(block_in.shape), "comp", split_axis=0, concat_axis=2, tiled=True
    ).astype(jnp.float32)
    updated = ocean[None] * (half_one + source)
    rimmed_mid = with_halo(updated, (("band", 1),), 2)
    final_field = half_step(rimmed_mid, lat_courant, lon_courant, depth_speed, ocean)
    return final_field.astype(jnp.bfloat16)


class Plan:
    def __init__(self, local_comps, columns):
        self.local = local_comps
        self.total = 2 * local_comps
        self.columns = columns
        self.half = local_comps // 4
        self.slots = 2 * self.half
        self.rows = -(-self.slots // 8) * 8
        self.pitch = -(-self.slots // 16) * 16
        self.out_rows = -(-(self.total + 1) // 16) * 16
        self.side = columns // 2
        self.cap = 3 * columns // 4

    def pieces(self):
        ends = [0, self.cap, (self.cap + 2 * self.columns) // 2, 2 * self.columns]
        return list(zip(ends[:-1], ends[1:]))

    def slot_parts(self, slot):
        east = slot < self.half
        j = jnp.where(east, slot, slot - self.half)
        f = (j * 10923) >> 16
        return east, f, j - 6 * f

    def courant(self, ids, group):
        east, f, turn = self.slot_parts(lax.broadcasted_iota(jnp.int32, (self.rows, 128), 0))
        factor = jnp.where(ids[1] >= 2, COURANT_TOP * FREQ_RATIO ** -(self.local // ND), COURANT_TOP).astype(F32)
        for bit in range(self.local.bit_length()):
            if 1 << bit < self.local // ND:
                factor = factor * jnp.where((f >> bit) & 1 == 1, FREQ_RATIO ** -(1 << bit), 1.0)
        falling = east == jnp.logical_not(southward(ids, group))
        place = jnp.where(falling, turn, 5 - turn)
        cosine, sine = factor, factor
        for i in range(6):
            cosine = jnp.where(place == i, factor * math.cos(2 * math.pi * (i + 0.5) / ND), cosine)
            sine = jnp.where(place == i, factor * math.sin(2 * math.pi * (i + 0.5) / ND), sine)
        return cosine, sine

    def slot_comp(self, slot, south):
        east, f, turn = self.slot_parts(slot)
        comp = ND * f + turn + jnp.where(east, jnp.where(south, 6, 0), jnp.where(south, 12, 18))
        return jnp.where(slot < self.slots, comp, -4 * self.total)


def southward(ids, group):
    return ids[0] == group


def actual_row(r, south):
    return jnp.where(south, 1 - r, r)


def one_hot(match):
    return jnp.where(match, 1.0, 0.0).astype(BF16)


def spread(value, width):
    parts = [value] * (width // 128)
    if width % 128:
        parts.append(value[:, : width % 128])
    return jnp.concatenate(parts, axis=1)


VMEM = pl.BlockSpec(memory_space=pltpu.VMEM)
SMEM = pl.BlockSpec(memory_space=pltpu.SMEM)


def call(body, ids, operands, outs, scratch=(), limit=40, cost=1.0):
    return pl.pallas_call(
        body,
        in_specs=[SMEM] + [VMEM] * len(operands),
        out_specs=[VMEM] * len(outs),
        scratch_shapes=list(scratch),
        out_shape=outs,
        compiler_params=pltpu.CompilerParams(vmem_limit_bytes=int(limit * 2**20)),
        cost_estimate=pl.CostEstimate(flops=int(cost * 1.1e9), bytes_accessed=0, transcendentals=0),
    )(ids, *operands)


def in_order(ids, value, group):
    south = southward(ids, group)
    one, two = value[0:1], value[1:2]
    return jnp.where(south, two, one), jnp.where(south, one, two)


def prep_body(plan, ids, energy, mask, field0, field1, courant, regroup):
    for group in range(2):
        courant[group, 0], courant[group, 1] = plan.courant(ids, group)
    width, pitch = 2 * plan.local, plan.pitch
    column = lax.broadcasted_iota(jnp.int32, (pitch, width), 1)
    for group in range(2):
        south = southward(ids, group)
        comp = plan.slot_comp(lax.broadcasted_iota(jnp.int32, (pitch, 128), 0), south)
        for r in range(2):
            begin = (2 * group + r) * pitch
            regroup[begin : begin + pitch] = one_hot(spread(2 * comp + actual_row(r, south), width) == column)
    ocean = mask[...].astype(F32)
    flat = energy[...].reshape(width, plan.columns)
    moved = jnp.dot(regroup[...], flat, preferred_element_type=F32)
    for group, field in enumerate((field0, field1)):
        rows = in_order(ids, ocean, group)
        for r in range(2):
            at = (2 * group + r) * pitch
            start = moved[at : at + plan.rows] * rows[r]
            if group == 0:
                place = lax.broadcasted_iota(jnp.int32, (8, plan.columns), 0) + (plan.rows - 8)
                tail = jnp.where(place == plan.slots, rows[r], start[-8:])
                start = jnp.concatenate([start[:-8], tail], axis=0)
            field[r] = start.astype(BF16)


def sweep(u, p, q, a):
    d = p - u
    e = (q - p) - d
    return u + a * (d + (0.5 * a - 0.5) * e)


def lon_sweep(u, a, shift, size):
    def back(x):
        return pltpu.roll(x, shift % size, 1)

    d = back(u) - u
    e = back(d) - d
    return u + a * (d + (0.5 * a - 0.5) * e)


def half_steps(plan, group, ids, courant, depth, mask, depth8, ocean8, load, store):
    size = plan.columns
    for r, row in enumerate(in_order(ids, depth[...], group)):
        depth8[r] = jnp.broadcast_to(row, (8, size))
    for r, row in enumerate(in_order(ids, mask[...].astype(F32), group)):
        ocean8[r] = jnp.broadcast_to(row, (8, size))

    def block(start, rows, side):
        u0, u1, h0, h1 = load(start, rows)
        c_lat = courant[group, 0, pl.ds(start, rows)]
        c_lon = courant[group, 1, pl.ds(start, rows)]
        news = ([], [])
        for s in range(0, rows, 8):
            part = slice(s, s + 8)
            lat, lon = spread(c_lat[part], size), spread(c_lon[part], size)
            stencil = ((u0[part], h0[part], h1[part]), (u1[part], u0[part], h0[part]))
            for r in range(2):
                dep = depth8[r]
                u = sweep(*stencil[r], lat * dep)
                a = lon * dep
                if side == 0:
                    at = lax.broadcasted_iota(jnp.int32, (8, size), 0) + (start + s)
                    u = jnp.where(at < plan.half, lon_sweep(u, a, 1, size), lon_sweep(u, a, -1, size))
                else:
                    u = lon_sweep(u, a, side, size)
                news[r].append(u * ocean8[r])
        store(start, rows, jnp.concatenate(news[0], axis=0), jnp.concatenate(news[1], axis=0))

    east = plan.half // 16
    west = -(-plan.half // 16)
    full = plan.rows // 16

    @pl.loop(0, east, unroll=2)
    def _(i):
        block(pl.multiple_of(i * 16, 16), 16, 1)

    for i in range(east, west):
        block(i * 16, 16, 0)

    @pl.loop(west, full, unroll=2)
    def _(i):
        block(pl.multiple_of(i * 16, 16), 16, -1)

    if plan.rows % 16:
        block(full * 16, plan.rows % 16, -1)


def within(ids, group, rows):
    return rows if group == 0 else [jnp.where(ids[2] == 1, row, 0.0) for row in rows]


def place_body(plan, neighbour, ids, mask, *placed):
    side = plan.side
    if neighbour:
        tail = slice(plan.slots // 8 * 8, plan.rows)
        at = plan.slots % 8
        rows = [mask[r, tail].astype(F32)[at : at + 1] for r in range(2)]
    else:
        rows = in_order(ids, mask[...].astype(F32), 0)
    parts = [row[:, b * side : (b + 1) * side] for b in range(2) for row in rows]
    stacked = jnp.concatenate(parts + [jnp.zeros((12, side), F32)], axis=0).astype(BF16)
    at = [lax.broadcasted_iota(jnp.int32, (side, side), axis) for axis in range(2)]
    ahead = jnp.dot(stacked, one_hot(at[0] < at[1]), preferred_element_type=F32)
    target = lax.broadcasted_iota(jnp.int32, (plan.cap, side), 0)
    for b in range(2):
        begin = jnp.zeros((1, 1), F32)
        for r in range(2):
            part = parts[2 * b + r]
            place = jnp.where(part > 0, ahead[2 * b + r : 2 * b + r + 1] + begin, -1.0).astype(jnp.int32)
            placed[b][:, r * side : (r + 1) * side] = one_hot(target == place)
            begin = begin + jnp.sum(part, axis=1, keepdims=True)


def gather_cells(cells, placed):
    dims = (((1,), (1,)), ((), ()))
    return lax.dot_general(cells, placed, dims, preferred_element_type=F32).astype(BF16)


def first_body(plan, group, ids, courant, depth, mask, field, halo, placed0, placed1, *rest):
    half, spectra, (depth8, ocean8, cells) = rest[:2], rest[2:-3], rest[-3:]
    side = plan.side

    def load(start, rows):
        at = pl.ds(start, rows)
        values = [ref[r, at].astype(F32) for ref, r in ((field, 0), (field, 1), (halo, 1), (halo, 0))]
        return values[:2] + within(ids, group, values[2:])

    def store(start, rows, new0, new1):
        at = pl.ds(start, rows)
        for r, new in enumerate((new0, new1)):
            half[r][at] = new
            begin = (r if group == 0 else 1 - r) * side
            for b in range(2):
                cells[b, at, begin : begin + side] = new[:, b * side : (b + 1) * side].astype(BF16)

    half_steps(plan, group, ids, courant, depth, mask, depth8, ocean8, load, store)
    for b, placed in enumerate((placed0, placed1)):
        gathered = gather_cells(cells[b], placed[...])
        if group == 0:
            spectra[0][:, b * plan.cap : (b + 1) * plan.cap] = gathered
        else:
            spectra[b][...] = gathered


def last_body(plan, group, ids, courant, depth, mask, full0, full1, *rest):
    *rest, done, depth8, ocean8 = rest
    width, pitch, rows, side = 2 * plan.local, plan.pitch, plan.rows, plan.side

    def scatter(cells, placed):
        return jnp.dot(cells[...], placed[...], preferred_element_type=F32)[:rows].astype(BF16)

    def both(a, b, at):
        return jnp.concatenate([a[at], b[at]], axis=1).astype(F32)

    def load(start, count):
        at = pl.ds(start, count)
        values = [both(full0.at[r], full1.at[r], at) for r in range(2)]
        if group == 0:
            rows_in = jnp.concatenate([piece[at] for piece in pieces], axis=1).astype(F32)
            return values + [rows_in[:, plan.columns :], rows_in[:, : plan.columns]]
        slots = [slice(slot * side, (slot + 1) * side) for slot in (1, 0)]
        return values + within(ids, group, [both(rim0.at[:, slot], rim1.at[:, slot], at) for slot in slots])

    def store(start, count, new0, new1):
        for r, new in enumerate((new0, new1)):
            at = r * pitch + start
            if count < 16:
                new = jnp.concatenate([new, jnp.zeros((16 - count, plan.columns), F32)], axis=0)
            done[pl.ds(pl.multiple_of(at, 16), 16)] = new.astype(BF16)

    if group == 0:
        *pieces, partial, restore = rest
    else:
        cells0, cells1, placed0, placed1, partial, restore, out, rim0, rim1 = rest
        rim0[...] = scatter(cells0, placed0)
        rim1[...] = scatter(cells1, placed1)
    half_steps(plan, group, ids, courant, depth, mask, depth8, ocean8, load, store)
    if group == 0:
        tables = []
        for g in range(2):
            lane = lax.broadcasted_iota(jnp.int32, (8, 2 * pitch), 1)
            r = jnp.where(lane >= pitch, 1, 0)
            south = southward(ids, g)
            target = 2 * plan.slot_comp(lane - pitch * r, south) + actual_row(r, south)
            target = jnp.concatenate([target] * (width // 8), axis=0)
            tables.append(one_hot(target == lax.broadcasted_iota(jnp.int32, (width, 2 * pitch), 0)))
        restore[...] = tables[1]
        partial[...] = jnp.dot(tables[0], done[...], preferred_element_type=F32)
    else:
        flat = partial[...] + jnp.dot(restore[...], done[...], preferred_element_type=F32)
        out[...] = flat.astype(BF16).reshape(plan.local, 2, plan.columns)


def weights_body(plan, ids, first, second, transfer, growth, first_out, second_out, transfer_out, growth_out, columns):
    total, local, pitch = plan.total, plan.local, plan.pitch
    comp_index = ids[1] // 2
    chosen = []
    for group in range(2):
        south = southward(ids, group)
        lane = lax.broadcasted_iota(jnp.int32, (8, 2 * pitch), 1)
        other = jnp.where(lane >= pitch, 1, 0)
        owner = jnp.where(other == 0, comp_index, 1 - comp_index)
        source = plan.slot_comp(lane - pitch * other, south) + local * owner
        source = jnp.concatenate([source] * (total // 8), axis=0)
        hot = one_hot(source == lax.broadcasted_iota(jnp.int32, (total, 2 * pitch), 0))
        columns[:, 2 * group * pitch : 2 * (group + 1) * pitch] = hot
        comp = plan.slot_comp(lax.broadcasted_iota(jnp.int32, (pitch, 128), 0), south) + local * comp_index
        chosen.append(spread(comp, total) == lax.broadcasted_iota(jnp.int32, (pitch, total), 1))
    first_out[:total] = jnp.dot(first[...], columns[...], preferred_element_type=F32).astype(BF16)
    extra = plan.out_rows - total
    place = lax.broadcasted_iota(jnp.int32, (extra, 4 * pitch), 1)
    for i in range(1, 4):
        place = jnp.where(place >= pitch, place - pitch, place)
    top = lax.broadcasted_iota(jnp.int32, (extra, 4 * pitch), 0) == 0
    first_out[total:] = one_hot(jnp.logical_and(top, place < plan.slots))
    second_out[...] = jnp.dot(second[...], columns[...], preferred_element_type=F32).astype(BF16)
    for group in range(2):
        at = slice(group * pitch, (group + 1) * pitch)
        pick = jnp.where(chosen[group], 1.0, 0.0)
        transfer_out[at] = jnp.dot(pick.astype(BF16), transfer[...], preferred_element_type=F32).astype(BF16)
        rate = jnp.sum(pick * growth[...], axis=1, keepdims=True)
        growth_out[at] = jnp.broadcast_to(rate, (pitch, 128))


TILE = 256


def fill_cells(plan, cells, blocks):
    rows, pitch = plan.rows, plan.pitch
    for i, block in enumerate(blocks):
        whole_rows = rows // 16 * 16
        cells[i * pitch : i * pitch + whole_rows] = block[:whole_rows]
        if whole_rows < pitch:
            tail = block[whole_rows:].astype(F32)
            tail = jnp.concatenate([tail, jnp.zeros((pitch - rows, tail.shape[1]), F32)], axis=0)
            cells[i * pitch + whole_rows : (i + 1) * pitch] = tail.astype(BF16)


def early_body(plan, ids, first, second, own0, peer0, own1_0, own1_1, *rest):
    outs, cells = rest[:4], rest[4]
    known = 3 * plan.pitch
    for b, own1 in enumerate((own1_0, own1_1)):
        block = slice(b * plan.cap, (b + 1) * plan.cap)
        fill_cells(plan, cells, (own0[:, block], peer0[:, block], own1[...]))
        for c in range(0, plan.cap, TILE):
            at = slice(c, c + TILE)
            outs[2 * b][:, at] = jnp.dot(first[:, :known], cells[:, at], preferred_element_type=F32)
            outs[2 * b + 1][:, at] = jnp.dot(second[:, :known], cells[:, at], preferred_element_type=F32)


def source_body(plan, b, ids, first, second, transfer, growth, placed, *rest):
    (early_first, early_second, own0, own1, peer1, half00, half01, half10, half11) = rest[:9]
    *outs, cells, sources, leaving = rest[9:]
    full0, sent0, full1 = outs[-6:-3] if b else outs
    total, rows, pitch, cap, side = plan.total, plan.rows, plan.pitch, plan.cap, plan.side
    known = 3 * pitch
    fill_cells(plan, cells, (peer1[...],))
    for c in range(0, cap, TILE):
        at = slice(c, c + TILE)
        piece = cells[:, at]
        forward = early_first[:, at] + jnp.dot(first[:, known:], piece, preferred_element_type=F32)
        backward = early_second[:, at] + jnp.dot(second[:, known:], piece, preferred_element_type=F32)
        product = (forward[:total] * backward).astype(BF16)
        nonlinear = jnp.dot(transfer[...], product, preferred_element_type=F32)
        level = forward[total : total + 1] / total
        damping = level * level / (1.0 + level * level)
        for group in range(2):
            begin = group * pitch
            spectra = (own1[:, at] if group else own0[:, b * cap + c : b * cap + c + TILE]).astype(F32)
            spectra = jnp.concatenate([spectra, jnp.zeros((pitch - rows, TILE), F32)], axis=0)
            rate = spread(growth[begin : begin + pitch], TILE)
            source = SOURCE_STEP * (nonlinear[begin : begin + pitch] + (rate - damping) * spectra)
            sources[begin : begin + pitch, at] = source.astype(BF16)
    block = slice(b * side, (b + 1) * side)
    for slot in range(2):
        here = placed[:, slot * side : (slot + 1) * side]
        spread_out = jnp.dot(sources[...], here, preferred_element_type=F32)
        full0[slot] = (half00, half01)[slot][:, block] + spread_out[:rows]
        leaving[:, slot * side : (slot + 1) * side] = full0[slot].astype(BF16)
        full1[1 - slot] = (half10, half11)[1 - slot][:, block] + spread_out[pitch : pitch + rows]
    gathered = gather_cells(leaving[...], placed[...]).astype(F32)
    sent0[...] = jnp.concatenate([gathered, jnp.zeros((sent0.shape[0] - rows, cap), F32)], axis=0).astype(BF16)
    if b:
        parts = [full[r].astype(BF16) for r in range(2) for full in (outs[0], full1)]
        for piece, (begin, end) in zip(outs[-3:], plan.pieces()):
            ends = [(max(begin - i * side, 0), min(end - i * side, side)) for i in range(4)]
            piece[...] = jnp.concatenate([parts[i][:, x:y] for i, (x, y) in enumerate(ends) if x < y], axis=1)


def paired_shards(energy, depth_speed, ocean_mask, interp_first, interp_second, transfer_matrix, growth):
    plan = Plan(energy.shape[0], energy.shape[2])
    size, rows, pitch, total = plan.columns, plan.rows, plan.pitch, plan.total
    bands = lax.axis_size("band")
    parity = lax.axis_index("band") % 2
    band = lax.axis_index("band")
    inside = jnp.logical_and(band > 0, band < bands - 1)
    ids = jnp.stack([parity, 2 * lax.axis_index("comp") + parity, inside.astype(jnp.int32)]).astype(jnp.int32)

    inner = [(i, i ^ 1) for i in range(bands)]
    outer = [(i, (i + 1 if i % 2 else i - 1) % bands) for i in range(bands)]
    outer_beside = [(2 * i + c, 2 * j + c) for i, j in outer if 0 < i < bands - 1 for c in range(2)]
    outer_beside += [(2 * i + c, 2 * i + 1 - c) for i in (0, bands - 1) for c in range(2)]
    peers = [(0, 1), (1, 0)]

    def shape(*dims, kind=BF16):
        return jax.ShapeDtypeStruct(dims, kind)

    rims = [pltpu.VMEM((2, 8, size), F32)] * 2

    field0, field1, courant = call(
        functools.partial(prep_body, plan),
        ids,
        (energy, ocean_mask),
        [shape(2, rows, size)] * 2 + [shape(2, 2, rows, 128, kind=F32)],
        [pltpu.VMEM((4 * pitch, 2 * plan.local), BF16)],
        cost=2,
    )
    halo0 = lax.ppermute(field1, "band", inner)
    halo1 = lax.ppermute(field0, "band", outer)

    cap, side = plan.cap, plan.side
    def place(mask, neighbour, cost):
        return call(functools.partial(place_body, plan, neighbour), ids, (mask,), [shape(cap, size)] * 2, cost=cost)

    placed = place(ocean_mask, False, 2)
    outer_placed = place(halo1, True, 0.01)

    def first_step(group, field, halo, spectra):
        operands = (courant, depth_speed, ocean_mask, field, halo, *placed)
        outs = [shape(rows, size, kind=F32)] * 2 + spectra
        scratch = rims + [pltpu.VMEM((2, rows, size), BF16)]
        return call(functools.partial(first_body, plan, group), ids, operands, outs, scratch, limit=20, cost=2)

    *half0, own0 = first_step(0, field0, halo0, [shape(rows, 2 * cap)])
    peer0 = lax.ppermute(own0, "comp", peers)
    first, second, transfer, rate = call(
        functools.partial(weights_body, plan),
        ids,
        (interp_first, interp_second, transfer_matrix, growth.reshape(1, total)),
        [shape(plan.out_rows, 4 * pitch), shape(total, 4 * pitch), shape(2 * pitch, total), shape(2 * pitch, 128, kind=F32)],
        [pltpu.VMEM((total, 4 * pitch), BF16)],
        cost=3,
    )
    *half1, own1_0, own1_1 = first_step(1, field1, halo1, [shape(rows, cap)] * 2)
    own1 = (own1_0, own1_1)
    peer1 = [lax.ppermute(own, "comp", peers) for own in own1]
    early = call(
        functools.partial(early_body, plan),
        ids,
        (first, second, own0, peer0, own1_0, own1_1),
        [shape(plan.out_rows, cap, kind=F32), shape(total, cap, kind=F32)] * 2,
        [pltpu.VMEM((3 * pitch, cap), BF16)],
        limit=30,
        cost=4,
    )

    full0, sent0, full1 = [], [], []
    for b in range(2):
        own = call(
            functools.partial(source_body, plan, b),
            ids,
            (first, second, transfer, rate, placed[b], early[2 * b], early[2 * b + 1], own0, own1[b], peer1[b])
            + (*half0, *half1, *full1),
            [shape(2, rows, side, kind=F32), shape(rows + (24, 8)[b], cap), shape(2, rows, side, kind=F32)]
            + [shape(rows, end - begin) for begin, end in plan.pieces()] * b,
            [pltpu.VMEM((pitch, cap), BF16), pltpu.VMEM((2 * pitch, cap), BF16), pltpu.VMEM((rows, size), BF16)],
            limit=30,
            cost=4,
        )
        full0.append(own[0])
        sent0.append(own[1])
        full1.append(own[2])
    rim1 = [lax.ppermute(sent0[0], "band", outer), lax.ppermute(sent0[1], ("band", "comp"), outer_beside)]
    rim0 = [lax.ppermute(x, "band", inner) for x in own[3:]]

    width = 2 * plan.local
    done = pltpu.VMEM((2 * pitch, size), BF16)
    partial, restore = call(
        functools.partial(last_body, plan, 0),
        ids,
        (courant, depth_speed, ocean_mask, *full0, *rim0),
        [shape(width, size, kind=F32), shape(width, 2 * pitch)],
        [done] + rims,
        limit=30,
        cost=0.01,
    )
    (out,) = call(
        functools.partial(last_body, plan, 1),
        ids,
        (courant, depth_speed, ocean_mask, *full1, *rim1, *outer_placed, partial, restore),
        [shape(*energy.shape)],
        [pltpu.VMEM((rows, size), BF16)] * 2 + [done] + rims,
        limit=30,
        cost=4,
    )
    return out


def solution(mesh):
    def shards(energy, *others):
        paired = lax.axis_size("comp") == 2 and lax.axis_size("band") % 2 == 0
        if paired and energy.shape[0] % ND == 0 and energy.shape[1] == 2 and energy.shape[2] % (4 * TILE) == 0 and energy.shape[0] // 2 % 8:
            return paired_shards(energy, *others)
        return general_shards(energy, *others)

    in_specs = (P("comp", "band", None), P("band", None), P("band", None), P(), P(), P(), P())
    out_specs = P("comp", "band", None)
    return jax.shard_map(shards, mesh=mesh, in_specs=in_specs, out_specs=out_specs, check_vma=False)
```

```python
import functools
import math

import jax
import jax.numpy as jnp
from jax import lax
from jax.experimental import pallas as pl
from jax.experimental.pallas import tpu as pltpu
from jax.sharding import PartitionSpec as P

ND = 24


SOURCE_STEP = 0.5
COURANT_TOP = 0.9
FREQ_RATIO = 1.1

F32 = jnp.float32
BF16 = jnp.bfloat16


def with_halo(value, sides, width):
    for axis, dim in sides:
        peers, length = (lax.axis_size(axis), value.shape[dim])
        up = [(i, (i + 1) % peers) for i in range(peers - 1)]
        down = [(j, i) for i, j in up]
        last = lax.slice_in_dim(value, length - width, length, axis=dim)
        first = lax.slice_in_dim(value, 0, width, axis=dim)
        before = lax.ppermute(last, axis, up)
        after = lax.ppermute(first, axis, down)
        value = jnp.concatenate([before, value, after], axis=dim)
    return value


def courant_numbers(first_comp, local_comps):
    components = first_comp + jnp.arange(local_comps, dtype=jnp.int32)
    frequency = (components // ND).astype(jnp.float32)
    direction = (components % ND).astype(jnp.float32)
    heading = 2.0 * jnp.pi * (direction + 0.5) / ND
    factor = COURANT_TOP * jnp.power(jnp.float32(FREQ_RATIO), -frequency)
    return (factor * jnp.cos(heading), factor * jnp.sin(heading))


def upwind(middle, lower_one, lower_two, upper_one, upper_two, courant):
    magnitude = jnp.abs(courant)
    first_up = jnp.where(courant > 0, lower_one, upper_one)
    second_up = jnp.where(courant > 0, lower_two, upper_two)
    return (
        middle
        - 0.5 * magnitude * (3.0 * middle - 4.0 * first_up + second_up)
        + 0.5 * magnitude * magnitude * (middle - 2.0 * first_up + second_up)
    )


def half_step(extended, lat_courant, lon_courant, depth_speed, ocean):
    widened = extended.astype(jnp.float32)
    swept = upwind(
        widened[:, 2:-2],
        widened[:, 1:-3],
        widened[:, :-4],
        widened[:, 3:-1],
        widened[:, 4:],
        lat_courant[:, None, None] * depth_speed[None],
    )
    lon_values = lon_courant[:, None, None] * depth_speed[None]
    swept = upwind(
        swept,
        jnp.roll(swept, 1, axis=2),
        jnp.roll(swept, 2, axis=2),
        jnp.roll(swept, -1, axis=2),
        jnp.roll(swept, -2, axis=2),
        lon_values,
    )
    return ocean[None] * swept


def source_terms(cell_spectra, interp_first, interp_second, transfer_matrix, growth):
    forward_interp = jnp.dot(interp_first, cell_spectra, preferred_element_type=jnp.float32)
    backward_interp = jnp.dot(interp_second, cell_spectra, preferred_element_type=jnp.float32)
    product = (forward_interp * backward_interp).astype(jnp.bfloat16)
    nonlinear = jnp.dot(transfer_matrix, product, preferred_element_type=jnp.float32)
    spectra32 = cell_spectra.astype(jnp.float32)
    mean_level = jnp.mean(spectra32, axis=0)
    damping = mean_level * mean_level / (1.0 + mean_level * mean_level)
    total = SOURCE_STEP * (nonlinear + (growth[:, None] - damping[None]) * spectra32)
    return total.astype(jnp.bfloat16)


def general_shards(energy, depth_speed, ocean_mask, interp_first, interp_second, transfer_matrix, growth):
    local_comps = energy.shape[0]
    lat_courant, lon_courant = courant_numbers(lax.axis_index("comp") * local_comps, local_comps)
    ocean = ocean_mask.astype(jnp.float32)
    start = (ocean[None] * energy.astype(jnp.float32)).astype(jnp.bfloat16)
    rimmed = with_halo(start, (("band", 1),), 2)
    half_one = half_step(rimmed, lat_courant, lon_courant, depth_speed, ocean)
    spectra = half_one.astype(jnp.bfloat16)
    block_in = lax.all_to_all(spectra, "comp", split_axis=2, concat_axis=0, tiled=True)
    total_comps = block_in.shape[0]
    flat_cells = block_in.reshape(total_comps, -1)
    result = source_terms(flat_cells, interp_first, interp_second, transfer_matrix, growth)
    source = lax.all_to_all(
        result.reshape(block_in.shape), "comp", split_axis=0, concat_axis=2, tiled=True
    ).astype(jnp.float32)
    updated = ocean[None] * (half_one + source)
    rimmed_mid = with_halo(updated, (("band", 1),), 2)
    final_field = half_step(rimmed_mid, lat_courant, lon_courant, depth_speed, ocean)
    return final_field.astype(jnp.bfloat16)


class Plan:
    def __init__(self, local_comps, columns):
        self.local = local_comps
        self.total = 2 * local_comps
        self.columns = columns
        self.half = local_comps // 4
        self.slots = 2 * self.half
        self.rows = -(-self.slots // 8) * 8
        self.pitch = -(-self.slots // 16) * 16
        self.out_rows = -(-(self.total + 1) // 16) * 16
        self.side = columns // 2
        self.cap = 3 * columns // 4

    def pieces(self):
        ends = [0, self.cap, (self.cap + 2 * self.columns) // 2, 2 * self.columns]
        return list(zip(ends[:-1], ends[1:]))

    def slot_parts(self, slot):
        east = slot < self.half
        j = jnp.where(east, slot, slot - self.half)
        f = (j * 10923) >> 16
        return east, f, j - 6 * f

    def courant(self, ids, group):
        east, f, turn = self.slot_parts(lax.broadcasted_iota(jnp.int32, (self.rows, 128), 0))
        factor = jnp.where(ids[1] >= 2, COURANT_TOP * FREQ_RATIO ** -(self.local // ND), COURANT_TOP).astype(F32)
        for bit in range(self.local.bit_length()):
            if 1 << bit < self.local // ND:
                factor = factor * jnp.where((f >> bit) & 1 == 1, FREQ_RATIO ** -(1 << bit), 1.0)
        falling = east == jnp.logical_not(southward(ids, group))
        place = jnp.where(falling, turn, 5 - turn)
        cosine, sine = factor, factor
        for i in range(6):
            cosine = jnp.where(place == i, factor * math.cos(2 * math.pi * (i + 0.5) / ND), cosine)
            sine = jnp.where(place == i, factor * math.sin(2 * math.pi * (i + 0.5) / ND), sine)
        return cosine, sine

    def slot_comp(self, slot, south):
        east, f, turn = self.slot_parts(slot)
        comp = ND * f + turn + jnp.where(east, jnp.where(south, 6, 0), jnp.where(south, 12, 18))
        return jnp.where(slot < self.slots, comp, -4 * self.total)


def southward(ids, group):
    return ids[0] == group


def actual_row(r, south):
    return jnp.where(south, 1 - r, r)


def one_hot(match):
    return jnp.where(match, 1.0, 0.0).astype(BF16)


def spread(value, width):
    parts = [value] * (width // 128)
    if width % 128:
        parts.append(value[:, : width % 128])
    return jnp.concatenate(parts, axis=1)


VMEM = pl.BlockSpec(memory_space=pltpu.VMEM)
SMEM = pl.BlockSpec(memory_space=pltpu.SMEM)


def call(body, ids, operands, outs, scratch=(), limit=40, cost=1.0):
    return pl.pallas_call(
        body,
        in_specs=[SMEM] + [VMEM] * len(operands),
        out_specs=[VMEM] * len(outs),
        scratch_shapes=list(scratch),
        out_shape=outs,
        compiler_params=pltpu.CompilerParams(vmem_limit_bytes=int(limit * 2**20)),
        cost_estimate=pl.CostEstimate(flops=int(cost * 1.1e9), bytes_accessed=0, transcendentals=0),
    )(ids, *operands)


def in_order(ids, value, group):
    south = southward(ids, group)
    one, two = value[0:1], value[1:2]
    return jnp.where(south, two, one), jnp.where(south, one, two)


def prep_body(plan, ids, energy, mask, field0, field1, courant, regroup):
    for group in range(2):
        courant[group, 0], courant[group, 1] = plan.courant(ids, group)
    width, pitch = 2 * plan.local, plan.pitch
    column = lax.broadcasted_iota(jnp.int32, (pitch, width), 1)
    for group in range(2):
        south = southward(ids, group)
        comp = plan.slot_comp(lax.broadcasted_iota(jnp.int32, (pitch, 128), 0), south)
        for r in range(2):
            begin = (2 * group + r) * pitch
            regroup[begin : begin + pitch] = one_hot(spread(2 * comp + actual_row(r, south), width) == column)
    ocean = mask[...]
    flat = energy[...].reshape(width, plan.columns)
    moved = jnp.dot(regroup[...], flat, preferred_element_type=F32)
    for group, field in enumerate((field0, field1)):
        rows = in_order(ids, ocean, group)
        for r in range(2):
            at = (2 * group + r) * pitch
            start = moved[at : at + plan.rows] * rows[r]
            if group == 0:
                place = lax.broadcasted_iota(jnp.int32, (8, plan.columns), 0) + (plan.rows - 8)
                tail = jnp.where(place == plan.slots, rows[r], start[-8:])
                start = jnp.concatenate([start[:-8], tail], axis=0)
            field[r] = start.astype(BF16)


def sweep(u, p, q, a):
    d = p - u
    e = (q - p) - d
    return u + a * (d + (0.5 * a - 0.5) * e)


def lon_sweep(u, a, shift, size):
    p, q = pltpu.roll(u, shift % size, 1), pltpu.roll(u, 2 * shift % size, 1)
    return sweep(u, p, q, a)


def half_steps(plan, group, ids, courant, depth, mask, depth8, ocean8, load, store):
    size = plan.columns
    for r, row in enumerate(in_order(ids, depth[...], group)):
        depth8[r] = jnp.broadcast_to(row, (8, size))
    for r, row in enumerate(in_order(ids, mask[...], group)):
        ocean8[r] = jnp.broadcast_to(row, (8, size))

    def block(start, rows, side):
        u0, u1, h0, h1 = load(start, rows)
        c_lat = courant[group, 0, pl.ds(start, rows)]
        c_lon = courant[group, 1, pl.ds(start, rows)]
        news = ([], [])
        for s in range(0, rows, 8):
            part = slice(s, s + 8)
            lat, lon = spread(c_lat[part], size), spread(c_lon[part], size)
            stencil = ((u0[part], h0[part], h1[part]), (u1[part], u0[part], h0[part]))
            for r in range(2):
                dep = depth8[r]
                u = sweep(*stencil[r], lat * dep)
                a = lon * dep
                if side == 0:
                    at = lax.broadcasted_iota(jnp.int32, (8, size), 0) + (start + s)
                    u = jnp.where(at < plan.half, lon_sweep(u, a, 1, size), lon_sweep(u, a, -1, size))
                else:
                    u = lon_sweep(u, a, side, size)
                news[r].append(u * ocean8[r])
        store(start, rows, jnp.concatenate(news[0], axis=0), jnp.concatenate(news[1], axis=0))

    east = plan.half // 16
    west = -(-plan.half // 16)
    full = plan.rows // 16

    @pl.loop(0, east, unroll=5)
    def _(i):
        block(pl.multiple_of(i * 16, 16), 16, 1)

    for i in range(east, west):
        block(i * 16, 16, 0)

    @pl.loop(west, full, unroll=5)
    def _(i):
        block(pl.multiple_of(i * 16, 16), 16, -1)

    if plan.rows % 16:
        block(full * 16, plan.rows % 16, -1)


def within(ids, group, rows):
    return rows if group == 0 else [jnp.where(ids[2] == 1, row, 0.0) for row in rows]


def place_body(plan, neighbour, ids, mask, *placed):
    side = plan.side
    if neighbour:
        tail = slice(plan.slots // 8 * 8, plan.rows)
        at = plan.slots % 8
        rows = [mask[r, tail].astype(F32)[at : at + 1] for r in range(2)]
    else:
        rows = in_order(ids, mask[...], 0)
    parts = [row[:, b * side : (b + 1) * side] for b in range(2) for row in rows]
    stacked = jnp.concatenate(parts + [jnp.zeros((12, side), F32)], axis=0).astype(BF16)
    at = [lax.broadcasted_iota(jnp.int32, (side, side), axis) for axis in range(2)]
    ahead = jnp.dot(stacked, one_hot(at[0] < at[1]), preferred_element_type=F32)
    target = lax.broadcasted_iota(jnp.int32, (16, side), 0)
    for b in range(2):
        begin = jnp.zeros((1, 1), F32)
        for r in range(2):
            part = parts[2 * b + r]
            place = jnp.where(part > 0, ahead[2 * b + r : 2 * b + r + 1] + begin, -1.0).astype(jnp.int32)
            beyond = jnp.broadcast_to(place, target.shape) - target
            for t in range(0, plan.cap, 16):
                placed[b][t : t + 16, r * side : (r + 1) * side] = one_hot(beyond == t)
            begin = begin + jnp.sum(part, axis=1, keepdims=True)


def gather_cells(cells, placed):
    dims = (((1,), (1,)), ((), ()))
    return lax.dot_general(cells, placed, dims, preferred_element_type=F32).astype(BF16)


def first_body(plan, group, ids, courant, depth, mask, field, halo, placed0, placed1, *rest):
    half, spectra, (depth8, ocean8, cells) = rest[:2], rest[2:-3], rest[-3:]
    side = plan.side

    def load(start, rows):
        at = pl.ds(start, rows)
        values = [ref[r, at].astype(F32) for ref, r in ((field, 0), (field, 1), (halo, 1), (halo, 0))]
        return values[:2] + within(ids, group, values[2:])

    def store(start, rows, new0, new1):
        at = pl.ds(start, rows)
        for r, new in enumerate((new0, new1)):
            half[r][at] = new
            begin = (r if group == 0 else 1 - r) * side
            for b in range(2):
                cells[b, at, begin : begin + side] = new[:, b * side : (b + 1) * side].astype(BF16)

    half_steps(plan, group, ids, courant, depth, mask, depth8, ocean8, load, store)
    for b, placed in enumerate((placed0, placed1)):
        gathered = gather_cells(cells[b], placed[...])
        if group == 0:
            spectra[0][:, b * plan.cap : (b + 1) * plan.cap] = gathered
        else:
            spectra[b][...] = gathered


def last_body(plan, group, ids, courant, depth, mask, full0, full1, *rest):
    *rest, done, depth8, ocean8 = rest
    width, pitch, rows, side = 2 * plan.local, plan.pitch, plan.rows, plan.side

    def scatter(cells, placed):
        return jnp.dot(cells[...], placed[...], preferred_element_type=F32)[:rows].astype(BF16)

    def both(a, b, at):
        return jnp.concatenate([a[at], b[at]], axis=1).astype(F32)

    def load(start, count):
        at = pl.ds(start, count)
        values = [both(full0.at[r], full1.at[r], at) for r in range(2)]
        if group == 0:
            rows_in = jnp.concatenate([piece[at] for piece in pieces], axis=1).astype(F32)
            return values + [rows_in[:, plan.columns :], rows_in[:, : plan.columns]]
        slots = [slice(slot * side, (slot + 1) * side) for slot in (1, 0)]
        return values + within(ids, group, [both(rim0.at[:, slot], rim1.at[:, slot], at) for slot in slots])

    def store(start, count, new0, new1):
        for r, new in enumerate((new0, new1)):
            at = r * pitch + start
            if count < 16:
                new = jnp.concatenate([new, jnp.zeros((16 - count, plan.columns), F32)], axis=0)
            done[pl.ds(pl.multiple_of(at, 16), 16)] = new.astype(BF16)

    if group == 0:
        *pieces, partial, restore = rest
    else:
        cells0, cells1, placed0, placed1, partial, restore, out, rim0, rim1 = rest
        rim0[...] = scatter(cells0, placed0)
        rim1[...] = scatter(cells1, placed1)
    half_steps(plan, group, ids, courant, depth, mask, depth8, ocean8, load, store)
    if group == 0:
        tables = []
        for g in range(2):
            lane = lax.broadcasted_iota(jnp.int32, (8, 2 * pitch), 1)
            r = jnp.where(lane >= pitch, 1, 0)
            south = southward(ids, g)
            target = 2 * plan.slot_comp(lane - pitch * r, south) + actual_row(r, south)
            target = jnp.concatenate([target] * (width // 8), axis=0)
            tables.append(one_hot(target == lax.broadcasted_iota(jnp.int32, (width, 2 * pitch), 0)))
        restore[...] = tables[1]
        partial[...] = jnp.dot(tables[0], done[...], preferred_element_type=F32)
    else:
        flat = partial[...] + jnp.dot(restore[...], done[...], preferred_element_type=F32)
        out[...] = flat.astype(BF16).reshape(plan.local, 2, plan.columns)


def weights_body(plan, ids, first, second, transfer, growth, first_out, second_out, transfer_out, growth_out, columns):
    total, local, pitch = plan.total, plan.local, plan.pitch
    comp_index = ids[1] // 2
    chosen = []
    for group in range(2):
        south = southward(ids, group)
        comp = plan.slot_comp(lax.broadcasted_iota(jnp.int32, (pitch, 128), 0), south) + local * comp_index
        chosen.append(spread(comp, total) == lax.broadcasted_iota(jnp.int32, (pitch, total), 1))
    for owner in (comp_index, 1 - comp_index):
        lane = lax.broadcasted_iota(jnp.int32, (8, 2 * pitch), 1)
        group = jnp.where(lane >= pitch, 1, 0)
        source = plan.slot_comp(lane - pitch * group, ids[0] == group) + local * owner
        source = jnp.concatenate([source] * (total // 8), axis=0)
        hot = one_hot(source == lax.broadcasted_iota(jnp.int32, (total, 2 * pitch), 0))
        if owner is comp_index:
            columns[:, : 2 * pitch] = hot
        else:
            columns[:, 2 * pitch :] = hot
    first_out[:total] = jnp.dot(first[...], columns[...], preferred_element_type=F32).astype(BF16)
    extra = plan.out_rows - total
    place = lax.broadcasted_iota(jnp.int32, (extra, 4 * pitch), 1)
    for i in range(1, 4):
        place = jnp.where(place >= pitch, place - pitch, place)
    top = lax.broadcasted_iota(jnp.int32, (extra, 4 * pitch), 0) == 0
    first_out[total:] = one_hot(jnp.logical_and(top, place < plan.slots))
    second_out[...] = jnp.dot(second[...], columns[...], preferred_element_type=F32).astype(BF16)
    for group in range(2):
        at = slice(group * pitch, (group + 1) * pitch)
        pick = jnp.where(chosen[group], 1.0, 0.0)
        transfer_out[at] = jnp.dot(pick.astype(BF16), transfer[...], preferred_element_type=F32).astype(BF16)
        rate = jnp.sum(pick * growth[...], axis=1, keepdims=True)
        growth_out[at] = jnp.broadcast_to(rate, (pitch, 128))


TILE = 256


def fill_cells(plan, cells, blocks):
    rows, pitch = plan.rows, plan.pitch
    for i, block in enumerate(blocks):
        whole_rows = rows // 16 * 16
        cells[i * pitch : i * pitch + whole_rows] = block[:whole_rows]
        if whole_rows < pitch:
            tail = block[whole_rows:].astype(F32)
            tail = jnp.concatenate([tail, jnp.zeros((pitch - rows, tail.shape[1]), F32)], axis=0)
            cells[i * pitch + whole_rows : (i + 1) * pitch] = tail.astype(BF16)


def early_body(plan, ids, first, second, own0, own1_0, own1_1, *rest):
    outs, cells = rest[:4], rest[4]
    pitch = plan.pitch
    for b, own1 in enumerate((own1_0, own1_1)):
        fill_cells(plan, cells, (own0[:, b * plan.cap : (b + 1) * plan.cap], own1[...]))
        for c in range(0, plan.cap, TILE):
            at = slice(c, c + TILE)
            for weights, out in ((first, outs[2 * b]), (second, outs[2 * b + 1])):
                out[:, at] = jnp.dot(weights[:, : 2 * pitch], cells[:, at], preferred_element_type=F32)


def middle_body(plan, ids, first, second, peer0, *rest):
    partial, outs, cells = rest[:4], rest[4:8], rest[8]
    known = slice(2 * plan.pitch, 3 * plan.pitch)
    for b in range(2):
        fill_cells(plan, cells, (peer0[:, b * plan.cap : (b + 1) * plan.cap],))
        for c in range(0, plan.cap, TILE):
            at = slice(c, c + TILE)
            for i, weights in ((2 * b, first), (2 * b + 1, second)):
                more = jnp.dot(weights[:, known], cells[:, at], preferred_element_type=F32)
                outs[i][:, at] = partial[i][:, at] + more


def source_body(plan, b, ids, first, second, transfer, growth, placed, *rest):
    (early_first, early_second, own0, own1, peer1, half00, half01, half10, half11) = rest[:9]
    *outs, cells, sources = rest[9:]
    full0, sent0, full1 = outs[-6:-3] if b else outs
    total, rows, pitch, cap, side = plan.total, plan.rows, plan.pitch, plan.cap, plan.side
    known = 3 * pitch
    fill_cells(plan, cells, (peer1[...],))
    spare = [jnp.zeros((sent0.shape[0] - pitch, TILE), F32)] if sent0.shape[0] > pitch else []
    for c in range(0, cap, TILE):
        at = slice(c, c + TILE)
        piece = cells[:, at]
        forward = early_first[:, at] + jnp.dot(first[:, known:], piece, preferred_element_type=F32)
        backward = early_second[:, at] + jnp.dot(second[:, known:], piece, preferred_element_type=F32)
        product = (forward[:total] * backward).astype(BF16)
        nonlinear = jnp.dot(transfer[...], product, preferred_element_type=F32)
        level = forward[total : total + 1] / total
        damping = level * level / (1.0 + level * level)
        for group in range(2):
            begin = group * pitch
            spectra = (own1[:, at] if group else own0[:, b * cap + c : b * cap + c + TILE]).astype(F32)
            spectra = jnp.concatenate([spectra, jnp.zeros((pitch - rows, TILE), F32)], axis=0)
            rate = spread(growth[begin : begin + pitch], TILE)
            source = SOURCE_STEP * (nonlinear[begin : begin + pitch] + (rate - damping) * spectra)
            sources[begin : begin + pitch, at] = source.astype(BF16)
            if group == 0:
                sum_here = spectra + source.astype(BF16).astype(F32)
                sent0[:, at] = jnp.concatenate([sum_here] + spare, axis=0)[: sent0.shape[0]].astype(BF16)
    block = slice(b * side, (b + 1) * side)
    for slot in range(2):
        here = placed[:, slot * side : (slot + 1) * side]
        spread_out = jnp.dot(sources[...], here, preferred_element_type=F32)
        full0[slot] = (half00, half01)[slot][:, block] + spread_out[:rows]
        full1[1 - slot] = (half10, half11)[1 - slot][:, block] + spread_out[pitch : pitch + rows]
    if b:
        parts = [full[r].astype(BF16) for r in range(2) for full in (outs[0], full1)]
        for piece, (begin, end) in zip(outs[-3:], plan.pieces()):
            ends = [(max(begin - i * side, 0), min(end - i * side, side)) for i in range(4)]
            piece[...] = jnp.concatenate([parts[i][:, x:y] for i, (x, y) in enumerate(ends) if x < y], axis=1)


def paired_shards(energy, depth_speed, ocean_mask, interp_first, interp_second, transfer_matrix, growth):
    plan = Plan(energy.shape[0], energy.shape[2])
    size, rows, pitch, total = plan.columns, plan.rows, plan.pitch, plan.total
    bands = lax.axis_size("band")
    parity = lax.axis_index("band") % 2
    band = lax.axis_index("band")
    inside = jnp.logical_and(band > 0, band < bands - 1)
    ids = jnp.stack([parity, 2 * lax.axis_index("comp") + parity, inside.astype(jnp.int32)]).astype(jnp.int32)

    inner = [(i, i ^ 1) for i in range(bands)]
    outer = [(i, (i + 1 if i % 2 else i - 1) % bands) for i in range(bands)]
    outer_beside = [(2 * i + c, 2 * j + c) for i, j in outer if 0 < i < bands - 1 for c in range(2)]
    outer_beside += [(2 * i + c, 2 * i + 1 - c) for i in (0, bands - 1) for c in range(2)]
    peers = [(0, 1), (1, 0)]

    def shape(*dims, kind=BF16):
        return jax.ShapeDtypeStruct(dims, kind)

    rims = [pltpu.VMEM((2, 8, size), F32)] * 2
    ocean = ocean_mask.astype(F32)

    field0, field1, courant = call(
        functools.partial(prep_body, plan),
        ids,
        (energy, ocean),
        [shape(2, rows, size)] * 2 + [shape(2, 2, rows, 128, kind=F32)],
        [pltpu.VMEM((4 * pitch, 2 * plan.local), BF16)],
        cost=2,
    )
    halo0 = lax.ppermute(field1, "band", inner)
    halo1 = lax.ppermute(field0, "band", outer)

    cap, side = plan.cap, plan.side
    def place(mask, neighbour, cost):
        return call(functools.partial(place_body, plan, neighbour), ids, (mask,), [shape(cap, size)] * 2, cost=cost)

    placed = place(ocean, False, 2)
    outer_placed = place(halo1, True, 0.01)

    def first_step(group, field, halo, spectra):
        operands = (courant, depth_speed, ocean, field, halo, *placed)
        outs = [shape(rows, size, kind=F32)] * 2 + spectra
        scratch = rims + [pltpu.VMEM((2, rows, size), BF16)]
        return call(functools.partial(first_body, plan, group), ids, operands, outs, scratch, limit=20, cost=2)

    *half0, own0 = first_step(0, field0, halo0, [shape(rows, 2 * cap)])
    peer0 = lax.ppermute(own0, "comp", peers)
    first, second, transfer, rate = call(
        functools.partial(weights_body, plan),
        ids,
        (interp_first, interp_second, transfer_matrix, growth.reshape(1, total)),
        [shape(plan.out_rows, 4 * pitch), shape(total, 4 * pitch), shape(2 * pitch, total), shape(2 * pitch, 128, kind=F32)],
        [pltpu.VMEM((total, 4 * pitch), BF16)],
        cost=3,
    )
    *half1, own1_0, own1_1 = first_step(1, field1, halo1, [shape(rows, cap)] * 2)
    own1 = (own1_0, own1_1)
    peer1 = [lax.ppermute(own, "comp", peers) for own in own1]
    early = call(
        functools.partial(early_body, plan),
        ids,
        (first, second, own0, own1_0, own1_1),
        [shape(plan.out_rows, cap, kind=F32), shape(total, cap, kind=F32)] * 2,
        [pltpu.VMEM((2 * pitch, cap), BF16)],
        limit=20,
        cost=3,
    )
    early = call(
        functools.partial(middle_body, plan),
        ids,
        (first, second, peer0, *early),
        [shape(plan.out_rows, cap, kind=F32), shape(total, cap, kind=F32)] * 2,
        [pltpu.VMEM((pitch, cap), BF16)],
        limit=20,
        cost=2,
    )

    full0, sent0, full1 = [], [], []
    for b in range(2):
        own = call(
            functools.partial(source_body, plan, b),
            ids,
            (first, second, transfer, rate, placed[b], early[2 * b], early[2 * b + 1], own0, own1[b], peer1[b])
            + (*half0, *half1, *full1),
            [shape(2, rows, side, kind=F32), shape(rows + (24, 8)[b], cap), shape(2, rows, side, kind=F32)]
            + [shape(rows, end - begin) for begin, end in plan.pieces()] * b,
            [pltpu.VMEM((pitch, cap), BF16), pltpu.VMEM((2 * pitch, cap), BF16)],
            limit=30,
            cost=4,
        )
        full0.append(own[0])
        sent0.append(own[1])
        full1.append(own[2])
    rim1 = [lax.ppermute(sent0[0], "band", outer), lax.ppermute(sent0[1], ("band", "comp"), outer_beside)]
    rim0 = [lax.ppermute(x, "band", inner) for x in own[3:]]

    width = 2 * plan.local
    done = pltpu.VMEM((2 * pitch, size), BF16)
    partial, restore = call(
        functools.partial(last_body, plan, 0),
        ids,
        (courant, depth_speed, ocean, *full0, *rim0),
        [shape(width, size, kind=F32), shape(width, 2 * pitch)],
        [done] + rims,
        limit=30,
        cost=0.01,
    )
    (out,) = call(
        functools.partial(last_body, plan, 1),
        ids,
        (courant, depth_speed, ocean, *full1, *rim1, *outer_placed, partial, restore),
        [shape(*energy.shape)],
        [pltpu.VMEM((rows, size), BF16)] * 2 + [done] + rims,
        limit=30,
        cost=4,
    )
    return out


def solution(mesh):
    def shards(energy, *others):
        paired = lax.axis_size("comp") == 2 and lax.axis_size("band") % 2 == 0
        if paired and energy.shape[0] % ND == 0 and energy.shape[1] == 2 and energy.shape[2] % (4 * TILE) == 0 and energy.shape[0] // 2 % 8:
            return paired_shards(energy, *others)
        return general_shards(energy, *others)

    in_specs = (P("comp", "band", None), P("band", None), P("band", None), P(), P(), P(), P())
    out_specs = P("comp", "band", None)
    return jax.shard_map(shards, mesh=mesh, in_specs=in_specs, out_specs=out_specs, check_vma=False)
```

```python
import functools
import math

import jax
import jax.numpy as jnp
from jax import lax
from jax.experimental import pallas as pl
from jax.experimental.pallas import tpu as pltpu
from jax.sharding import PartitionSpec as P

ND = 24


SOURCE_STEP = 0.5
COURANT_TOP = 0.9
FREQ_RATIO = 1.1

F32 = jnp.float32
BF16 = jnp.bfloat16


def with_halo(value, sides, width):
    for axis, dim in sides:
        peers, length = (lax.axis_size(axis), value.shape[dim])
        up = [(i, (i + 1) % peers) for i in range(peers - 1)]
        down = [(j, i) for i, j in up]
        last = lax.slice_in_dim(value, length - width, length, axis=dim)
        first = lax.slice_in_dim(value, 0, width, axis=dim)
        before = lax.ppermute(last, axis, up)
        after = lax.ppermute(first, axis, down)
        value = jnp.concatenate([before, value, after], axis=dim)
    return value


def courant_numbers(first_comp, local_comps):
    components = first_comp + jnp.arange(local_comps, dtype=jnp.int32)
    frequency = (components // ND).astype(jnp.float32)
    direction = (components % ND).astype(jnp.float32)
    heading = 2.0 * jnp.pi * (direction + 0.5) / ND
    factor = COURANT_TOP * jnp.power(jnp.float32(FREQ_RATIO), -frequency)
    return (factor * jnp.cos(heading), factor * jnp.sin(heading))


def upwind(middle, lower_one, lower_two, upper_one, upper_two, courant):
    magnitude = jnp.abs(courant)
    first_up = jnp.where(courant > 0, lower_one, upper_one)
    second_up = jnp.where(courant > 0, lower_two, upper_two)
    return (
        middle
        - 0.5 * magnitude * (3.0 * middle - 4.0 * first_up + second_up)
        + 0.5 * magnitude * magnitude * (middle - 2.0 * first_up + second_up)
    )


def half_step(extended, lat_courant, lon_courant, depth_speed, ocean):
    widened = extended.astype(jnp.float32)
    swept = upwind(
        widened[:, 2:-2],
        widened[:, 1:-3],
        widened[:, :-4],
        widened[:, 3:-1],
        widened[:, 4:],
        lat_courant[:, None, None] * depth_speed[None],
    )
    lon_values = lon_courant[:, None, None] * depth_speed[None]
    swept = upwind(
        swept,
        jnp.roll(swept, 1, axis=2),
        jnp.roll(swept, 2, axis=2),
        jnp.roll(swept, -1, axis=2),
        jnp.roll(swept, -2, axis=2),
        lon_values,
    )
    return ocean[None] * swept


def source_terms(cell_spectra, interp_first, interp_second, transfer_matrix, growth):
    forward_interp = jnp.dot(interp_first, cell_spectra, preferred_element_type=jnp.float32)
    backward_interp = jnp.dot(interp_second, cell_spectra, preferred_element_type=jnp.float32)
    product = (forward_interp * backward_interp).astype(jnp.bfloat16)
    nonlinear = jnp.dot(transfer_matrix, product, preferred_element_type=jnp.float32)
    spectra32 = cell_spectra.astype(jnp.float32)
    mean_level = jnp.mean(spectra32, axis=0)
    damping = mean_level * mean_level / (1.0 + mean_level * mean_level)
    total = SOURCE_STEP * (nonlinear + (growth[:, None] - damping[None]) * spectra32)
    return total.astype(jnp.bfloat16)


def general_shards(energy, depth_speed, ocean_mask, interp_first, interp_second, transfer_matrix, growth):
    local_comps = energy.shape[0]
    lat_courant, lon_courant = courant_numbers(lax.axis_index("comp") * local_comps, local_comps)
    ocean = ocean_mask.astype(jnp.float32)
    start = (ocean[None] * energy.astype(jnp.float32)).astype(jnp.bfloat16)
    rimmed = with_halo(start, (("band", 1),), 2)
    half_one = half_step(rimmed, lat_courant, lon_courant, depth_speed, ocean)
    spectra = half_one.astype(jnp.bfloat16)
    block_in = lax.all_to_all(spectra, "comp", split_axis=2, concat_axis=0, tiled=True)
    total_comps = block_in.shape[0]
    flat_cells = block_in.reshape(total_comps, -1)
    result = source_terms(flat_cells, interp_first, interp_second, transfer_matrix, growth)
    source = lax.all_to_all(
        result.reshape(block_in.shape), "comp", split_axis=0, concat_axis=2, tiled=True
    ).astype(jnp.float32)
    updated = ocean[None] * (half_one + source)
    rimmed_mid = with_halo(updated, (("band", 1),), 2)
    final_field = half_step(rimmed_mid, lat_courant, lon_courant, depth_speed, ocean)
    return final_field.astype(jnp.bfloat16)


class Plan:
    def __init__(self, local_comps, columns):
        self.local = local_comps
        self.total = 2 * local_comps
        self.columns = columns
        self.half = local_comps // 4
        self.slots = 2 * self.half
        self.rows = -(-self.slots // 8) * 8
        self.pitch = -(-self.slots // 16) * 16
        self.out_rows = -(-(self.total + 1) // 16) * 16
        self.side = columns // 2
        self.cap = 3 * columns // 4

    def slot_parts(self, slot):
        east = slot < self.half
        j = jnp.where(east, slot, slot - self.half)
        f = (j * 10923) >> 16
        return east, f, j - 6 * f

    def courant(self, ids, group):
        east, f, turn = self.slot_parts(lax.broadcasted_iota(jnp.int32, (self.rows, 128), 0))
        factor = jnp.where(ids[1] >= 2, COURANT_TOP * FREQ_RATIO ** -(self.local // ND), COURANT_TOP).astype(F32)
        for bit in range(self.local.bit_length()):
            if 1 << bit < self.local // ND:
                factor = factor * jnp.where((f >> bit) & 1 == 1, FREQ_RATIO ** -(1 << bit), 1.0)
        falling = east == jnp.logical_not(southward(ids, group))
        place = jnp.where(falling, turn, 5 - turn)
        cosine, sine = factor, factor
        for i in range(6):
            cosine = jnp.where(place == i, factor * math.cos(2 * math.pi * (i + 0.5) / ND), cosine)
            sine = jnp.where(place == i, factor * math.sin(2 * math.pi * (i + 0.5) / ND), sine)
        return cosine, sine

    def slot_comp(self, slot, south):
        east, f, turn = self.slot_parts(slot)
        comp = ND * f + turn + jnp.where(east, jnp.where(south, 6, 0), jnp.where(south, 12, 18))
        return jnp.where(slot < self.slots, comp, -4 * self.total)


def southward(ids, group):
    return ids[0] == group


def actual_row(r, south):
    return jnp.where(south, 1 - r, r)


def one_hot(match):
    return jnp.where(match, 1.0, 0.0).astype(BF16)


def spread(value, width):
    parts = [value] * (width // 128)
    if width % 128:
        parts.append(value[:, : width % 128])
    return jnp.concatenate(parts, axis=1)


VMEM = pl.BlockSpec(memory_space=pltpu.VMEM)
SMEM = pl.BlockSpec(memory_space=pltpu.SMEM)


def call(body, ids, operands, outs, scratch=(), limit=20, cost=1.0):
    return pl.pallas_call(
        body,
        in_specs=[SMEM] + [VMEM] * len(operands),
        out_specs=[VMEM] * len(outs),
        scratch_shapes=list(scratch),
        out_shape=outs,
        compiler_params=pltpu.CompilerParams(vmem_limit_bytes=int(limit * 2**20)),
        cost_estimate=pl.CostEstimate(flops=int(cost * 1.1e9), bytes_accessed=0, transcendentals=0),
    )(ids, *operands)


def in_order(ids, value, group):
    south = southward(ids, group)
    one, two = value[0:1], value[1:2]
    return jnp.where(south, two, one), jnp.where(south, one, two)


def prep_body(plan, ids, energy, mask, field0, field1, courant, regroup):
    for group in range(2):
        courant[group, 0], courant[group, 1] = plan.courant(ids, group)
    width, pitch = 2 * plan.local, plan.pitch
    column = lax.broadcasted_iota(jnp.int32, (pitch, width), 1)
    for group in range(2):
        south = southward(ids, group)
        comp = plan.slot_comp(lax.broadcasted_iota(jnp.int32, (pitch, 128), 0), south)
        for r in range(2):
            begin = (2 * group + r) * pitch
            regroup[begin : begin + pitch] = one_hot(spread(2 * comp + actual_row(r, south), width) == column)
    ocean = mask[...]
    flat = energy[...].reshape(width, plan.columns)
    moved = jnp.dot(regroup[...], flat, preferred_element_type=F32)
    for group, field in enumerate((field0, field1)):
        rows = in_order(ids, ocean, group)
        for r in range(2):
            at = (2 * group + r) * pitch
            start = moved[at : at + plan.rows] * rows[r]
            if group == 0:
                place = lax.broadcasted_iota(jnp.int32, (8, plan.columns), 0) + (plan.rows - 8)
                tail = jnp.where(place == plan.slots, rows[r], start[-8:])
                start = jnp.concatenate([start[:-8], tail], axis=0)
            field[r] = start.astype(BF16)


def sweep(u, p, q, a):
    d = p - u
    e = (q - p) - d
    return u + a * (d + (0.5 * a - 0.5) * e)


def lon_sweep(u, a, shift, size):
    p, q = pltpu.roll(u, shift % size, 1), pltpu.roll(u, 2 * shift % size, 1)
    return sweep(u, p, q, a)


def half_steps(plan, group, ids, courant, depth, mask, depth8, ocean8, load, store):
    size = plan.columns
    for r, row in enumerate(in_order(ids, depth[...], group)):
        depth8[r] = jnp.broadcast_to(row, (8, size))
    for r, row in enumerate(in_order(ids, mask[...], group)):
        ocean8[r] = jnp.broadcast_to(row, (8, size))

    def block(start, rows, side):
        u0, u1, h0, h1 = load(start, rows)
        c_lat = courant[group, 0, pl.ds(start, rows)]
        c_lon = courant[group, 1, pl.ds(start, rows)]
        news = ([], [])
        for s in range(0, rows, 8):
            part = slice(s, s + 8)
            lat, lon = spread(c_lat[part], size), spread(c_lon[part], size)
            stencil = ((u0[part], h0[part], h1[part]), (u1[part], u0[part], h0[part]))
            for r in range(2):
                dep = depth8[r]
                u = sweep(*stencil[r], lat * dep)
                a = lon * dep
                if side == 0:
                    at = lax.broadcasted_iota(jnp.int32, (8, size), 0) + (start + s)
                    u = jnp.where(at < plan.half, lon_sweep(u, a, 1, size), lon_sweep(u, a, -1, size))
                else:
                    u = lon_sweep(u, a, side, size)
                news[r].append(u * ocean8[r])
        store(start, rows, jnp.concatenate(news[0], axis=0), jnp.concatenate(news[1], axis=0))

    east = plan.half // 16
    west = -(-plan.half // 16)
    full = plan.rows // 16

    @pl.loop(0, east, unroll=5)
    def _(i):
        block(pl.multiple_of(i * 16, 16), 16, 1)

    for i in range(east, west):
        block(i * 16, 16, 0)

    @pl.loop(west, full, unroll=5)
    def _(i):
        block(pl.multiple_of(i * 16, 16), 16, -1)

    if plan.rows % 16:
        block(full * 16, plan.rows % 16, -1)


def within(ids, group, rows):
    return rows if group == 0 else [jnp.where(ids[2] == 1, row, 0.0) for row in rows]


def place_body(plan, neighbour, ids, mask, *placed):
    side = plan.side
    if neighbour:
        tail = slice(plan.slots // 8 * 8, plan.rows)
        at = plan.slots % 8
        rows = [mask[r, tail].astype(F32)[at : at + 1] for r in range(2)]
    else:
        rows = in_order(ids, mask[...], 0)
    parts = [row[:, b * side : (b + 1) * side] for b in range(2) for row in rows]
    stacked = jnp.concatenate(parts + [jnp.zeros((12, side), F32)], axis=0).astype(BF16)
    at = [lax.broadcasted_iota(jnp.int32, (side, side), axis) for axis in range(2)]
    ahead = jnp.dot(stacked, one_hot(at[0] < at[1]), preferred_element_type=F32)
    target = lax.broadcasted_iota(jnp.int32, (16, side), 0)
    for b in range(2):
        begin = jnp.zeros((1, 1), F32)
        for r in range(2):
            part = parts[2 * b + r]
            place = jnp.where(part > 0, ahead[2 * b + r : 2 * b + r + 1] + begin, -1.0).astype(jnp.int32)
            beyond = jnp.broadcast_to(place, target.shape) - target
            for t in range(0, plan.cap, 16):
                placed[b][t : t + 16, r * side : (r + 1) * side] = one_hot(beyond == t)
            begin = begin + jnp.sum(part, axis=1, keepdims=True)


def gather_cells(cells, placed):
    dims = (((1,), (1,)), ((), ()))
    return lax.dot_general(cells, placed, dims, preferred_element_type=F32).astype(BF16)


def first_body(plan, group, ids, courant, depth, mask, field, halo, placed0, placed1, *rest):
    half, spectra, (depth8, ocean8, cells) = rest[:2], rest[2:-3], rest[-3:]
    side = plan.side

    def load(start, rows):
        at = pl.ds(start, rows)
        values = [ref[r, at].astype(F32) for ref, r in ((field, 0), (field, 1), (halo, 1), (halo, 0))]
        return values[:2] + within(ids, group, values[2:])

    def store(start, rows, new0, new1):
        at = pl.ds(start, rows)
        for r, new in enumerate((new0, new1)):
            half[r][at] = new
            begin = (r if group == 0 else 1 - r) * side
            for b in range(2):
                cells[b, at, begin : begin + side] = new[:, b * side : (b + 1) * side].astype(BF16)

    half_steps(plan, group, ids, courant, depth, mask, depth8, ocean8, load, store)
    for b, placed in enumerate((placed0, placed1)):
        gathered = gather_cells(cells[b], placed[...])
        if group == 0:
            spectra[0][:, b * plan.cap : (b + 1) * plan.cap] = gathered
        else:
            spectra[b][...] = gathered


def last_body(plan, group, ids, courant, depth, mask, full, *rest):
    *rest, done, depth8, ocean8 = rest
    width, pitch, rows, side = 2 * plan.local, plan.pitch, plan.rows, plan.side

    def scatter(cells, placed):
        return jnp.dot(cells[...], placed[...], preferred_element_type=F32)[:rows].astype(BF16)

    def load(start, count):
        at = pl.ds(start, count)
        values = [full[r, at] for r in range(2)]
        if group == 0:
            return values + [inner_rows[r, at].astype(F32) for r in (1, 0)]
        slots = [slice(slot * side, (slot + 1) * side) for slot in (1, 0)]
        outer = [jnp.concatenate([rim[at, slot] for rim in (rim0, rim1)], axis=1).astype(F32) for slot in slots]
        return values + within(ids, group, outer)

    def store(start, count, new0, new1):
        for r, new in enumerate((new0, new1)):
            at = r * pitch + start
            if count < 16:
                new = jnp.concatenate([new, jnp.zeros((16 - count, plan.columns), F32)], axis=0)
            done[pl.ds(pl.multiple_of(at, 16), 16)] = new.astype(BF16)

    if group == 0:
        *pieces, restore, partial, inner_rows = rest
        for r in range(2):
            inner_rows[r, :SPLIT] = pieces[r][...]
            inner_rows[r, SPLIT:] = pieces[2][r * (pitch - SPLIT) : (r + 1) * (pitch - SPLIT)]
    else:
        cells0, cells1, placed0, placed1, partial, restore, out, rim0, rim1 = rest
        rim0[...] = scatter(cells0, placed0)
        rim1[...] = scatter(cells1, placed1)
    half_steps(plan, group, ids, courant, depth, mask, depth8, ocean8, load, store)
    if group == 0:
        partial[...] = jnp.dot(restore[...], done[...], preferred_element_type=F32)
    else:
        flat = partial[...] + jnp.dot(restore[...], done[...], preferred_element_type=F32)
        out[...] = flat.astype(BF16).reshape(plan.local, 2, plan.columns)


def restore_body(plan, ids, growth, *tables):
    width, pitch = 2 * plan.local, plan.pitch
    for group in range(2):
        lane = lax.broadcasted_iota(jnp.int32, (8, 2 * pitch), 1)
        r = jnp.where(lane >= pitch, 1, 0)
        south = southward(ids, group)
        target = 2 * plan.slot_comp(lane - pitch * r, south) + actual_row(r, south)
        target = jnp.concatenate([target] * (width // 8), axis=0)
        tables[group][...] = one_hot(target == lax.broadcasted_iota(jnp.int32, (width, 2 * pitch), 0))


def weights_body(plan, ids, first, second, transfer, growth, first_out, second_out, transfer_out, growth_out, columns):
    total, local, pitch = plan.total, plan.local, plan.pitch
    comp_index = ids[1] // 2
    chosen = []
    for group in range(2):
        south = southward(ids, group)
        comp = plan.slot_comp(lax.broadcasted_iota(jnp.int32, (pitch, 128), 0), south) + local * comp_index
        chosen.append(spread(comp, total) == lax.broadcasted_iota(jnp.int32, (pitch, total), 1))
    for owner in (comp_index, 1 - comp_index):
        lane = lax.broadcasted_iota(jnp.int32, (8, 2 * pitch), 1)
        group = jnp.where(lane >= pitch, 1, 0)
        source = plan.slot_comp(lane - pitch * group, ids[0] == group) + local * owner
        source = jnp.concatenate([source] * (total // 8), axis=0)
        hot = one_hot(source == lax.broadcasted_iota(jnp.int32, (total, 2 * pitch), 0))
        if owner is comp_index:
            columns[:, : 2 * pitch] = hot
        else:
            columns[:, 2 * pitch :] = hot
    first_out[:total] = jnp.dot(first[...], columns[...], preferred_element_type=F32).astype(BF16)
    extra = plan.out_rows - total
    place = lax.broadcasted_iota(jnp.int32, (extra, 4 * pitch), 1)
    for i in range(1, 4):
        place = jnp.where(place >= pitch, place - pitch, place)
    top = lax.broadcasted_iota(jnp.int32, (extra, 4 * pitch), 0) == 0
    first_out[total:] = one_hot(jnp.logical_and(top, place < plan.slots))
    second_out[...] = jnp.dot(second[...], columns[...], preferred_element_type=F32).astype(BF16)
    for group in range(2):
        at = slice(group * pitch, (group + 1) * pitch)
        pick = jnp.where(chosen[group], 1.0, 0.0)
        transfer_out[at] = jnp.dot(pick.astype(BF16), transfer[...], preferred_element_type=F32).astype(BF16)
        rate = jnp.sum(pick * growth[...], axis=1, keepdims=True)
        growth_out[at] = jnp.broadcast_to(rate, (pitch, 128))


TILE = 256


def fill_cells(plan, cells, blocks):
    rows, pitch = plan.rows, plan.pitch
    for i, block in enumerate(blocks):
        whole_rows = rows // 16 * 16
        cells[i * pitch : i * pitch + whole_rows] = block[:whole_rows]
        if whole_rows < pitch:
            tail = block[whole_rows:].astype(F32)
            tail = jnp.concatenate([tail, jnp.zeros((pitch - rows, tail.shape[1]), F32)], axis=0)
            cells[i * pitch + whole_rows : (i + 1) * pitch] = tail.astype(BF16)


def early_body(plan, ids, first, second, own0, own1_0, own1_1, *rest):
    outs, cells = rest[:4], rest[4]
    pitch = plan.pitch
    for b, own1 in enumerate((own1_0, own1_1)):
        fill_cells(plan, cells, (own0[:, b * plan.cap : (b + 1) * plan.cap], own1[...]))
        for c in range(0, plan.cap, TILE):
            at = slice(c, c + TILE)
            for weights, out in ((first, outs[2 * b]), (second, outs[2 * b + 1])):
                out[:, at] = jnp.dot(weights[:, : 2 * pitch], cells[:, at], preferred_element_type=F32)


def middle_body(plan, ids, first, second, peer0, *rest):
    partial, outs, cells = rest[:4], rest[4:8], rest[8]
    known = slice(2 * plan.pitch, 3 * plan.pitch)
    for b in range(2):
        fill_cells(plan, cells, (peer0[:, b * plan.cap : (b + 1) * plan.cap],))
        for c in range(0, plan.cap, TILE):
            at = slice(c, c + TILE)
            for i, weights in ((2 * b, first), (2 * b + 1, second)):
                more = jnp.dot(weights[:, known], cells[:, at], preferred_element_type=F32)
                outs[i][:, at] = partial[i][:, at] + more


def source_body(plan, b, ids, first, second, transfer, growth, *rest):
    early_first, early_second, own0, own1, peer1, sources, sent0, cells = rest
    total, rows, pitch = plan.total, plan.rows, plan.pitch
    known = 3 * pitch
    fill_cells(plan, cells, (peer1[...],))
    extra = sent0.shape[0] - rows
    for c in range(0, plan.cap, TILE):
        at = slice(c, c + TILE)
        piece = cells[:, at]
        forward = early_first[:, at] + jnp.dot(first[:, known:], piece, preferred_element_type=F32)
        backward = early_second[:, at] + jnp.dot(second[:, known:], piece, preferred_element_type=F32)
        product = (forward[:total] * backward).astype(BF16)
        nonlinear = jnp.dot(transfer[...], product, preferred_element_type=F32)
        level = forward[total : total + 1] / total
        damping = level * level / (1.0 + level * level)
        for group in range(2):
            begin = group * pitch
            spectra = (own1[:, at] if group else own0[:, b * plan.cap + c : b * plan.cap + c + TILE]).astype(F32)
            spectra = jnp.concatenate([spectra, jnp.zeros((pitch - rows, TILE), F32)], axis=0)
            rate = spread(growth[begin : begin + pitch], TILE)
            source = SOURCE_STEP * (nonlinear[begin : begin + pitch] + (rate - damping) * spectra)
            source = source.astype(BF16)
            sources[begin : begin + pitch, at] = source
            if group == 0:
                sent0[:, at] = (spectra + source.astype(F32))[: rows + extra].astype(BF16)


SPLIT = 128


def spread_body(plan, ids, sources0, sources1, placed0, placed1, half00, half01, half10, half11, full0, full1, *pieces):
    rows, pitch, side = plan.rows, plan.pitch, plan.side
    halves, fulls = ((half00, half01), (half10, half11)), (full0, full1)
    for b, (sources, placed) in enumerate(((sources0, placed0), (sources1, placed1))):
        block = slice(b * side, (b + 1) * side)
        for slot in range(2):
            here = placed[:, slot * side : (slot + 1) * side]
            spread_out = jnp.dot(sources[...], here, preferred_element_type=F32)
            for group in range(2):
                r = 1 - slot if group else slot
                updated = halves[group][r][:, block] + spread_out[group * pitch : group * pitch + rows]
                fulls[group][r, :, block] = updated
                if group:
                    spare = jnp.zeros((pitch - rows, side), F32)
                    pieces[r][:, block] = updated[:SPLIT].astype(BF16)
                    tail = jnp.concatenate([updated[SPLIT:], spare], axis=0).astype(BF16)
                    pieces[2][r * (pitch - SPLIT) : (r + 1) * (pitch - SPLIT), block] = tail


def paired_shards(energy, depth_speed, ocean_mask, interp_first, interp_second, transfer_matrix, growth):
    plan = Plan(energy.shape[0], energy.shape[2])
    size, rows, pitch, total = plan.columns, plan.rows, plan.pitch, plan.total
    bands = lax.axis_size("band")
    parity = lax.axis_index("band") % 2
    band = lax.axis_index("band")
    inside = jnp.logical_and(band > 0, band < bands - 1)
    ids = jnp.stack([parity, 2 * lax.axis_index("comp") + parity, inside.astype(jnp.int32)]).astype(jnp.int32)

    inner = [(i, i ^ 1) for i in range(bands)]
    outer = [(i, (i + 1 if i % 2 else i - 1) % bands) for i in range(bands)]
    outer_beside = [(2 * i + c, 2 * j + c) for i, j in outer if 0 < i < bands - 1 for c in range(2)]
    outer_beside += [(2 * i + c, 2 * i + 1 - c) for i in (0, bands - 1) for c in range(2)]
    peers = [(0, 1), (1, 0)]

    def shape(*dims, kind=BF16):
        return jax.ShapeDtypeStruct(dims, kind)

    rims = [pltpu.VMEM((2, 8, size), F32)] * 2
    ocean = ocean_mask.astype(F32)

    field0, field1, courant = call(
        functools.partial(prep_body, plan),
        ids,
        (energy, ocean),
        [shape(2, rows, size)] * 2 + [shape(2, 2, rows, 128, kind=F32)],
        [pltpu.VMEM((4 * pitch, 2 * plan.local), BF16)],
        cost=2,
    )
    halo0 = lax.ppermute(field1, "band", inner)
    halo1 = lax.ppermute(field0, "band", outer)

    cap, side = plan.cap, plan.side
    def place(mask, neighbour, cost):
        return call(functools.partial(place_body, plan, neighbour), ids, (mask,), [shape(cap, size)] * 2, cost=cost)

    placed = place(ocean, False, 2)
    outer_placed = place(halo1, True, 0.01)

    def first_step(group, field, halo, spectra):
        operands = (courant, depth_speed, ocean, field, halo, *placed)
        outs = [shape(rows, size, kind=F32)] * 2 + spectra
        scratch = rims + [pltpu.VMEM((2, rows, size), BF16)]
        return call(functools.partial(first_body, plan, group), ids, operands, outs, scratch, limit=20, cost=2)

    *half0, own0 = first_step(0, field0, halo0, [shape(rows, 2 * cap)])
    peer0 = lax.ppermute(own0, "comp", peers)
    growth, own0 = lax.optimization_barrier((growth, own0))
    first, second, transfer, rate = call(
        functools.partial(weights_body, plan),
        ids,
        (interp_first, interp_second, transfer_matrix, growth.reshape(1, total)),
        [shape(plan.out_rows, 4 * pitch), shape(total, 4 * pitch), shape(2 * pitch, total), shape(2 * pitch, 128, kind=F32)],
        [pltpu.VMEM((total, 4 * pitch), BF16)],
        cost=3,
    )
    restore = call(
        functools.partial(restore_body, plan), ids, (rate,), [shape(2 * plan.local, 2 * pitch)] * 2, limit=14, cost=0.5
    )
    halo1, restore = lax.optimization_barrier((halo1, restore))
    *half1, own1_0, own1_1 = first_step(1, field1, halo1, [shape(rows, cap)] * 2)
    own1 = (own1_0, own1_1)
    peer1 = [lax.ppermute(own, "comp", peers) for own in own1]
    early = call(
        functools.partial(early_body, plan),
        ids,
        (first, second, own0, own1_0, own1_1),
        [shape(plan.out_rows, cap, kind=F32), shape(total, cap, kind=F32)] * 2,
        [pltpu.VMEM((2 * pitch, cap), BF16)],
        limit=20,
        cost=3,
    )
    early = call(
        functools.partial(middle_body, plan),
        ids,
        (first, second, peer0, *early),
        [shape(plan.out_rows, cap, kind=F32), shape(total, cap, kind=F32)] * 2,
        [pltpu.VMEM((pitch, cap), BF16)],
        limit=20,
        cost=2,
    )

    sources, sent0 = [], []
    for b in range(2):
        source, sent = call(
            functools.partial(source_body, plan, b),
            ids,
            (first, second, transfer, rate, early[2 * b], early[2 * b + 1], own0, own1[b], peer1[b]),
            [shape(2 * pitch, cap), shape((pitch, rows)[b], cap)],
            [pltpu.VMEM((pitch, cap), BF16)],
            limit=20,
            cost=3,
        )
        sources.append(source)
        sent0.append(sent)
    rim1 = [lax.ppermute(sent0[0], "band", outer), lax.ppermute(sent0[1], ("band", "comp"), outer_beside)]
    full0, full1, *pieces = call(
        functools.partial(spread_body, plan),
        ids,
        (*sources, *placed, *half0, *half1),
        [shape(2, rows, size, kind=F32)] * 2 + [shape(SPLIT, size)] * 2 + [shape(2 * (pitch - SPLIT), size)],
        limit=14,
        cost=2,
    )
    rim0 = [lax.ppermute(x, "band", inner) for x in pieces]

    width = 2 * plan.local
    done = pltpu.VMEM((2 * pitch, size), BF16)
    (partial,) = call(
        functools.partial(last_body, plan, 0),
        ids,
        (courant, depth_speed, ocean, full0, *rim0, restore[0]),
        [shape(width, size, kind=F32)],
        [pltpu.VMEM((2, pitch, size), BF16), done] + rims,
        limit=20,
        cost=0.01,
    )
    (out,) = call(
        functools.partial(last_body, plan, 1),
        ids,
        (courant, depth_speed, ocean, full1, *rim1, *outer_placed, partial, restore[1]),
        [shape(*energy.shape)],
        [pltpu.VMEM((rows, size), BF16)] * 2 + [done] + rims,
        limit=20,
        cost=4,
    )
    return out


def solution(mesh):
    def shards(energy, *others):
        paired = lax.axis_size("comp") == 2 and lax.axis_size("band") % 2 == 0
        if paired and energy.shape[0] % ND == 0 and energy.shape[1] == 2 and energy.shape[2] % (4 * TILE) == 0 and energy.shape[0] // 2 % 8:
            return paired_shards(energy, *others)
        return general_shards(energy, *others)

    in_specs = (P("comp", "band", None), P("band", None), P("band", None), P(), P(), P(), P())
    out_specs = P("comp", "band", None)
    return jax.shard_map(shards, mesh=mesh, in_specs=in_specs, out_specs=out_specs, check_vma=False)
```

```python
import functools
import math

import jax
import jax.numpy as jnp
from jax import lax
from jax.experimental import pallas as pl
from jax.experimental.pallas import tpu as pltpu
from jax.sharding import PartitionSpec as P

ND = 24


SOURCE_STEP = 0.5
COURANT_TOP = 0.9
FREQ_RATIO = 1.1

F32 = jnp.float32
BF16 = jnp.bfloat16


def with_halo(value, sides, width):
    for axis, dim in sides:
        peers, length = (lax.axis_size(axis), value.shape[dim])
        up = [(i, (i + 1) % peers) for i in range(peers - 1)]
        down = [(j, i) for i, j in up]
        last = lax.slice_in_dim(value, length - width, length, axis=dim)
        first = lax.slice_in_dim(value, 0, width, axis=dim)
        before = lax.ppermute(last, axis, up)
        after = lax.ppermute(first, axis, down)
        value = jnp.concatenate([before, value, after], axis=dim)
    return value


def courant_numbers(first_comp, local_comps):
    components = first_comp + jnp.arange(local_comps, dtype=jnp.int32)
    frequency = (components // ND).astype(jnp.float32)
    direction = (components % ND).astype(jnp.float32)
    heading = 2.0 * jnp.pi * (direction + 0.5) / ND
    factor = COURANT_TOP * jnp.power(jnp.float32(FREQ_RATIO), -frequency)
    return (factor * jnp.cos(heading), factor * jnp.sin(heading))


def upwind(middle, lower_one, lower_two, upper_one, upper_two, courant):
    magnitude = jnp.abs(courant)
    first_up = jnp.where(courant > 0, lower_one, upper_one)
    second_up = jnp.where(courant > 0, lower_two, upper_two)
    return (
        middle
        - 0.5 * magnitude * (3.0 * middle - 4.0 * first_up + second_up)
        + 0.5 * magnitude * magnitude * (middle - 2.0 * first_up + second_up)
    )


def half_step(extended, lat_courant, lon_courant, depth_speed, ocean):
    widened = extended.astype(jnp.float32)
    swept = upwind(
        widened[:, 2:-2],
        widened[:, 1:-3],
        widened[:, :-4],
        widened[:, 3:-1],
        widened[:, 4:],
        lat_courant[:, None, None] * depth_speed[None],
    )
    lon_values = lon_courant[:, None, None] * depth_speed[None]
    swept = upwind(
        swept,
        jnp.roll(swept, 1, axis=2),
        jnp.roll(swept, 2, axis=2),
        jnp.roll(swept, -1, axis=2),
        jnp.roll(swept, -2, axis=2),
        lon_values,
    )
    return ocean[None] * swept


def source_terms(cell_spectra, interp_first, interp_second, transfer_matrix, growth):
    forward_interp = jnp.dot(interp_first, cell_spectra, preferred_element_type=jnp.float32)
    backward_interp = jnp.dot(interp_second, cell_spectra, preferred_element_type=jnp.float32)
    product = (forward_interp * backward_interp).astype(jnp.bfloat16)
    nonlinear = jnp.dot(transfer_matrix, product, preferred_element_type=jnp.float32)
    spectra32 = cell_spectra.astype(jnp.float32)
    mean_level = jnp.mean(spectra32, axis=0)
    damping = mean_level * mean_level / (1.0 + mean_level * mean_level)
    total = SOURCE_STEP * (nonlinear + (growth[:, None] - damping[None]) * spectra32)
    return total.astype(jnp.bfloat16)


def general_shards(energy, depth_speed, ocean_mask, interp_first, interp_second, transfer_matrix, growth):
    local_comps = energy.shape[0]
    lat_courant, lon_courant = courant_numbers(lax.axis_index("comp") * local_comps, local_comps)
    ocean = ocean_mask.astype(jnp.float32)
    start = (ocean[None] * energy.astype(jnp.float32)).astype(jnp.bfloat16)
    rimmed = with_halo(start, (("band", 1),), 2)
    half_one = half_step(rimmed, lat_courant, lon_courant, depth_speed, ocean)
    spectra = half_one.astype(jnp.bfloat16)
    block_in = lax.all_to_all(spectra, "comp", split_axis=2, concat_axis=0, tiled=True)
    total_comps = block_in.shape[0]
    flat_cells = block_in.reshape(total_comps, -1)
    result = source_terms(flat_cells, interp_first, interp_second, transfer_matrix, growth)
    source = lax.all_to_all(
        result.reshape(block_in.shape), "comp", split_axis=0, concat_axis=2, tiled=True
    ).astype(jnp.float32)
    updated = ocean[None] * (half_one + source)
    rimmed_mid = with_halo(updated, (("band", 1),), 2)
    final_field = half_step(rimmed_mid, lat_courant, lon_courant, depth_speed, ocean)
    return final_field.astype(jnp.bfloat16)


class Plan:
    def __init__(self, local_comps, columns):
        self.local = local_comps
        self.total = 2 * local_comps
        self.columns = columns
        self.half = local_comps // 4
        self.slots = 2 * self.half
        self.rows = -(-self.slots // 8) * 8
        self.pitch = -(-self.slots // 16) * 16
        self.out_rows = -(-(self.total + 1) // 16) * 16
        self.side = columns // 2
        self.starts = (0, 2 * self.pitch, 3 * self.pitch, self.pitch)
        self.cap = 3 * columns // 4

    def slot_parts(self, slot):
        east = slot < self.half
        j = jnp.where(east, slot, slot - self.half)
        f = (j * 10923) >> 16
        return east, f, j - 6 * f

    def courant(self, ids, group):
        east, f, turn = self.slot_parts(lax.broadcasted_iota(jnp.int32, (self.rows, 128), 0))
        factor = jnp.where(ids[1] >= 2, COURANT_TOP * FREQ_RATIO ** -(self.local // ND), COURANT_TOP).astype(F32)
        for bit in range(self.local.bit_length()):
            if 1 << bit < self.local // ND:
                factor = factor * jnp.where((f >> bit) & 1 == 1, FREQ_RATIO ** -(1 << bit), 1.0)
        falling = east == jnp.logical_not(southward(ids, group))
        place = jnp.where(falling, turn, 5 - turn)
        cosine, sine = factor, factor
        for i in range(6):
            cosine = jnp.where(place == i, factor * math.cos(2 * math.pi * (i + 0.5) / ND), cosine)
            sine = jnp.where(place == i, factor * math.sin(2 * math.pi * (i + 0.5) / ND), sine)
        return cosine, sine

    def slot_comp(self, slot, south):
        east, f, turn = self.slot_parts(slot)
        comp = ND * f + turn + jnp.where(east, jnp.where(south, 6, 0), jnp.where(south, 12, 18))
        return jnp.where(slot < self.slots, comp, -4 * self.total)


def southward(ids, group):
    return ids[0] == group


def actual_row(r, south):
    return jnp.where(south, 1 - r, r)


def one_hot(match):
    return jnp.where(match, 1.0, 0.0).astype(BF16)


def spread(value, width):
    parts = [value] * (width // 128)
    if width % 128:
        parts.append(value[:, : width % 128])
    return jnp.concatenate(parts, axis=1)


VMEM = pl.BlockSpec(memory_space=pltpu.VMEM)
SMEM = pl.BlockSpec(memory_space=pltpu.SMEM)


def call(body, ids, operands, outs, scratch=(), limit=20, cost=1.0):
    return pl.pallas_call(
        body,
        in_specs=[SMEM] + [VMEM] * len(operands),
        out_specs=[VMEM] * len(outs),
        scratch_shapes=list(scratch),
        out_shape=outs,
        compiler_params=pltpu.CompilerParams(vmem_limit_bytes=int(limit * 2**20)),
        cost_estimate=pl.CostEstimate(flops=int(cost * 1.1e9), bytes_accessed=0, transcendentals=0),
    )(ids, *operands)


def in_order(ids, value, group):
    south = southward(ids, group)
    one, two = value[0:1], value[1:2]
    return jnp.where(south, two, one), jnp.where(south, one, two)


def prep_body(plan, ids, energy, mask, field0, field1, courant, regroup):
    for group in range(2):
        courant[group, 0], courant[group, 1] = plan.courant(ids, group)
    width, pitch = 2 * plan.local, plan.pitch
    column = lax.broadcasted_iota(jnp.int32, (pitch, width), 1)
    for group in range(2):
        south = southward(ids, group)
        comp = plan.slot_comp(lax.broadcasted_iota(jnp.int32, (pitch, 128), 0), south)
        for r in range(2):
            begin = (2 * group + r) * pitch
            regroup[begin : begin + pitch] = one_hot(spread(2 * comp + actual_row(r, south), width) == column)
    ocean = mask[...]
    flat = energy[...].reshape(width, plan.columns)
    moved = jnp.dot(regroup[...], flat, preferred_element_type=F32)
    for group, field in enumerate((field0, field1)):
        rows = in_order(ids, ocean, group)
        for r in range(2):
            at = (2 * group + r) * pitch
            start = moved[at : at + plan.rows] * rows[r]
            if group == 0:
                place = lax.broadcasted_iota(jnp.int32, (8, plan.columns), 0) + (plan.rows - 8)
                tail = jnp.where(place == plan.slots, rows[r], start[-8:])
                start = jnp.concatenate([start[:-8], tail], axis=0)
            field[r] = start.astype(BF16)


def sweep(u, p, q, a):
    d = p - u
    e = (q - p) - d
    return u + a * (d + (0.5 * a - 0.5) * e)


def lon_sweep(u, a, shift, size):
    p, q = pltpu.roll(u, shift % size, 1), pltpu.roll(u, 2 * shift % size, 1)
    return sweep(u, p, q, a)


def half_steps(plan, group, ids, courant, depth, mask, depth8, ocean8, load, store):
    size = plan.columns
    for r, row in enumerate(in_order(ids, depth[...], group)):
        depth8[r] = jnp.broadcast_to(row, (8, size))
    for r, row in enumerate(in_order(ids, mask[...], group)):
        ocean8[r] = jnp.broadcast_to(row, (8, size))

    def block(start, rows, side):
        u0, u1, h0, h1 = load(start, rows)
        c_lat = courant[group, 0, pl.ds(start, rows)]
        c_lon = courant[group, 1, pl.ds(start, rows)]
        news = ([], [])
        for s in range(0, rows, 8):
            part = slice(s, s + 8)
            lat, lon = spread(c_lat[part], size), spread(c_lon[part], size)
            stencil = ((u0[part], h0[part], h1[part]), (u1[part], u0[part], h0[part]))
            for r in range(2):
                dep = depth8[r]
                u = sweep(*stencil[r], lat * dep)
                a = lon * dep
                if side == 0:
                    at = lax.broadcasted_iota(jnp.int32, (8, size), 0) + (start + s)
                    u = jnp.where(at < plan.half, lon_sweep(u, a, 1, size), lon_sweep(u, a, -1, size))
                else:
                    u = lon_sweep(u, a, side, size)
                news[r].append(u * ocean8[r])
        store(start, rows, jnp.concatenate(news[0], axis=0), jnp.concatenate(news[1], axis=0))

    east = plan.half // 16
    west = -(-plan.half // 16)
    full = plan.rows // 16

    @pl.loop(0, east, unroll=5)
    def _(i):
        block(pl.multiple_of(i * 16, 16), 16, 1)

    for i in range(east, west):
        block(i * 16, 16, 0)

    @pl.loop(west, full, unroll=5)
    def _(i):
        block(pl.multiple_of(i * 16, 16), 16, -1)

    if plan.rows % 16:
        block(full * 16, plan.rows % 16, -1)


def within(ids, group, rows):
    return rows if group == 0 else [jnp.where(ids[2] == 1, row, 0.0) for row in rows]


def place_body(plan, neighbour, ids, mask, *placed):
    side = plan.side
    if neighbour:
        tail = slice(plan.slots // 8 * 8, plan.rows)
        at = plan.slots % 8
        rows = [mask[r, tail].astype(F32)[at : at + 1] for r in range(2)]
    else:
        rows = in_order(ids, mask[...], 0)
    parts = [row[:, b * side : (b + 1) * side] for b in range(2) for row in rows]
    stacked = jnp.concatenate(parts + [jnp.zeros((12, side), F32)], axis=0).astype(BF16)
    at = [lax.broadcasted_iota(jnp.int32, (side, side), axis) for axis in range(2)]
    ahead = jnp.dot(stacked, one_hot(at[0] < at[1]), preferred_element_type=F32)
    target = lax.broadcasted_iota(jnp.int32, (16, side), 0)
    for b in range(2):
        begin = jnp.zeros((1, 1), F32)
        for r in range(2):
            part = parts[2 * b + r]
            place = jnp.where(part > 0, ahead[2 * b + r : 2 * b + r + 1] + begin, -1.0).astype(jnp.int32)
            beyond = jnp.broadcast_to(place, target.shape) - target
            for t in range(0, plan.cap, 16):
                placed[b][t : t + 16, r * side : (r + 1) * side] = one_hot(beyond == t)
            begin = begin + jnp.sum(part, axis=1, keepdims=True)


def gather_cells(cells, placed):
    dims = (((1,), (1,)), ((), ()))
    return lax.dot_general(cells, placed, dims, preferred_element_type=F32).astype(BF16)


def first_body(plan, group, ids, courant, depth, mask, field, halo, placed0, placed1, *rest):
    half, spectra, (depth8, ocean8, cells) = rest[:2], rest[2:-3], rest[-3:]
    side = plan.side

    def load(start, rows):
        at = pl.ds(start, rows)
        values = [ref[r, at].astype(F32) for ref, r in ((field, 0), (field, 1), (halo, 1), (halo, 0))]
        return values[:2] + within(ids, group, values[2:])

    def store(start, rows, new0, new1):
        at = pl.ds(start, rows)
        for r, new in enumerate((new0, new1)):
            half[r][at] = new
            begin = (r if group == 0 else 1 - r) * side
            for b in range(2):
                cells[b, at, begin : begin + side] = new[:, b * side : (b + 1) * side].astype(BF16)

    half_steps(plan, group, ids, courant, depth, mask, depth8, ocean8, load, store)
    for b, placed in enumerate((placed0, placed1)):
        gathered = gather_cells(cells[b], placed[...])
        if group == 0:
            spectra[0][:, b * plan.cap : (b + 1) * plan.cap] = gathered
        else:
            whole_rows = plan.rows // 16 * 16
            spectra[b][:whole_rows] = gathered[:whole_rows]
            tail = gathered[whole_rows:].astype(F32)
            if spectra[b].shape[0] > plan.rows:
                spare = jnp.zeros((spectra[b].shape[0] - plan.rows, plan.cap), F32)
                tail = jnp.concatenate([tail, spare], axis=0)
            spectra[b][whole_rows:] = tail.astype(BF16)


def last_body(plan, group, ids, courant, depth, mask, full, *rest):
    *rest, done, depth8, ocean8 = rest
    width, pitch, rows, side = 2 * plan.local, plan.pitch, plan.rows, plan.side

    def scatter(cells, placed):
        return jnp.dot(cells[...], placed[...], preferred_element_type=F32)[:rows].astype(BF16)

    def load(start, count):
        at = pl.ds(start, count)
        values = [full[r, at] for r in range(2)]
        if group == 0:
            return values + [inner_rows[r, at].astype(F32) for r in (1, 0)]
        slots = [slice(slot * side, (slot + 1) * side) for slot in (1, 0)]
        outer = [jnp.concatenate([rim[at, slot] for rim in (rim0, rim1)], axis=1).astype(F32) for slot in slots]
        return values + within(ids, group, outer)

    def store(start, count, new0, new1):
        for r, new in enumerate((new0, new1)):
            at = r * pitch + start
            if count < 16:
                new = jnp.concatenate([new, jnp.zeros((16 - count, plan.columns), F32)], axis=0)
            done[pl.ds(pl.multiple_of(at, 16), 16)] = new.astype(BF16)

    if group == 0:
        *pieces, restore, partial, inner_rows = rest
        for r in range(2):
            inner_rows[r, :SPLIT] = pieces[r][...]
            inner_rows[r, SPLIT:] = pieces[2][r * (pitch - SPLIT) : (r + 1) * (pitch - SPLIT)]
    else:
        cells0, cells1, placed0, placed1, partial, restore, out, rim0, rim1 = rest
        rim0[...] = scatter(cells0, placed0)
        rim1[...] = scatter(cells1, placed1)
    half_steps(plan, group, ids, courant, depth, mask, depth8, ocean8, load, store)
    if group == 0:
        partial[...] = jnp.dot(restore[...], done[...], preferred_element_type=F32)
    else:
        flat = partial[...] + jnp.dot(restore[...], done[...], preferred_element_type=F32)
        out[...] = flat.astype(BF16).reshape(plan.local, 2, plan.columns)


def restore_body(plan, ids, growth, *tables):
    width, pitch = 2 * plan.local, plan.pitch
    for group in range(2):
        lane = lax.broadcasted_iota(jnp.int32, (8, 2 * pitch), 1)
        r = jnp.where(lane >= pitch, 1, 0)
        south = southward(ids, group)
        target = 2 * plan.slot_comp(lane - pitch * r, south) + actual_row(r, south)
        target = jnp.concatenate([target] * (width // 8), axis=0)
        tables[group][...] = one_hot(target == lax.broadcasted_iota(jnp.int32, (width, 2 * pitch), 0))


def weights_body(plan, ids, first, second, transfer, growth, first_out, second_out, transfer_out, growth_out, columns):
    total, local, pitch = plan.total, plan.local, plan.pitch
    comp_index = ids[1] // 2
    chosen = []
    for group in range(2):
        south = southward(ids, group)
        comp = plan.slot_comp(lax.broadcasted_iota(jnp.int32, (pitch, 128), 0), south) + local * comp_index
        chosen.append(spread(comp, total) == lax.broadcasted_iota(jnp.int32, (pitch, total), 1))
    lane = lax.broadcasted_iota(jnp.int32, (8, 4 * pitch), 1)
    source, summed = jnp.full(lane.shape, -4 * total, jnp.int32), jnp.zeros(lane.shape, F32)
    for i, start in enumerate(plan.starts):
        slot = lane - start
        here = jnp.logical_and(slot >= 0, slot < pitch)
        owner = comp_index if i < 2 else 1 - comp_index
        source = jnp.where(here, plan.slot_comp(slot, southward(ids, i % 2)) + local * owner, source)
        summed = jnp.where(jnp.logical_and(here, slot < plan.slots), 1.0, summed)
    source = jnp.concatenate([source] * (total // 8), axis=0)
    columns[...] = one_hot(source == lax.broadcasted_iota(jnp.int32, (total, 4 * pitch), 0))
    first_out[:total] = jnp.dot(first[...], columns[...], preferred_element_type=F32).astype(BF16)
    extra = plan.out_rows - total
    top = lax.broadcasted_iota(jnp.int32, (extra, 4 * pitch), 0) == 0
    first_out[total:] = jnp.where(top, jnp.concatenate([summed] * (extra // 8), axis=0), 0.0).astype(BF16)
    second_out[...] = jnp.dot(second[...], columns[...], preferred_element_type=F32).astype(BF16)
    for group in range(2):
        at = slice(group * pitch, (group + 1) * pitch)
        pick = jnp.where(chosen[group], 1.0, 0.0)
        transfer_out[at] = jnp.dot(pick.astype(BF16), transfer[...], preferred_element_type=F32).astype(BF16)
        rate = jnp.sum(pick * growth[...], axis=1, keepdims=True)
        growth_out[at] = jnp.broadcast_to(rate, (pitch, 128))


TILE = 256


def fill_cells(plan, cells, blocks):
    rows, pitch = plan.rows, plan.pitch
    for i, block in enumerate(blocks):
        whole_rows = rows // 16 * 16
        cells[i * pitch : i * pitch + whole_rows] = block[:whole_rows]
        if whole_rows < pitch:
            tail = block[whole_rows:].astype(F32)
            tail = jnp.concatenate([tail, jnp.zeros((pitch - rows, tail.shape[1]), F32)], axis=0)
            cells[i * pitch + whole_rows : (i + 1) * pitch] = tail.astype(BF16)


def early_body(plan, ids, first, second, own0, *rest):
    outs, cells = rest[:4], rest[4]
    for b in range(2):
        fill_cells(plan, cells, (own0[:, b * plan.cap : (b + 1) * plan.cap],))
        for c in range(0, plan.cap, TILE):
            at = slice(c, c + TILE)
            for weights, out in ((first, outs[2 * b]), (second, outs[2 * b + 1])):
                out[:, at] = jnp.dot(weights[:, : plan.pitch], cells[:, at], preferred_element_type=F32)


def middle_body(plan, ids, first, second, own1_0, own1_1, peer0, *rest):
    partial, outs, cells = rest[:4], rest[4:8], rest[8]
    known = slice(plan.starts[1], plan.starts[1] + 2 * plan.pitch)
    for b, own1 in enumerate((own1_0, own1_1)):
        fill_cells(plan, cells, (own1[: plan.rows], peer0[:, b * plan.cap : (b + 1) * plan.cap]))
        for c in range(0, plan.cap, TILE):
            at = slice(c, c + TILE)
            for i, weights in ((2 * b, first), (2 * b + 1, second)):
                more = jnp.dot(weights[:, known], cells[:, at], preferred_element_type=F32)
                outs[i][:, at] = partial[i][:, at] + more


def source_body(plan, b, ids, first, second, transfer, growth, *rest):
    early_first, early_second, own0, own1, peer1, sources, sent0, cells = rest
    total, rows, pitch = plan.total, plan.rows, plan.pitch
    known = slice(plan.starts[3], plan.starts[3] + pitch)
    fill_cells(plan, cells, (peer1[:rows],))
    extra = sent0.shape[0] - rows
    piece = cells[...]
    forward = early_first[...] + jnp.dot(first[:, known], piece, preferred_element_type=F32)
    backward = early_second[...] + jnp.dot(second[:, known], piece, preferred_element_type=F32)
    product = (forward[:total] * backward).astype(BF16)
    nonlinear = jnp.dot(transfer[...], product, preferred_element_type=F32)
    level = forward[total : total + 1] / total
    damping = level * level / (1.0 + level * level)
    for group in range(2):
        begin = group * pitch
        spectra = (own1[:rows] if group else own0[:, b * plan.cap : (b + 1) * plan.cap]).astype(F32)
        spectra = jnp.concatenate([spectra, jnp.zeros((pitch - rows, plan.cap), F32)], axis=0)
        rate = spread(growth[begin : begin + pitch], plan.cap)
        source = SOURCE_STEP * (nonlinear[begin : begin + pitch] + (rate - damping) * spectra)
        source = source.astype(BF16)
        sources[begin : begin + pitch] = source
        if group == 0:
            sent0[...] = (spectra + source.astype(F32))[: rows + extra].astype(BF16)


SPLIT = 128


def spread_body(plan, group, ids, sources0, sources1, placed0, placed1, half0, half1, full, *pieces):
    rows, pitch, side = plan.rows, plan.pitch, plan.side
    own = slice(group * pitch, (group + 1) * pitch)
    for b, (sources, placed) in enumerate(((sources0, placed0), (sources1, placed1))):
        block = slice(b * side, (b + 1) * side)
        for slot in range(2):
            r = 1 - slot if group else slot
            here = placed[:, slot * side : (slot + 1) * side]
            spread_out = jnp.dot(sources[own], here, preferred_element_type=F32)
            updated = (half0, half1)[r][:, block] + spread_out[:rows]
            full[r, :, block] = updated
            if group:
                spare = jnp.zeros((pitch - rows, side), F32)
                pieces[r][:, block] = updated[:SPLIT].astype(BF16)
                tail = jnp.concatenate([updated[SPLIT:], spare], axis=0).astype(BF16)
                pieces[2][r * (pitch - SPLIT) : (r + 1) * (pitch - SPLIT), block] = tail


def paired_shards(energy, depth_speed, ocean_mask, interp_first, interp_second, transfer_matrix, growth):
    plan = Plan(energy.shape[0], energy.shape[2])
    size, rows, pitch, total = plan.columns, plan.rows, plan.pitch, plan.total
    bands = lax.axis_size("band")
    parity = lax.axis_index("band") % 2
    band = lax.axis_index("band")
    inside = jnp.logical_and(band > 0, band < bands - 1)
    ids = jnp.stack([parity, 2 * lax.axis_index("comp") + parity, inside.astype(jnp.int32)]).astype(jnp.int32)

    inner = [(i, i ^ 1) for i in range(bands)]
    outer = [(i, (i + 1 if i % 2 else i - 1) % bands) for i in range(bands)]
    outer_beside = [(2 * i + c, 2 * j + c) for i, j in outer if 0 < i < bands - 1 for c in range(2)]
    outer_beside += [(2 * i + c, 2 * i + 1 - c) for i in (0, bands - 1) for c in range(2)]
    peers = [(0, 1), (1, 0)]

    def shape(*dims, kind=BF16):
        return jax.ShapeDtypeStruct(dims, kind)

    rims = [pltpu.VMEM((2, 8, size), F32)] * 2
    ocean = ocean_mask.astype(F32)

    cap, side = plan.cap, plan.side
    def place(mask, neighbour, cost):
        return call(functools.partial(place_body, plan, neighbour), ids, (mask,), [shape(cap, size)] * 2, limit=14, cost=cost)

    placed = place(ocean, False, 2)
    first_ocean, *placed = lax.optimization_barrier((ocean, *placed))
    field0, field1, courant = call(
        functools.partial(prep_body, plan),
        ids,
        (energy, first_ocean),
        [shape(2, rows, size)] * 2 + [shape(2, 2, rows, 128, kind=F32)],
        [pltpu.VMEM((4 * pitch, 2 * plan.local), BF16)],
        cost=2,
    )
    halo0 = lax.ppermute(field1, "band", inner)
    halo1 = lax.ppermute(field0, "band", outer)


    def first_step(group, field, halo, spectra):
        operands = (courant, depth_speed, ocean, field, halo, *placed)
        outs = [shape(rows, size, kind=F32)] * 2 + spectra
        scratch = rims + [pltpu.VMEM((2, rows, size), BF16)]
        return call(functools.partial(first_body, plan, group), ids, operands, outs, scratch, limit=20, cost=2)

    *half0, own0 = first_step(0, field0, halo0, [shape(rows, 2 * cap)])
    peer0 = lax.ppermute(own0, "comp", peers)
    growth, own0 = lax.optimization_barrier((growth, own0))
    first, second, transfer, rate = call(
        functools.partial(weights_body, plan),
        ids,
        (interp_first, interp_second, transfer_matrix, growth.reshape(1, total)),
        [shape(plan.out_rows, 4 * pitch), shape(total, 4 * pitch), shape(2 * pitch, total), shape(2 * pitch, 128, kind=F32)],
        [pltpu.VMEM((total, 4 * pitch), BF16)],
        cost=3,
    )
    restore = call(
        functools.partial(restore_body, plan), ids, (rate,), [shape(2 * plan.local, 2 * pitch)] * 2, limit=14, cost=0.5
    )
    early = call(
        functools.partial(early_body, plan),
        ids,
        (first, second, own0),
        [shape(plan.out_rows, cap, kind=F32), shape(total, cap, kind=F32)] * 2,
        [pltpu.VMEM((pitch, cap), BF16)],
        limit=14,
        cost=2,
    )
    halo1, restore, early = lax.optimization_barrier((halo1, restore, early))
    *half1, own1_0, own1_1 = first_step(1, field1, halo1, [shape(rows, cap), shape(pitch, cap)])
    own1 = (own1_0, own1_1)
    peer1 = [lax.ppermute(own, "comp", peers) for own in own1]
    halo1, own1_0 = lax.optimization_barrier((halo1, own1_0))
    outer_placed = place(halo1, True, 1)
    peer0, *outer_placed = lax.optimization_barrier((peer0, *outer_placed))
    early = call(
        functools.partial(middle_body, plan),
        ids,
        (first, second, own1_0, own1_1, peer0, *early),
        [shape(plan.out_rows, cap, kind=F32), shape(total, cap, kind=F32)] * 2,
        [pltpu.VMEM((2 * pitch, cap), BF16)],
        limit=14,
        cost=3,
    )

    sources, sent0 = [], []
    for b in range(2):
        source, sent = call(
            functools.partial(source_body, plan, b),
            ids,
            (first, second, transfer, rate, early[2 * b], early[2 * b + 1], own0, own1[b], peer1[b]),
            [shape(2 * pitch, cap), shape((pitch, rows)[b], cap)],
            [pltpu.VMEM((pitch, cap), BF16)],
            limit=20,
            cost=3,
        )
        sources.append(source)
        sent0.append(sent)
    rim1 = [lax.ppermute(sent0[0], "band", outer), lax.ppermute(sent0[1], ("band", "comp"), outer_beside)]

    def spread_out(group, half, outs):
        operands = (*sources, *placed, *half)
        outs = [shape(2, rows, size, kind=F32)] + outs
        return call(functools.partial(spread_body, plan, group), ids, operands, outs, limit=14, cost=1)

    full1, *pieces = spread_out(1, half1, [shape(SPLIT, size)] * 2 + [shape(2 * (pitch - SPLIT), size)])
    rim0 = [lax.ppermute(x, "band", inner) for x in pieces]

    (full0,) = spread_out(0, half0, [])
    width = 2 * plan.local
    done = pltpu.VMEM((2 * pitch, size), BF16)
    (partial,) = call(
        functools.partial(last_body, plan, 0),
        ids,
        (courant, depth_speed, ocean, full0, *rim0, restore[0]),
        [shape(width, size, kind=F32)],
        [pltpu.VMEM((2, pitch, size), BF16), done] + rims,
        limit=20,
        cost=0.01,
    )
    (out,) = call(
        functools.partial(last_body, plan, 1),
        ids,
        (courant, depth_speed, ocean, full1, *rim1, *outer_placed, partial, restore[1]),
        [shape(*energy.shape)],
        [pltpu.VMEM((rows, size), BF16)] * 2 + [done] + rims,
        limit=20,
        cost=4,
    )
    return out


def solution(mesh):
    def shards(energy, *others):
        paired = lax.axis_size("comp") == 2 and lax.axis_size("band") % 2 == 0
        if paired and energy.shape[0] % ND == 0 and energy.shape[1] == 2 and energy.shape[2] % (4 * TILE) == 0 and energy.shape[0] // 2 % 8:
            return paired_shards(energy, *others)
        return general_shards(energy, *others)

    in_specs = (P("comp", "band", None), P("band", None), P("band", None), P(), P(), P(), P())
    out_specs = P("comp", "band", None)
    return jax.shard_map(shards, mesh=mesh, in_specs=in_specs, out_specs=out_specs, check_vma=False)
```
